512 devices in a mesh: dp: 64 (over y, z), tensor: 8 (over x, core).
Axes of the slice: x: 4, y: 4, z: 16, core: 2. Of those that a mesh axis runs over, the one named last changes fastest.
Arguments:
- acts: bfloat16 [8192, 1024], P('dp', 'tensor'), may hold values from -6 to 6
- grad_out: bfloat16 [8192, 1024], P('dp', 'tensor'), may hold values from -6 to 6
- master: float32 [3, 1536, 1024], P(None, 'dp', 'tensor'), may hold values from -0.1875 to 0.1875
- moment_one: float32 [3, 1536, 1024], P(None, 'dp', 'tensor'), may hold values from -3 to 3
- moment_two: float32 [3, 1536, 1024], P(None, 'dp', 'tensor'), may hold values from 0.25 to 4
- bit_widths: int32 [3, 24], replicated, may hold values from 2 to 8
- row_dither: int32 [3, 1536], replicated, may hold values from 0 to 1023
- col_dither: int32 [1024], P('tensor'), may hold values from 0 to 1023
Outputs:
- grad_in: bfloat16 [8192, 1024], P('dp', 'tensor')
- new_master: float32 [3, 1536, 1024], P(None, 'dp', 'tensor')
- new_moment_one: float32 [3, 1536, 1024], P(None, 'dp', 'tensor')
- new_moment_two: float32 [3, 1536, 1024], P(None, 'dp', 'tensor')
- new_weights: bfloat16 [3, 1536, 1024], P(None, None, 'tensor')
The draws below stay inside these ranges and needn't reach their ends.
All inputs are finite; a program needn't handle non-finite values.
Results may differ from the reference program's by a relative error of at most 0.002.
The reference program's roundings to bfloat16 on the way (of `eightbit` and `weights`) count: a program that leaves them out, or rounds other values in their place, can miss the bound.
Values may be sent and summed in bfloat16 or wider, within the bound.
No kernel may reach another device: no remote copies, remote signals or barrier semaphores. Data moves between devices by JAX's collectives and lax.ppermute only.
A program may use at most 64 MiB of HBM per device.

```python
import math
import jax
import jax.numpy as jnp
from jax import lax

D = 1024
TOK = 128
NBUCK = 24
BROWS = 64
QB = 128
HID = 1536
TOKENS = 8192
N_DP = 64


def place_ends(drawn, rng, least, top_value):
    longest = drawn.shape.index(max(drawn.shape))
    spots = []
    for shift in (0, 1):
        where = [jax.random.randint(jax.random.fold_in(rng, axis), (), 0, length) for axis, length in enumerate(drawn.shape)]
        where[longest] = (where[longest] + shift) % drawn.shape[longest]
        spots.append(tuple(where))
    return drawn.at[spots[0]].set(least).at[spots[1]].set(top_value)


def steps_of(stream_key, extent, split, smallest, top_value):
    factor_of = 1.0
    for axis_at, parts in split:
        heights = jax.random.uniform(jax.random.fold_in(jax.random.fold_in(stream_key, 6), axis_at), (parts,), jnp.float32, smallest / len(split), top_value / len(split))
        factor_of = factor_of * jnp.repeat(jnp.exp(heights), extent[axis_at] // parts).reshape((-1,) + (1,) * (len(extent) - 1 - axis_at))
    return factor_of


def centred(stream_key, shape, deviation, limit, shards=(), kind=jnp.bfloat16):
    level = steps_of(stream_key, shape, shards, -0.22, 0.18) if shards else 1.0
    result = jax.random.normal(stream_key, shape, jnp.float32) * deviation * level
    return jnp.minimum(jnp.maximum(result, -limit), limit).astype(kind)


def setup_inputs(seed: int = 0) -> dict:
    key_of = jax.random.split(jax.random.key(seed), 9)
    acts = centred(key_of[0], (TOKENS, D), 1.0, 6.0, ((0, 64), (1, 8)))
    grad_out = centred(key_of[1], (TOKENS, D), 1.0, 6.0, ((0, 64), (1, 8)))
    master = centred(key_of[2], (3, HID, D), D ** -0.5, 0.1875, ((1, 64), (2, 8)), jnp.float32)
    moment_one = centred(key_of[3], (3, HID, D), 0.5, 3.0, ((1, 64), (2, 8)), jnp.float32)
    moment_two = jnp.clip(jnp.exp(math.log(4.0) - 2.7725887 * jax.random.uniform(key_of[4], (3, HID, D), jnp.float32) ** steps_of(key_of[4], (3, HID, D), ((1, 64), (2, 8)), -0.2, 0.2)), 0.25, 4.0)
    bit_widths = place_ends(jax.random.randint(key_of[5], (3, NBUCK), 2, 9), jax.random.fold_in(key_of[5], 1), 2, 8).astype(jnp.int32)
    row_dither = place_ends(jax.random.randint(key_of[6], (3, HID), 0, 1024), jax.random.fold_in(key_of[6], 1), 0, 1023).astype(jnp.int32)
    col_dither = place_ends(jax.random.randint(key_of[7], (D,), 0, 1024), jax.random.fold_in(key_of[7], 1), 0, 1023).astype(jnp.int32)
    return {"acts": acts, "grad_out": grad_out, "master": master, "moment_one": moment_one, "moment_two": moment_two, "bit_widths": bit_widths, "row_dither": row_dither, "col_dither": col_dither}


BETA_ONE = 0.9
BETA_TWO = 0.95
LEARN_RATE = 0.004
WEIGHT_DECAY = 0.1
ADAM_EPS = 1e-08
RANGE_EPS = 1e-06

def soft_round(value):
    return value - jnp.sin(2.0 * math.pi * value) / (2.0 * math.pi)

def eightbit(weights):
    count, rows, cols = weights.shape
    blocks = weights.reshape(count, rows, cols // QB, QB)
    scale = (lax.optimization_barrier(jnp.max(jnp.abs(blocks), axis=3, keepdims=True)) + RANGE_EPS) / 127.0
    return (soft_round(blocks / scale) * scale).reshape(count, rows, cols).astype(jnp.bfloat16)

def hidden_terms(gate, upper, delta):
    sig = jax.nn.sigmoid(gate)
    active = gate * sig
    dgate = delta * upper * sig * (1.0 + gate * (1.0 - sig))
    dupper = delta * active
    hidden = active * upper
    return jnp.stack([dgate, dupper, hidden]).astype(jnp.bfloat16)

def grads_of(terms, xrows, grows):
    return jnp.stack([jnp.dot(terms[0], xrows, preferred_element_type=jnp.float32), jnp.dot(terms[1], xrows, preferred_element_type=jnp.float32), jnp.dot(terms[2], grows, preferred_element_type=jnp.float32)])

def bucket_max(grads):
    return lax.optimization_barrier(jnp.max(jnp.abs(grads).reshape(grads.shape[0], HID // BROWS, -1), axis=2))

def reference(acts, grad_out, master, moment_one, moment_two, bit_widths, row_dither, col_dither):
    weights = eightbit(master)
    acts_rep = acts.reshape(N_DP, TOK, D)
    grad_rep = grad_out.reshape(N_DP, TOK, D)

    def first_pass(pair):
        xrows, grows = pair
        gate = jnp.dot(weights[0], xrows.T, preferred_element_type=jnp.float32)
        upper = jnp.dot(weights[1], xrows.T, preferred_element_type=jnp.float32)
        delta = jnp.dot(weights[2], grows.T, preferred_element_type=jnp.float32)
        terms = hidden_terms(gate, upper, delta)
        grads = grads_of(terms, xrows, grows)
        back = jnp.dot(terms[0].T, weights[0], preferred_element_type=jnp.float32)
        back = back + jnp.dot(terms[1].T, weights[1], preferred_element_type=jnp.float32)
        return (terms, bucket_max(grads), back.astype(jnp.bfloat16))
    terms_all, maxima_all, grad_rows = lax.map(first_pass, (acts_rep, grad_rep))
    ranges = lax.optimization_barrier(jnp.max(maxima_all, axis=0))
    levels = jnp.exp2((bit_widths - 1).astype(jnp.float32)) - 1.0
    scale = (ranges + RANGE_EPS) / levels
    scale_rows = jnp.repeat(scale, BROWS, axis=1)[:, :, None]
    offsets = row_dither[:, :, None] + col_dither[None, None, :]

    def second_pass(total, item):
        terms, xrows, grows, index = item
        grads = grads_of(terms, xrows, grows)
        phase = jnp.mod(offsets + 389 * index, 1024).astype(jnp.float32) / 1024.0 - 0.5
        quant = soft_round(grads / scale_rows + phase) - phase
        return (total + quant, None)
    total, unused = lax.scan(second_pass, jnp.zeros((3, HID, D), jnp.float32), (terms_all, acts_rep, grad_rep, jnp.arange(N_DP, dtype=jnp.int32)))
    mean_grad = total * scale_rows / N_DP
    first = BETA_ONE * moment_one + (1.0 - BETA_ONE) * mean_grad
    second = BETA_TWO * moment_two + (1.0 - BETA_TWO) * mean_grad * mean_grad
    updated = master - LEARN_RATE * (first / (jnp.sqrt(second) + ADAM_EPS) + WEIGHT_DECAY * master)
    return (grad_rows.reshape(TOKENS, D), updated, first, second, eightbit(updated))
```

```python
import jax
import jax.numpy as jnp
from jax import lax
from jax.experimental import pallas as pl
from jax.experimental.pallas import tpu as pltpu
from jax.sharding import Mesh, PartitionSpec as P

F32 = jnp.float32
BF16 = jnp.bfloat16

TOK = 128
BROWS = 64
COLS = 128
SHARD = 24
BLOCK = 48
REPS = 4

BETA_ONE = 0.9
BETA_TWO = 0.95
LEARN_RATE = 0.004
WEIGHT_DECAY = 0.1
ADAM_EPS = 1e-08
RANGE_EPS = 1e-06
N_DP = 64

SINE = (
    0.9999995827674866,
    -6.579691410064697,
    12.986435890197754,
    -12.188101768493652,
    6.558042526245117,
    -1.95303213596344,
)

DP = ("y", "z")
TENSOR = ("xh", "xl", "c")
SIZES = (4, 16, 2, 2, 2)

VMEM_LIMIT = 40 * 1024 * 1024


def turn(value):
    frac = value - jnp.floor(value + 0.5)
    square = frac * frac
    total = jnp.full_like(square, SINE[-1])
    for coef in SINE[-2::-1]:
        total = total * square + coef
    return total * frac


def soft_round(value):
    return value - turn(value)


def eightbit_f32(weights):
    scale = (jnp.max(jnp.abs(weights), axis=-1, keepdims=True) + RANGE_EPS) / 127.0
    return soft_round(weights / scale) * scale


def dot(left, right, left_dim, right_dim):
    return lax.dot_general(
        left, right, (((left_dim,), (right_dim,)), ((), ())), preferred_element_type=F32
    )


def front_kernel(pos_ref, own_ref, other_ref, weights_ref, xs_ref, gs_ref, terms_ref, col_ref, peak_ref):
    core = pos_ref[0]
    for chip in range(4):
        for source, which in ((own_ref, core), (other_ref, 1 - core)):
            cols = pl.ds(pl.multiple_of((2 * chip + which) * COLS, COLS), COLS)
            for rep in range(REPS):
                rows = slice(rep * TOK, (rep + 1) * TOK)
                xs_ref[rows, cols] = source[rep * 4 + chip, 0:TOK, :]
                gs_ref[rows, cols] = source[rep * 4 + chip, TOK : 2 * TOK, :]
            pair = source[chip, 2 * TOK : 2 * TOK + 16, :].astype(F32)
            dither = pair[0:1] * 8.0 + pair[1:2]
            col_ref[:, cols] = jnp.broadcast_to(dither * (1.0 / 1024.0), (8, COLS))
    front = dot(weights_ref[0 : 2 * BLOCK, :], xs_ref[...], 1, 1)
    delta = dot(weights_ref[2 * BLOCK : 3 * BLOCK, :], gs_ref[...], 1, 1)
    gate = front[0:BLOCK]
    upper = front[BLOCK:]
    sig = jax.nn.sigmoid(gate)
    active = gate * sig
    dgate = (delta * upper * sig * (1.0 + gate * (1.0 - sig))).astype(BF16)
    dupper = (delta * active).astype(BF16)
    hidden = (active * upper).astype(BF16)
    peak = jnp.zeros((3 * BLOCK, COLS), F32)
    for rep in range(REPS):
        rows = slice(rep * TOK, (rep + 1) * TOK)
        terms_ref[rep, 0:BLOCK, :] = dgate[:, rows]
        terms_ref[rep, BLOCK : 2 * BLOCK, :] = dupper[:, rows]
        terms_ref[rep, 2 * BLOCK : 3 * BLOCK, :] = hidden[:, rows]
        for part in range(4):
            cols = slice(part * 256, (part + 1) * 256)
            grad_front = dot(terms_ref[rep, 0 : 2 * BLOCK, :], xs_ref[rows, cols], 1, 0)
            grad_down = dot(terms_ref[rep, 2 * BLOCK : 3 * BLOCK, :], gs_ref[rows, cols], 1, 0)
            grads = jnp.abs(jnp.concatenate([grad_front, grad_down], axis=0))
            peak = jnp.maximum(peak, jnp.maximum(grads[:, :COLS], grads[:, COLS:]))
    lane = lax.broadcasted_iota(jnp.int32, (1, COLS), 1)
    packed = jnp.zeros((1, COLS), F32)
    for group in range(9):
        top = jnp.max(peak[group * 16 : (group + 1) * 16], axis=0, keepdims=True)
        top = jnp.max(top, axis=1, keepdims=True)
        packed = jnp.where(lane == group, top, packed)
    peak_ref[...] = jnp.broadcast_to(packed.reshape(1, 1, COLS), peak_ref.shape)


def quant_kernel(pos_ref, xs_ref, gs_ref, terms_ref, peaks_ref, bits_ref, row_ref, col_ref, out_ref):
    spot = pos_ref[1]
    unit = pos_ref[2]
    depth = pos_ref[3]
    lane = lax.broadcasted_iota(jnp.int32, (1, COLS), 1)
    buck = lax.broadcasted_iota(jnp.int32, (1, 24), 1)
    tops = [jnp.max(peaks_ref[i * 16 : (i + 1) * 16], axis=0) for i in range(4)]
    scales = []
    for mat in range(3):
        per_bucket = []
        for bucket in range(3):
            held = jnp.zeros((1, COLS), F32)
            for sub in range(4 * bucket, 4 * bucket + 4):
                held = jnp.maximum(held, jnp.where(lane == mat * 3 + sub % 3, tops[sub // 3], 0.0))
            ranges = jnp.max(held, axis=1, keepdims=True)
            bits = jnp.where(buck == 3 * unit + bucket, bits_ref[mat : mat + 1, :].astype(F32), 0.0)
            bits = jnp.max(bits, axis=1, keepdims=True)
            levels = jnp.ones_like(bits)
            for count in range(3, 9):
                levels = jnp.where(bits == float(count), float(2 ** (count - 1) - 1), levels)
            per_bucket.append((ranges + RANGE_EPS) / levels)
        for sub in range(3):
            which = (3 * spot + sub) // 4
            chosen = jnp.where(which == 0, per_bucket[0], jnp.where(which == 1, per_bucket[1], per_bucket[2]))
            scales.append(jnp.broadcast_to(chosen, (16, COLS)))
    scale = jnp.concatenate(scales, axis=0)
    inverse = 1.0 / scale
    scale = scale * (1.0 / N_DP)
    row_part = row_ref[...]
    for part in range(4):
        cols = slice(part * 256, (part + 1) * 256)
        halves = [jnp.zeros((3 * BLOCK, COLS), F32) for _ in range(2)]
        for rep in range(REPS):
            rows = slice(rep * TOK, (rep + 1) * TOK)
            grad_front = dot(terms_ref[rep, 0 : 2 * BLOCK, :], xs_ref[rows, cols], 1, 0)
            grad_down = dot(terms_ref[rep, 2 * BLOCK : 3 * BLOCK, :], gs_ref[rows, cols], 1, 0)
            grads = jnp.concatenate([grad_front, grad_down], axis=0)
            offset = lax.rem(389 * (rep * 16 + depth), 1024).astype(F32) * (1.0 / 1024.0)
            for half in range(2):
                lanes = slice(half * COLS, (half + 1) * COLS)
                whole = slice(part * 256 + half * COLS, part * 256 + (half + 1) * COLS)
                ratio = grads[:, lanes] * inverse
                phase = row_part + (col_ref[0:1, whole] + offset)
                halves[half] = halves[half] + (ratio + turn(ratio + phase))
        for half in range(2):
            result = halves[half] * scale
            for mat in range(3):
                for low in range(2):
                    start = mat * BLOCK + low * SHARD
                    out_ref[2 * (2 * part + half) + low, mat, :, :] = result[start : start + SHARD]


def adam_kernel(mean_ref, master_ref, one_ref, two_ref, new_master_ref, new_one_ref, new_two_ref, coded_ref):
    mean_grad = mean_ref[...]
    master = master_ref[...]
    first = BETA_ONE * one_ref[...] + (1.0 - BETA_ONE) * mean_grad
    second = BETA_TWO * two_ref[...] + (1.0 - BETA_TWO) * mean_grad * mean_grad
    updated = master - LEARN_RATE * (first / (jnp.sqrt(second) + ADAM_EPS) + WEIGHT_DECAY * master)
    new_one_ref[...] = first
    new_two_ref[...] = second
    new_master_ref[...] = updated
    coded_ref[...] = eightbit_f32(updated)


def back_kernel(terms_ref, weights_ref, out_ref, rows_ref):
    for tensor in range(8):
        for plane in range(4):
            base = (tensor * 4 + plane) * 2 * BLOCK
            start = (8 * plane + tensor) * BLOCK
            rows_ref[base : base + BLOCK, :] = weights_ref[0, start : start + BLOCK, :]
            rows_ref[base + BLOCK : base + 2 * BLOCK, :] = weights_ref[1, start : start + BLOCK, :]
    out_ref[...] = dot(terms_ref[...], rows_ref[...], 0, 0).astype(BF16)


def call(kernel, out_shape, smem=0, operands=(), scratch=()):
    specs = [pl.BlockSpec(memory_space=pltpu.SMEM if i < smem else pltpu.VMEM) for i in range(len(operands))]
    return pl.pallas_call(
        kernel,
        out_shape=out_shape,
        in_specs=specs,
        scratch_shapes=scratch,
        compiler_params=pltpu.CompilerParams(vmem_limit_bytes=VMEM_LIMIT),
    )(*operands)


def struct(shape, dtype=F32):
    return jax.ShapeDtypeStruct(shape, dtype)


def to_all(value, axes, peers):
    return lax.all_to_all(jnp.broadcast_to(value[None], (peers,) + value.shape), axes, 0, 0)


def swap_pairs():
    pairs = []
    for z in range(16):
        for t in range(8):
            pairs.append((z * 8 + t, (2 * t + z % 2) * 8 + z // 2))
    return pairs


def on_device(acts, grad_out, master, moment_one, moment_two, bit_widths, row_dither, col_dither):
    y = lax.axis_index("y")
    z = lax.axis_index("z")
    core = lax.axis_index("c")
    tensor = lax.axis_index(TENSOR)
    spot = tensor % 4
    unit = 2 * y + tensor // 4
    pos = jnp.stack([core, spot, unit, z]).astype(jnp.int32)
    pairs = swap_pairs()

    coded = eightbit_f32(master).astype(BF16)
    moved = lax.ppermute(coded, ("z",) + TENSOR, pairs)
    all_weights = lax.all_gather(coded, DP, axis=1, tiled=True)

    high = (col_dither // 8).astype(BF16)[None]
    low = (col_dither % 8).astype(BF16)[None]
    extra = jnp.concatenate([high, low, jnp.zeros((14, COLS), BF16)])
    packed = jnp.concatenate([acts, grad_out, extra])
    own = to_all(packed, ("y", "xh", "xl"), 16)
    other = lax.ppermute(own, "c", [(0, 1), (1, 0)])

    rows = to_all(moved, "z", 16)
    rows = rows.reshape(8, 2, 3, SHARD, COLS).transpose(2, 1, 3, 0, 4).reshape(3 * BLOCK, 8 * COLS)
    row_part = lax.dynamic_slice(row_dither, (0, BLOCK * (8 * y + tensor)), (3, BLOCK))
    row_part = jnp.broadcast_to(row_part.astype(F32).reshape(3 * BLOCK, 1) * (1.0 / 1024.0), (3 * BLOCK, COLS))

    xs, gs, terms, col_part, peak = call(
        front_kernel,
        (
            struct((REPS * TOK, 1024), BF16),
            struct((REPS * TOK, 1024), BF16),
            struct((REPS, 3 * BLOCK, TOK), BF16),
            struct((8, 1024)),
            struct((64, 1, COLS)),
        ),
        1,
        (pos, own, other, rows),
    )
    peaks = lax.all_to_all(peak, ("xl", "c", "z"), 0, 0)
    mine = lax.all_to_all(terms[:, : 2 * BLOCK], "y", 0, 0)
    mine = to_all(mine, TENSOR, 8)

    shares = call(
        quant_kernel,
        struct((16, 3, SHARD, COLS)),
        1,
        (pos, xs, gs, terms, peaks, bit_widths, row_part, col_part),
    )
    mean_grad = jnp.sum(lax.all_to_all(shares, "z", 0, 0), axis=0)
    mean_grad = lax.ppermute(mean_grad, ("z",) + TENSOR, pairs)

    updated, first, second, new_coded = call(
        adam_kernel,
        tuple(struct((3, SHARD, COLS)) for _ in range(4)),
        0,
        (mean_grad, master, moment_one, moment_two),
    )
    ring = to_all(new_coded.astype(BF16), "z", 16)
    ring = ring.transpose(1, 0, 2, 3).reshape(3, 16 * SHARD, COLS)
    new_weights = to_all(ring, "y", 4).transpose(1, 0, 2, 3).reshape(3, 64 * SHARD, COLS)

    grad_in = call(
        back_kernel,
        struct((TOK, COLS), BF16),
        0,
        (mine.reshape(64 * BLOCK, TOK), all_weights),
        (pltpu.VMEM((64 * BLOCK, COLS), BF16),),
    )
    return (grad_in, updated, first, second, new_weights)


def solution(mesh):
    grid = Mesh(mesh.devices.reshape(SIZES), DP + TENSOR)
    return jax.shard_map(
        on_device,
        mesh=grid,
        in_specs=(
            P(DP, TENSOR),
            P(DP, TENSOR),
            P(None, DP, TENSOR),
            P(None, DP, TENSOR),
            P(None, DP, TENSOR),
            P(),
            P(),
            P(TENSOR),
        ),
        out_specs=(
            P(DP, TENSOR),
            P(None, DP, TENSOR),
            P(None, DP, TENSOR),
            P(None, DP, TENSOR),
            P(None, None, TENSOR),
        ),
        check_vma=False,
    )
```

```python
import jax
import jax.numpy as jnp
from jax import lax
from jax.experimental import pallas as pl
from jax.experimental.pallas import tpu as pltpu
from jax.sharding import Mesh, PartitionSpec as P

F32 = jnp.float32
BF16 = jnp.bfloat16

TOK = 128
BROWS = 64
COLS = 128
SHARD = 24
BLOCK = 48
REPS = 4

BETA_ONE = 0.9
BETA_TWO = 0.95
LEARN_RATE = 0.004
WEIGHT_DECAY = 0.1
ADAM_EPS = 1e-08
RANGE_EPS = 1e-06
N_DP = 64

SINE = (
    0.9999995827674866,
    -6.579691410064697,
    12.986435890197754,
    -12.188101768493652,
    6.558042526245117,
    -1.95303213596344,
)

DP = ("y", "z")
TENSOR = ("xh", "xl", "c")
SIZES = (4, 16, 2, 2, 2)

VMEM_LIMIT = 20 * 1024 * 1024


def turn(value):
    frac = value - jnp.floor(value + 0.5)
    square = frac * frac
    total = jnp.full_like(square, SINE[-1])
    for coef in SINE[-2::-1]:
        total = total * square + coef
    return total * frac


def soft_round(value):
    return value - turn(value)


def eightbit_f32(weights):
    scale = (jnp.max(jnp.abs(weights), axis=-1, keepdims=True) + RANGE_EPS) / 127.0
    return soft_round(weights / scale) * scale


def dot(left, right, left_dim, right_dim):
    return lax.dot_general(
        left, right, (((left_dim,), (right_dim,)), ((), ())), preferred_element_type=F32
    )


def pack_kernel(acts_ref, grad_ref, dither_ref, master_ref, one_ref, two_ref, packed_ref, state_ref):
    high = (dither_ref[...] >> 3).astype(F32)
    low = (dither_ref[...] & 7).astype(F32)
    row = lax.broadcasted_iota(jnp.int32, (16, COLS), 0)
    extra = jnp.where(row == 0, high, jnp.where(row == 1, low, 0.0)).astype(BF16)
    for peer in range(16):
        packed_ref[peer, 0:TOK, :] = acts_ref[...]
        packed_ref[peer, TOK : 2 * TOK, :] = grad_ref[...]
        packed_ref[peer, 2 * TOK : 2 * TOK + 16, :] = extra
    state_ref[0] = master_ref[...]
    state_ref[1] = one_ref[...]
    state_ref[2] = two_ref[...]


def code_kernel(state_ref, coded_ref):
    coded_ref[...] = eightbit_f32(state_ref[0])


def front_kernel(pos_ref, own_ref, other_ref, weights_ref, xs_ref, gs_ref, terms_ref, col_ref, peak_ref, keep_ref, give_ref):
    core = pos_ref[0]
    for chip in range(4):
        for source, which in ((own_ref, core), (other_ref, 1 - core)):
            cols = pl.ds(pl.multiple_of((2 * chip + which) * COLS, COLS), COLS)
            for rep in range(REPS):
                rows = slice(rep * TOK, (rep + 1) * TOK)
                xs_ref[rows, cols] = source[rep * 4 + chip, 0:TOK, :]
                gs_ref[rows, cols] = source[rep * 4 + chip, TOK : 2 * TOK, :]
            pair = source[chip, 2 * TOK : 2 * TOK + 16, :].astype(F32)
            dither = pair[0:1] * 8.0 + pair[1:2]
            col_ref[:, cols] = jnp.broadcast_to(dither * (1.0 / 1024.0), (8, COLS))
    front = dot(weights_ref[0 : 2 * BLOCK, :], xs_ref[...], 1, 1)
    delta = dot(weights_ref[2 * BLOCK : 3 * BLOCK, :], gs_ref[...], 1, 1)
    gate = front[0:BLOCK]
    upper = front[BLOCK:]
    sig = jax.nn.sigmoid(gate)
    active = gate * sig
    dgate = (delta * upper * sig * (1.0 + gate * (1.0 - sig))).astype(BF16)
    dupper = (delta * active).astype(BF16)
    hidden = (active * upper).astype(BF16)
    terms = jnp.concatenate([dgate, dupper], axis=0)
    for target, which in ((keep_ref, core), (give_ref, 1 - core)):
        side = []
        for chip in range(4):
            cols = pl.ds(pl.multiple_of((2 * chip + which) * COLS, COLS), COLS)
            side.append(weights_ref[0 : 2 * BLOCK, cols])
        back = dot(terms, jnp.concatenate(side, axis=1), 0, 0)
        for rep in range(REPS):
            for chip in range(4):
                target[rep * 4 + chip] = back[rep * TOK : (rep + 1) * TOK, chip * COLS : (chip + 1) * COLS]
    peak = jnp.zeros((3 * BLOCK, COLS), F32)
    for rep in range(REPS):
        rows = slice(rep * TOK, (rep + 1) * TOK)
        terms_ref[rep, 0:BLOCK, :] = dgate[:, rows]
        terms_ref[rep, BLOCK : 2 * BLOCK, :] = dupper[:, rows]
        terms_ref[rep, 2 * BLOCK : 3 * BLOCK, :] = hidden[:, rows]
        for part in range(4):
            cols = slice(part * 256, (part + 1) * 256)
            grad_front = dot(terms_ref[rep, 0 : 2 * BLOCK, :], xs_ref[rows, cols], 1, 0)
            grad_down = dot(terms_ref[rep, 2 * BLOCK : 3 * BLOCK, :], gs_ref[rows, cols], 1, 0)
            grads = jnp.abs(jnp.concatenate([grad_front, grad_down], axis=0))
            peak = jnp.maximum(peak, jnp.maximum(grads[:, :COLS], grads[:, COLS:]))
    lane = lax.broadcasted_iota(jnp.int32, (1, COLS), 1)
    packed = jnp.zeros((1, COLS), F32)
    for group in range(9):
        top = jnp.max(peak[group * 16 : (group + 1) * 16], axis=0, keepdims=True)
        top = jnp.max(top, axis=1, keepdims=True)
        packed = jnp.where(lane == group, top, packed)
    peak_ref[...] = jnp.broadcast_to(packed.reshape(1, 1, COLS), peak_ref.shape)


def quant_kernel(pos_ref, xs_ref, gs_ref, terms_ref, peaks_ref, bits_ref, row_ref, col_ref, keep_ref, got_ref, out_ref, *back_refs):
    plane = pos_ref[4]
    for step, back_ref in enumerate(back_refs):
        first = ((plane + step) % 4) * 4
        for chip in range(4):
            back_ref[chip] = keep_ref[first + chip] + got_ref[first + chip]
    spot = pos_ref[1]
    unit = pos_ref[2]
    depth = pos_ref[3]
    lane = lax.broadcasted_iota(jnp.int32, (1, COLS), 1)
    buck = lax.broadcasted_iota(jnp.int32, (1, 24), 1)
    tops = [jnp.max(peaks_ref[i * 16 : (i + 1) * 16], axis=0) for i in range(4)]
    scales = []
    for mat in range(3):
        per_bucket = []
        for bucket in range(3):
            held = jnp.zeros((1, COLS), F32)
            for sub in range(4 * bucket, 4 * bucket + 4):
                held = jnp.maximum(held, jnp.where(lane == mat * 3 + sub % 3, tops[sub // 3], 0.0))
            ranges = jnp.max(held, axis=1, keepdims=True)
            bits = jnp.where(buck == 3 * unit + bucket, bits_ref[mat : mat + 1, :].astype(F32), 0.0)
            bits = jnp.max(bits, axis=1, keepdims=True)
            levels = jnp.ones_like(bits)
            for count in range(3, 9):
                levels = jnp.where(bits == float(count), float(2 ** (count - 1) - 1), levels)
            per_bucket.append((ranges + RANGE_EPS) / levels)
        for sub in range(3):
            which = (3 * spot + sub) // 4
            chosen = jnp.where(which == 0, per_bucket[0], jnp.where(which == 1, per_bucket[1], per_bucket[2]))
            scales.append(jnp.broadcast_to(chosen, (16, COLS)))
    scale = jnp.concatenate(scales, axis=0)
    inverse = 1.0 / scale
    scale = scale * (1.0 / N_DP)
    row_part = row_ref[...]
    for part in range(4):
        cols = slice(part * 256, (part + 1) * 256)
        halves = [jnp.zeros((3 * BLOCK, COLS), F32) for _ in range(2)]
        for rep in range(REPS):
            rows = slice(rep * TOK, (rep + 1) * TOK)
            grad_front = dot(terms_ref[rep, 0 : 2 * BLOCK, :], xs_ref[rows, cols], 1, 0)
            grad_down = dot(terms_ref[rep, 2 * BLOCK : 3 * BLOCK, :], gs_ref[rows, cols], 1, 0)
            grads = jnp.concatenate([grad_front, grad_down], axis=0)
            offset = lax.rem(389 * (rep * 16 + depth), 1024).astype(F32) * (1.0 / 1024.0)
            for half in range(2):
                lanes = slice(half * COLS, (half + 1) * COLS)
                whole = slice(part * 256 + half * COLS, part * 256 + (half + 1) * COLS)
                ratio = grads[:, lanes] * inverse
                phase = row_part + (col_ref[0:1, whole] + offset)
                halves[half] = halves[half] + (ratio + turn(ratio + phase))
        for half in range(2):
            result = halves[half] * scale
            for mat in range(3):
                for low in range(2):
                    start = mat * BLOCK + low * SHARD
                    out_ref[2 * (2 * part + half) + low, mat, :, :] = result[start : start + SHARD]


def adam_kernel(pos_ref, shares_ref, state_ref, own_ref, up_ref, across_ref, down_ref, new_state_ref, coded_ref, *back_refs):
    chip = pos_ref[5]
    for step, back_ref in enumerate(back_refs):
        which = (chip + step) % 4
        back_ref[...] = (own_ref[which] + up_ref[which]) + (across_ref[which] + down_ref[which])
    mean_grad = shares_ref[0]
    for peer in range(1, 16):
        mean_grad = mean_grad + shares_ref[peer]
    master = state_ref[0]
    first = BETA_ONE * state_ref[1] + (1.0 - BETA_ONE) * mean_grad
    second = BETA_TWO * state_ref[2] + (1.0 - BETA_TWO) * mean_grad * mean_grad
    updated = master - LEARN_RATE * (first / (jnp.sqrt(second) + ADAM_EPS) + WEIGHT_DECAY * master)
    new_state_ref[0] = updated
    new_state_ref[1] = first
    new_state_ref[2] = second
    coded_ref[...] = eightbit_f32(updated)


def call(kernel, out_shape, smem=0, operands=()):
    specs = [pl.BlockSpec(memory_space=pltpu.SMEM if i < smem else pltpu.VMEM) for i in range(len(operands))]
    return pl.pallas_call(
        kernel,
        out_shape=out_shape,
        in_specs=specs,
        compiler_params=pltpu.CompilerParams(vmem_limit_bytes=VMEM_LIMIT),
    )(*operands)


def struct(shape, dtype=F32):
    return jax.ShapeDtypeStruct(shape, dtype)


def to_all(value, axes, peers):
    return lax.all_to_all(jnp.broadcast_to(value[None], (peers,) + value.shape), axes, 0, 0)


def shift(value, axes, step):
    return lax.ppermute(value, axes, [(i, (i + step) % 4) for i in range(4)])


def swap_pairs():
    pairs = []
    for z in range(16):
        for t in range(8):
            pairs.append((z * 8 + t, (2 * t + z % 2) * 8 + z // 2))
    return pairs


def on_device(acts, grad_out, master, moment_one, moment_two, bit_widths, row_dither, col_dither):
    y = lax.axis_index("y")
    z = lax.axis_index("z")
    core = lax.axis_index("c")
    tensor = lax.axis_index(TENSOR)
    spot = tensor % 4
    unit = 2 * y + tensor // 4
    pos = jnp.stack([core, spot, unit, z, y, tensor // 2]).astype(jnp.int32)
    pairs = swap_pairs()

    packed, state = call(
        pack_kernel,
        (struct((16, 2 * TOK + 16, COLS), BF16), struct((3, 3, SHARD, COLS))),
        0,
        (acts, grad_out, col_dither[None], master, moment_one, moment_two),
    )
    state = lax.ppermute(state, ("z",) + TENSOR, pairs)
    coded = call(code_kernel, struct((3, SHARD, COLS)), 0, (state,))
    rows = to_all(coded.astype(BF16), "z", 16)
    own = lax.all_to_all(packed, ("y", "xh", "xl"), 0, 0)
    other = lax.ppermute(own, "c", [(0, 1), (1, 0)])

    rows = rows.reshape(8, 2, 3, SHARD, COLS).transpose(2, 1, 3, 0, 4).reshape(3 * BLOCK, 8 * COLS)
    row_part = lax.dynamic_slice(row_dither, (0, BLOCK * (8 * y + tensor)), (3, BLOCK))
    row_part = jnp.broadcast_to(row_part.astype(F32).reshape(3 * BLOCK, 1) * (1.0 / 1024.0), (3 * BLOCK, COLS))

    xs, gs, terms, col_part, peak, keep, give = call(
        front_kernel,
        (
            struct((REPS * TOK, 1024), BF16),
            struct((REPS * TOK, 1024), BF16),
            struct((REPS, 3 * BLOCK, TOK), BF16),
            struct((8, 1024)),
            struct((64, 1, COLS)),
            struct((16, TOK, COLS)),
            struct((16, TOK, COLS)),
        ),
        1,
        (pos, own, other, rows),
    )
    peaks = lax.all_to_all(peak, ("xl", "c", "z"), 0, 0)
    got = lax.ppermute(give, "c", [(0, 1), (1, 0)])

    shares, *back = call(
        quant_kernel,
        (struct((16, 3, SHARD, COLS)),) + (struct((4, TOK, COLS)),) * 4,
        1,
        (pos, xs, gs, terms, peaks, bit_widths, row_part, col_part, keep, got),
    )
    back = [back[0]] + [shift(back[step], "y", step) for step in (1, 2, 3)]
    shares = lax.all_to_all(shares, "z", 0, 0)

    new_state, new_coded, *back = call(
        adam_kernel,
        (struct((3, 3, SHARD, COLS)), struct((3, SHARD, COLS))) + (struct((TOK, COLS)),) * 4,
        1,
        (pos, shares, state, *back),
    )
    back = [back[0]] + [shift(back[step], ("xh", "xl"), step) for step in (1, 2, 3)]
    ring = to_all(new_coded.astype(BF16), "z", 16)
    new_state = lax.ppermute(new_state, ("z",) + TENSOR, pairs)
    grad_in = ((back[0] + back[1]) + (back[2] + back[3])).astype(BF16)
    ring = jnp.broadcast_to(ring.reshape(1, 8, 2, 3, SHARD, COLS), (4, 8, 2, 3, SHARD, COLS))
    ring = lax.all_to_all(ring.reshape(32, 2, 3, SHARD, COLS), ("y",) + TENSOR, 0, 0)
    new_weights = ring.transpose(2, 0, 1, 3, 4).reshape(3, 64 * SHARD, COLS)
    return (grad_in, new_state[0], new_state[1], new_state[2], new_weights)


def solution(mesh):
    grid = Mesh(mesh.devices.reshape(SIZES), DP + TENSOR)
    return jax.shard_map(
        on_device,
        mesh=grid,
        in_specs=(
            P(DP, TENSOR),
            P(DP, TENSOR),
            P(None, DP, TENSOR),
            P(None, DP, TENSOR),
            P(None, DP, TENSOR),
            P(),
            P(),
            P(TENSOR),
        ),
        out_specs=(
            P(DP, TENSOR),
            P(None, DP, TENSOR),
            P(None, DP, TENSOR),
            P(None, DP, TENSOR),
            P(None, None, TENSOR),
        ),
        check_vma=False,
    )
```

```python
import jax
import jax.numpy as jnp
from jax import lax
from jax.experimental import pallas as pl
from jax.experimental.pallas import tpu as pltpu
from jax.sharding import Mesh, PartitionSpec as P

F32 = jnp.float32
BF16 = jnp.bfloat16

TOK = 128
BROWS = 64
COLS = 128
SHARD = 24
BLOCK = 48
REPS = 4

BETA_ONE = 0.9
BETA_TWO = 0.95
LEARN_RATE = 0.004
WEIGHT_DECAY = 0.1
ADAM_EPS = 1e-08
RANGE_EPS = 1e-06
N_DP = 64

SINE = (
    0.9999995827674866,
    -6.579691410064697,
    12.986435890197754,
    -12.188101768493652,
    6.558042526245117,
    -1.95303213596344,
)

Z = ("zh", "zl")
DP = ("y",) + Z
TENSOR = ("xh", "xl", "c")
SIZES = (4, 4, 4, 2, 2, 2)

SMALL_LIMIT = 20 * 1024 * 1024
LARGE_LIMIT = 60 * 1024 * 1024


def turn(value):
    frac = value - jnp.floor(value + 0.5)
    square = frac * frac
    total = jnp.full_like(square, SINE[-1])
    for coef in SINE[-2::-1]:
        total = total * square + coef
    return total * frac


def soft_round(value):
    return value - turn(value)


def eightbit_f32(weights):
    scale = (jnp.max(jnp.abs(weights), axis=-1, keepdims=True) + RANGE_EPS) / 127.0
    return soft_round(weights / scale) * scale


def dot(left, right, left_dim, right_dim):
    return lax.dot_general(
        left, right, (((left_dim,), (right_dim,)), ((), ())), preferred_element_type=F32
    )


def pack_kernel(acts_ref, grad_ref, dither_ref, master_ref, one_ref, two_ref, packed_ref, state_ref):
    high = (dither_ref[...] >> 3).astype(F32)
    low = (dither_ref[...] & 7).astype(F32)
    row = lax.broadcasted_iota(jnp.int32, (16, COLS), 0)
    extra = jnp.where(row == 0, high, jnp.where(row == 1, low, 0.0)).astype(BF16)
    for peer in range(16):
        packed_ref[peer, 0:TOK, :] = acts_ref[...]
        packed_ref[peer, TOK : 2 * TOK, :] = grad_ref[...]
        packed_ref[peer, 2 * TOK : 2 * TOK + 16, :] = extra
    state_ref[0] = master_ref[...]
    state_ref[1] = one_ref[...]
    state_ref[2] = two_ref[...]


def code_kernel(state_ref, coded_ref):
    coded_ref[...] = eightbit_f32(state_ref[0])


def spread_kernel(own_ref, *refs):
    parts, (_, out_ref, wide_ref) = refs[:4], refs[4:]
    for step, part in enumerate(parts):
        wide_ref[step * 3 * SHARD : (step + 1) * 3 * SHARD, :] = part[...].astype(F32)
    narrow = wide_ref[...].astype(BF16)
    for peer in range(4):
        out_ref[peer] = narrow


def front_kernel(pos_ref, own_ref, other_ref, rows_ref, xs_ref, gs_ref, terms_ref, col_ref, peak_ref, keep_ref, give_ref, wide_ref, full_ref, weights_ref):
    core = pos_ref[0]
    for chip in range(4):
        for source, which in ((own_ref, core), (other_ref, 1 - core)):
            cols = pl.ds(pl.multiple_of((2 * chip + which) * COLS, COLS), COLS)
            for rep in range(REPS):
                rows = slice(rep * TOK, (rep + 1) * TOK)
                xs_ref[rows, cols] = source[rep * 4 + chip, 0:TOK, :]
                gs_ref[rows, cols] = source[rep * 4 + chip, TOK : 2 * TOK, :]
            pair = source[chip, 2 * TOK : 2 * TOK + 16, :].astype(F32)
            dither = pair[0:1] * 8.0 + pair[1:2]
            col_ref[:, cols] = jnp.broadcast_to(dither * (1.0 / 1024.0), (8, COLS))
    wide_ref[...] = rows_ref[...].astype(F32)
    for low in range(4):
        for step in range(4):
            column = 2 * ((pos_ref[6] + 4 - step) % 4) + low // 2
            cols = pl.ds(pl.multiple_of(column * COLS, COLS), COLS)
            for mat in range(3):
                source = ((low * 4 + step) * 3 + mat) * SHARD
                target = mat * BLOCK + (low % 2) * SHARD
                full_ref[target : target + SHARD, cols] = wide_ref[source : source + SHARD, :]
    weights_ref[...] = full_ref[...].astype(BF16)
    front = dot(weights_ref[0 : 2 * BLOCK, :], xs_ref[...], 1, 1)
    delta = dot(weights_ref[2 * BLOCK : 3 * BLOCK, :], gs_ref[...], 1, 1)
    gate = front[0:BLOCK]
    upper = front[BLOCK:]
    sig = jax.nn.sigmoid(gate)
    active = gate * sig
    dgate = (delta * upper * sig * (1.0 + gate * (1.0 - sig))).astype(BF16)
    dupper = (delta * active).astype(BF16)
    hidden = (active * upper).astype(BF16)
    terms = jnp.concatenate([dgate, dupper], axis=0)
    for target, which in ((keep_ref, core), (give_ref, 1 - core)):
        side = []
        for chip in range(4):
            cols = pl.ds(pl.multiple_of((2 * chip + which) * COLS, COLS), COLS)
            side.append(weights_ref[0 : 2 * BLOCK, cols])
        back = dot(terms, jnp.concatenate(side, axis=1), 0, 0)
        for rep in range(REPS):
            for chip in range(4):
                target[rep * 4 + chip] = back[rep * TOK : (rep + 1) * TOK, chip * COLS : (chip + 1) * COLS]
    peak = jnp.zeros((3 * BLOCK, COLS), F32)
    for rep in range(REPS):
        rows = slice(rep * TOK, (rep + 1) * TOK)
        terms_ref[rep, 0:BLOCK, :] = dgate[:, rows]
        terms_ref[rep, BLOCK : 2 * BLOCK, :] = dupper[:, rows]
        terms_ref[rep, 2 * BLOCK : 3 * BLOCK, :] = hidden[:, rows]
        for part in range(4):
            cols = slice(part * 256, (part + 1) * 256)
            grad_front = dot(terms_ref[rep, 0 : 2 * BLOCK, :], xs_ref[rows, cols], 1, 0)
            grad_down = dot(terms_ref[rep, 2 * BLOCK : 3 * BLOCK, :], gs_ref[rows, cols], 1, 0)
            grads = jnp.abs(jnp.concatenate([grad_front, grad_down], axis=0))
            peak = jnp.maximum(peak, jnp.maximum(grads[:, :COLS], grads[:, COLS:]))
    lane = lax.broadcasted_iota(jnp.int32, (1, COLS), 1)
    packed = jnp.zeros((1, COLS), F32)
    for group in range(9):
        top = jnp.max(peak[group * 16 : (group + 1) * 16], axis=0, keepdims=True)
        top = jnp.max(top, axis=1, keepdims=True)
        packed = jnp.where(lane == group, top, packed)
    peak_ref[...] = jnp.broadcast_to(packed.reshape(1, 1, COLS), peak_ref.shape)


def quant_kernel(pos_ref, xs_ref, gs_ref, terms_ref, peaks_ref, bits_ref, row_ref, col_ref, keep_ref, got_ref, out_ref, *back_refs):
    plane = pos_ref[4]
    for step, back_ref in enumerate(back_refs):
        first = ((plane + step) % 4) * 4
        for chip in range(4):
            back_ref[chip] = keep_ref[first + chip] + got_ref[first + chip]
    spot = pos_ref[1]
    unit = pos_ref[2]
    depth = pos_ref[3]
    lane = lax.broadcasted_iota(jnp.int32, (1, COLS), 1)
    buck = lax.broadcasted_iota(jnp.int32, (1, 24), 1)
    tops = [jnp.max(peaks_ref[i * 16 : (i + 1) * 16], axis=0) for i in range(4)]
    scales = []
    for mat in range(3):
        per_bucket = []
        for bucket in range(3):
            held = jnp.zeros((1, COLS), F32)
            for sub in range(4 * bucket, 4 * bucket + 4):
                held = jnp.maximum(held, jnp.where(lane == mat * 3 + sub % 3, tops[sub // 3], 0.0))
            ranges = jnp.max(held, axis=1, keepdims=True)
            bits = jnp.where(buck == 3 * unit + bucket, bits_ref[mat : mat + 1, :].astype(F32), 0.0)
            bits = jnp.max(bits, axis=1, keepdims=True)
            levels = jnp.ones_like(bits)
            for count in range(3, 9):
                levels = jnp.where(bits == float(count), float(2 ** (count - 1) - 1), levels)
            per_bucket.append((ranges + RANGE_EPS) / levels)
        for sub in range(3):
            which = (3 * spot + sub) // 4
            chosen = jnp.where(which == 0, per_bucket[0], jnp.where(which == 1, per_bucket[1], per_bucket[2]))
            scales.append(jnp.broadcast_to(chosen, (16, COLS)))
    scale = jnp.concatenate(scales, axis=0)
    inverse = 1.0 / scale
    scale = scale * (1.0 / N_DP)
    row_part = row_ref[...]
    for part in range(4):
        cols = slice(part * 256, (part + 1) * 256)
        halves = [jnp.zeros((3 * BLOCK, COLS), F32) for _ in range(2)]
        for rep in range(REPS):
            rows = slice(rep * TOK, (rep + 1) * TOK)
            grad_front = dot(terms_ref[rep, 0 : 2 * BLOCK, :], xs_ref[rows, cols], 1, 0)
            grad_down = dot(terms_ref[rep, 2 * BLOCK : 3 * BLOCK, :], gs_ref[rows, cols], 1, 0)
            grads = jnp.concatenate([grad_front, grad_down], axis=0)
            offset = lax.rem(389 * (rep * 16 + depth), 1024).astype(F32) * (1.0 / 1024.0)
            for half in range(2):
                lanes = slice(half * COLS, (half + 1) * COLS)
                whole = slice(part * 256 + half * COLS, part * 256 + (half + 1) * COLS)
                ratio = grads[:, lanes] * inverse
                phase = row_part + (col_ref[0:1, whole] + offset)
                halves[half] = halves[half] + (ratio + turn(ratio + phase))
        for half in range(2):
            result = halves[half] * scale
            for mat in range(3):
                for low in range(2):
                    start = mat * BLOCK + low * SHARD
                    out_ref[2 * (2 * part + half) + low, mat, :, :] = result[start : start + SHARD]


def adam_kernel(pos_ref, shares_ref, state_ref, own_ref, up_ref, across_ref, down_ref, new_state_ref, coded_ref, *back_refs):
    chip = pos_ref[5]
    for step, back_ref in enumerate(back_refs):
        which = (chip + step) % 4
        back_ref[...] = (own_ref[which] + up_ref[which]) + (across_ref[which] + down_ref[which])
    mean_grad = shares_ref[0]
    for peer in range(1, 16):
        mean_grad = mean_grad + shares_ref[peer]
    master = state_ref[0]
    first = BETA_ONE * state_ref[1] + (1.0 - BETA_ONE) * mean_grad
    second = BETA_TWO * state_ref[2] + (1.0 - BETA_TWO) * mean_grad * mean_grad
    updated = master - LEARN_RATE * (first / (jnp.sqrt(second) + ADAM_EPS) + WEIGHT_DECAY * master)
    new_state_ref[0] = updated
    new_state_ref[1] = first
    new_state_ref[2] = second
    coded_ref[...] = eightbit_f32(updated)


def call(kernel, out_shape, smem=0, operands=(), scratch=(), limit=SMALL_LIMIT):
    single = not isinstance(out_shape, tuple)
    outs = (out_shape,) if single else out_shape
    n_in = len(operands) - smem
    n_out = len(outs)

    def body(*refs):
        small = refs[:smem]
        sources = refs[smem : smem + n_in]
        targets = refs[smem + n_in : smem + n_in + n_out]
        held = refs[smem + n_in + n_out :]
        taken, made, rest, sems = held[:n_in], held[n_in : n_in + n_out], held[n_in + n_out : -1], held[-1]
        loads = [pltpu.make_async_copy(sources[i], taken[i], sems.at[i]) for i in range(n_in)]
        for load in loads:
            load.start()
        for load in loads:
            load.wait()
        kernel(*small, *taken, *made, *rest)
        stores = [pltpu.make_async_copy(made[i], targets[i], sems.at[n_in + i]) for i in range(n_out)]
        for store in stores:
            store.start()
        for store in stores:
            store.wait()

    anywhere = pl.BlockSpec(memory_space=pl.ANY)
    specs = [pl.BlockSpec(memory_space=pltpu.SMEM)] * smem + [anywhere] * n_in
    buffers = [pltpu.VMEM(item.shape, item.dtype) for item in tuple(operands[smem:]) + outs]
    return pl.pallas_call(
        body,
        out_shape=out_shape,
        in_specs=specs,
        out_specs=anywhere if single else (anywhere,) * n_out,
        scratch_shapes=buffers + list(scratch) + [pltpu.SemaphoreType.DMA((n_in + n_out,))],
        compiler_params=pltpu.CompilerParams(vmem_limit_bytes=limit),
    )(*operands)


def struct(shape, dtype=F32):
    return jax.ShapeDtypeStruct(shape, dtype)


def to_all(value, axes, peers):
    return lax.all_to_all(jnp.broadcast_to(value[None], (peers,) + value.shape), axes, 0, 0)


def shift(value, axes, step):
    return lax.ppermute(value, axes, [(i, (i + step) % 4) for i in range(4)])


def swap_pairs():
    pairs = []
    for z in range(16):
        for t in range(8):
            pairs.append((z * 8 + t, (2 * t + z % 2) * 8 + z // 2))
    return pairs


def on_device(acts, grad_out, master, moment_one, moment_two, bit_widths, row_dither, col_dither):
    y = lax.axis_index("y")
    z = lax.axis_index(Z)
    core = lax.axis_index("c")
    tensor = lax.axis_index(TENSOR)
    spot = tensor % 4
    unit = 2 * y + tensor // 4
    pos = jnp.stack([core, spot, unit, z, y, tensor // 2, z // 4]).astype(jnp.int32)
    pairs = swap_pairs()

    packed, state = call(
        pack_kernel,
        (struct((16, 2 * TOK + 16, COLS), BF16), struct((3, 3, SHARD, COLS))),
        0,
        (acts, grad_out, col_dither[None], master, moment_one, moment_two),
        limit=LARGE_LIMIT,
    )
    state = lax.ppermute(state, Z + TENSOR, pairs)
    coded = call(code_kernel, struct((3, SHARD, COLS)), 0, (state,))
    coded = coded.astype(BF16).reshape(3 * SHARD, COLS)
    parts = [coded] + [shift(coded, "zh", step) for step in (1, 2, 3)]
    own = lax.all_to_all(packed, ("y", "xh", "xl"), 0, 0)
    own, rows = pl.pallas_call(
        spread_kernel,
        out_shape=(struct(own.shape, BF16), struct((4, 12 * SHARD, COLS), BF16)),
        in_specs=[pl.BlockSpec(memory_space=pl.ANY)] + [pl.BlockSpec(memory_space=pltpu.VMEM)] * 4,
        out_specs=(pl.BlockSpec(memory_space=pl.ANY), pl.BlockSpec(memory_space=pltpu.VMEM)),
        scratch_shapes=[pltpu.VMEM((12 * SHARD, COLS), F32)],
        input_output_aliases={0: 0},
        compiler_params=pltpu.CompilerParams(vmem_limit_bytes=SMALL_LIMIT),
    )(own, *parts)
    rows = lax.all_to_all(rows, "zl", 0, 0).reshape(16 * 3 * SHARD, COLS)
    other = lax.ppermute(own, "c", [(0, 1), (1, 0)])

    row_part = lax.dynamic_slice(row_dither, (0, BLOCK * (8 * y + tensor)), (3, BLOCK))
    row_part = jnp.broadcast_to(row_part.astype(F32).reshape(3 * BLOCK, 1) * (1.0 / 1024.0), (3 * BLOCK, COLS))

    xs, gs, terms, col_part, peak, keep, give = call(
        front_kernel,
        (
            struct((REPS * TOK, 1024), BF16),
            struct((REPS * TOK, 1024), BF16),
            struct((REPS, 3 * BLOCK, TOK), BF16),
            struct((8, 1024)),
            struct((64, 1, COLS)),
            struct((16, TOK, COLS)),
            struct((16, TOK, COLS)),
        ),
        1,
        (pos, own, other, rows),
        (
            pltpu.VMEM((48 * SHARD, COLS), F32),
            pltpu.VMEM((3 * BLOCK, 1024), F32),
            pltpu.VMEM((3 * BLOCK, 1024), BF16),
        ),
        limit=LARGE_LIMIT,
    )
    peaks = lax.all_to_all(peak, ("xl", "c") + Z, 0, 0)
    got = lax.ppermute(give, "c", [(0, 1), (1, 0)])

    shares, *back = call(
        quant_kernel,
        (struct((16, 3, SHARD, COLS)),) + (struct((4, TOK, COLS)),) * 4,
        1,
        (pos, xs, gs, terms, peaks, bit_widths, row_part, col_part, keep, got),
        limit=LARGE_LIMIT,
    )
    back = [back[0]] + [shift(back[step], "y", step) for step in (1, 2, 3)]
    shares = lax.all_to_all(shares, Z, 0, 0)

    new_state, new_coded, *back = call(
        adam_kernel,
        (struct((3, 3, SHARD, COLS)), struct((3, SHARD, COLS))) + (struct((TOK, COLS)),) * 4,
        1,
        (pos, shares, state, *back),
    )
    back = [back[0]] + [shift(back[step], ("xh", "xl"), step) for step in (1, 2, 3)]
    ring = to_all(new_coded.astype(BF16), Z, 16)
    new_state = lax.ppermute(new_state, Z + TENSOR, pairs)
    grad_in = ((back[0] + back[1]) + (back[2] + back[3])).astype(BF16)
    ring = jnp.broadcast_to(ring.reshape(1, 8, 2, 3, SHARD, COLS), (4, 8, 2, 3, SHARD, COLS))
    ring = lax.all_to_all(ring.reshape(32, 2, 3, SHARD, COLS), ("y",) + TENSOR, 0, 0)
    new_weights = ring.transpose(2, 0, 1, 3, 4).reshape(3, 64 * SHARD, COLS)
    return (grad_in, new_state[0], new_state[1], new_state[2], new_weights)


def solution(mesh):
    grid = Mesh(mesh.devices.reshape(SIZES), DP + TENSOR)
    return jax.shard_map(
        on_device,
        mesh=grid,
        in_specs=(
            P(DP, TENSOR),
            P(DP, TENSOR),
            P(None, DP, TENSOR),
            P(None, DP, TENSOR),
            P(None, DP, TENSOR),
            P(),
            P(),
            P(TENSOR),
        ),
        out_specs=(
            P(DP, TENSOR),
            P(None, DP, TENSOR),
            P(None, DP, TENSOR),
            P(None, DP, TENSOR),
            P(None, None, TENSOR),
        ),
        check_vma=False,
    )
```

```python
import jax
import jax.numpy as jnp
from jax import lax
from jax.experimental import pallas as pl
from jax.experimental.pallas import tpu as pltpu
from jax.sharding import Mesh, PartitionSpec as P

F32 = jnp.float32
BF16 = jnp.bfloat16

TOK = 128
BROWS = 64
COLS = 128
SHARD = 24
BLOCK = 48
PACK = 2 * TOK + 16
REPS = 4

BETA_ONE = 0.9
BETA_TWO = 0.95
LEARN_RATE = 0.004
WEIGHT_DECAY = 0.1
ADAM_EPS = 1e-08
RANGE_EPS = 1e-06
N_DP = 64

SINE = (
    0.9999995827674866,
    -6.579691410064697,
    12.986435890197754,
    -12.188101768493652,
    6.558042526245117,
    -1.95303213596344,
)

Z = ("zh", "zl")
DP = ("y",) + Z
TENSOR = ("xh", "xl", "c")
SIZES = (4, 4, 4, 2, 2, 2)

SMALL_LIMIT = 20 * 1024 * 1024
LARGE_LIMIT = 60 * 1024 * 1024


def turn(value):
    frac = value - jnp.floor(value + 0.5)
    square = frac * frac
    total = jnp.full_like(square, SINE[-1])
    for coef in SINE[-2::-1]:
        total = total * square + coef
    return total * frac


def soft_round(value):
    return value - turn(value)


def eightbit_f32(weights):
    scale = (jnp.max(jnp.abs(weights), axis=-1, keepdims=True) + RANGE_EPS) / 127.0
    return soft_round(weights / scale) * scale


def dot(left, right, left_dim, right_dim):
    return lax.dot_general(
        left, right, (((left_dim,), (right_dim,)), ((), ())), preferred_element_type=F32
    )


def pack_kernel(acts_ref, grad_ref, dither_ref, master_ref, one_ref, two_ref, packed_ref, state_ref):
    high = (dither_ref[...] >> 3).astype(F32)
    low = (dither_ref[...] & 7).astype(F32)
    row = lax.broadcasted_iota(jnp.int32, (16, COLS), 0)
    extra = jnp.where(row == 0, high, jnp.where(row == 1, low, 0.0)).astype(BF16)
    packed_ref[0:TOK, :] = acts_ref[...]
    packed_ref[TOK : 2 * TOK, :] = grad_ref[...]
    packed_ref[2 * TOK : PACK, :] = extra
    state_ref[0] = master_ref[...]
    state_ref[1] = one_ref[...]
    state_ref[2] = two_ref[...]


def spread_kernel(state_ref, *refs):
    parts, (coded_ref, joined_ref, wide_ref) = refs[:4], refs[4:]
    coded = eightbit_f32(state_ref[0])
    for mat in range(6):
        wide_ref[mat * SHARD : (mat + 1) * SHARD, :] = coded[mat % 3]
    narrow = wide_ref[...].astype(BF16)
    for pair in range(8):
        coded_ref[pair * 6 * SHARD : (pair + 1) * 6 * SHARD, :] = narrow
    for step, part in enumerate(parts):
        joined_ref[step] = part[...]


def front_kernel(need, done, pos_ref, *refs):
    planes, refs = (refs[:4], refs[4:8]), refs[8:]
    rows_ref, xs_ref, gs_ref, terms_ref, col_ref, peak_ref, keep_ref, give_ref = refs[:8]
    wide_ref, full_ref, weights_ref = refs[8:]
    core = pos_ref[0]
    need(8)
    wide_ref[...] = rows_ref[...].astype(F32)
    for depth in range(16):
        cols = slice((depth // 2) * COLS, (depth // 2 + 1) * COLS)
        for mat in range(3):
            source = (depth * 3 + mat) * SHARD
            target = mat * BLOCK + (depth % 2) * SHARD
            full_ref[target : target + SHARD, cols] = wide_ref[source : source + SHARD, :]
    weights_ref[...] = full_ref[...].astype(BF16)
    for step in range(REPS):
        rep = (pos_ref[4] + 4 - step) % 4
        rows = pl.ds(pl.multiple_of(rep * TOK, TOK), TOK)
        for side, which in ((0, core), (1, 1 - core)):
            group = planes[side]
            need(4 * side + step)
            for chip in range(4):
                column = (pos_ref[5] + 4 - chip) % 4
                cols = pl.ds(pl.multiple_of((2 * column + which) * COLS, COLS), COLS)
                xs_ref[rows, cols] = group[step][chip, 0:TOK, :]
                gs_ref[rows, cols] = group[step][chip, TOK : 2 * TOK, :]
                if step == 0:
                    pair = group[0][chip, 2 * TOK : PACK, :].astype(F32)
                    dither = pair[0:1] * 8.0 + pair[1:2]
                    col_ref[:, cols] = jnp.broadcast_to(dither * (1.0 / 1024.0), (8, COLS))
    done(0, 1, 3)
    front = dot(weights_ref[0 : 2 * BLOCK, :], xs_ref[...], 1, 1)
    delta = dot(weights_ref[2 * BLOCK : 3 * BLOCK, :], gs_ref[...], 1, 1)
    gate = front[0:BLOCK]
    upper = front[BLOCK:]
    sig = jax.nn.sigmoid(gate)
    active = gate * sig
    dgate = (delta * upper * sig * (1.0 + gate * (1.0 - sig))).astype(BF16)
    dupper = (delta * active).astype(BF16)
    hidden = (active * upper).astype(BF16)
    for rep in range(REPS):
        rows = slice(rep * TOK, (rep + 1) * TOK)
        terms_ref[rep, 0:BLOCK, :] = dgate[:, rows]
        terms_ref[rep, BLOCK : 2 * BLOCK, :] = dupper[:, rows]
        terms_ref[rep, 2 * BLOCK : 3 * BLOCK, :] = hidden[:, rows]
    done(2)
    terms = jnp.concatenate([dgate, dupper], axis=0)
    for target, which in ((keep_ref, core), (give_ref, 1 - core)):
        side = []
        for chip in range(4):
            cols = pl.ds(pl.multiple_of((2 * chip + which) * COLS, COLS), COLS)
            side.append(weights_ref[0 : 2 * BLOCK, cols])
        back = dot(terms, jnp.concatenate(side, axis=1), 0, 0)
        for rep in range(REPS):
            for chip in range(4):
                target[rep * 4 + chip] = back[rep * TOK : (rep + 1) * TOK, chip * COLS : (chip + 1) * COLS]
    done(5, 6)
    peak = jnp.zeros((3 * BLOCK, COLS), F32)
    for rep in range(REPS):
        rows = slice(rep * TOK, (rep + 1) * TOK)
        for part in range(4):
            cols = slice(part * 256, (part + 1) * 256)
            grad_front = dot(terms_ref[rep, 0 : 2 * BLOCK, :], xs_ref[rows, cols], 1, 0)
            grad_down = dot(terms_ref[rep, 2 * BLOCK : 3 * BLOCK, :], gs_ref[rows, cols], 1, 0)
            grads = jnp.abs(jnp.concatenate([grad_front, grad_down], axis=0))
            peak = jnp.maximum(peak, jnp.maximum(grads[:, :COLS], grads[:, COLS:]))
    lane = lax.broadcasted_iota(jnp.int32, (1, COLS), 1)
    packed = jnp.zeros((1, COLS), F32)
    for group in range(9):
        top = jnp.max(peak[group * 16 : (group + 1) * 16], axis=0, keepdims=True)
        top = jnp.max(top, axis=1, keepdims=True)
        packed = jnp.where(lane == group, top, packed)
    peak_ref[...] = jnp.broadcast_to(packed.reshape(1, 1, COLS), peak_ref.shape)
    done(4)


def quant_kernel(need, done, pos_ref, xs_ref, gs_ref, terms_ref, peaks_ref, bits_ref, row_ref, col_ref, keep_ref, got_ref, out_ref, *back_refs):
    need(3, 4)
    spot = pos_ref[1]
    unit = pos_ref[2]
    depth = pos_ref[3]
    lane = lax.broadcasted_iota(jnp.int32, (1, COLS), 1)
    buck = lax.broadcasted_iota(jnp.int32, (1, 24), 1)
    tops = [jnp.max(peaks_ref[i * 16 : (i + 1) * 16], axis=0) for i in range(4)]
    scales = []
    for mat in range(3):
        per_bucket = []
        for bucket in range(3):
            held = jnp.zeros((1, COLS), F32)
            for sub in range(4 * bucket, 4 * bucket + 4):
                held = jnp.maximum(held, jnp.where(lane == mat * 3 + sub % 3, tops[sub // 3], 0.0))
            ranges = jnp.max(held, axis=1, keepdims=True)
            bits = jnp.where(buck == 3 * unit + bucket, bits_ref[mat : mat + 1, :].astype(F32), 0.0)
            bits = jnp.max(bits, axis=1, keepdims=True)
            levels = jnp.ones_like(bits)
            for count in range(3, 9):
                levels = jnp.where(bits == float(count), float(2 ** (count - 1) - 1), levels)
            per_bucket.append((ranges + RANGE_EPS) / levels)
        for sub in range(3):
            which = (3 * spot + sub) // 4
            chosen = jnp.where(which == 0, per_bucket[0], jnp.where(which == 1, per_bucket[1], per_bucket[2]))
            scales.append(jnp.broadcast_to(chosen, (16, COLS)))
    scale = jnp.concatenate(scales, axis=0)
    inverse = 1.0 / scale
    scale = scale * (1.0 / N_DP)
    need(0, 1, 2, 5, 6)
    row_part = row_ref[...]
    for part in range(4):
        cols = slice(part * 256, (part + 1) * 256)
        halves = [jnp.zeros((3 * BLOCK, COLS), F32) for _ in range(2)]
        for rep in range(REPS):
            rows = slice(rep * TOK, (rep + 1) * TOK)
            grad_front = dot(terms_ref[rep, 0 : 2 * BLOCK, :], xs_ref[rows, cols], 1, 0)
            grad_down = dot(terms_ref[rep, 2 * BLOCK : 3 * BLOCK, :], gs_ref[rows, cols], 1, 0)
            grads = jnp.concatenate([grad_front, grad_down], axis=0)
            offset = lax.rem(389 * (rep * 16 + depth), 1024).astype(F32) * (1.0 / 1024.0)
            for half in range(2):
                lanes = slice(half * COLS, (half + 1) * COLS)
                whole = slice(part * 256 + half * COLS, part * 256 + (half + 1) * COLS)
                ratio = grads[:, lanes] * inverse
                phase = row_part + (col_ref[0:1, whole] + offset)
                halves[half] = halves[half] + (ratio + turn(ratio + phase))
        for half in range(2):
            result = halves[half] * scale
            for mat in range(3):
                for low in range(2):
                    start = mat * BLOCK + low * SHARD
                    out_ref[2 * (2 * part + half) + low, mat, :, :] = result[start : start + SHARD]
    done(0)
    need(7, 8)
    plane = pos_ref[4]
    for step, back_ref in enumerate(back_refs):
        first = ((plane + step) % 4) * 4
        for chip in range(4):
            back_ref[chip] = keep_ref[first + chip] + got_ref[first + chip]
        done(1 + step)


def adam_kernel(pos_ref, shares_ref, state_ref, own_ref, up_ref, across_ref, down_ref, new_state_ref, coded_ref, *back_refs):
    chip = pos_ref[5]
    for step, back_ref in enumerate(back_refs):
        which = (chip + step) % 4
        back_ref[...] = (own_ref[which] + up_ref[which]) + (across_ref[which] + down_ref[which])
    mean_grad = shares_ref[0]
    for peer in range(1, 16):
        mean_grad = mean_grad + shares_ref[peer]
    master = state_ref[0]
    first = BETA_ONE * state_ref[1] + (1.0 - BETA_ONE) * mean_grad
    second = BETA_TWO * state_ref[2] + (1.0 - BETA_TWO) * mean_grad * mean_grad
    updated = master - LEARN_RATE * (first / (jnp.sqrt(second) + ADAM_EPS) + WEIGHT_DECAY * master)
    new_state_ref[0] = updated
    new_state_ref[1] = first
    new_state_ref[2] = second
    coded_ref[...] = eightbit_f32(updated)


def call(kernel, out_shape, smem=0, operands=(), scratch=(), limit=SMALL_LIMIT, first=None):
    single = not isinstance(out_shape, tuple)
    outs = (out_shape,) if single else out_shape
    n_in = len(operands) - smem
    n_out = len(outs)

    def body(*refs):
        small = refs[:smem]
        sources = refs[smem : smem + n_in]
        targets = refs[smem + n_in : smem + n_in + n_out]
        held = refs[smem + n_in + n_out :]
        taken, made, rest, sems = held[:n_in], held[n_in : n_in + n_out], held[n_in + n_out : -1], held[-1]
        loads = [pltpu.make_async_copy(sources[i], taken[i], sems.at[i]) for i in range(n_in)]
        stores = [pltpu.make_async_copy(made[i], targets[i], sems.at[n_in + i]) for i in range(n_out)]
        if first is None:
            for load in loads:
                load.start()
            for load in loads:
                load.wait()
            kernel(*small, *taken, *made, *rest)
            for store in stores:
                store.start()
        else:
            for i in first:
                loads[i].start()

            def need(*which):
                for i in which:
                    loads[i].wait()

            def done(*which):
                for i in which:
                    stores[i].start()

            kernel(need, done, *small, *taken, *made, *rest)
        for store in stores:
            store.wait()

    anywhere = pl.BlockSpec(memory_space=pl.ANY)
    specs = [pl.BlockSpec(memory_space=pltpu.SMEM)] * smem + [anywhere] * n_in
    buffers = [pltpu.VMEM(item.shape, item.dtype) for item in tuple(operands[smem:]) + outs]
    return pl.pallas_call(
        body,
        out_shape=out_shape,
        in_specs=specs,
        out_specs=anywhere if single else (anywhere,) * n_out,
        scratch_shapes=buffers + list(scratch) + [pltpu.SemaphoreType.DMA((n_in + n_out,))],
        compiler_params=pltpu.CompilerParams(vmem_limit_bytes=limit),
    )(*operands)


def struct(shape, dtype=F32):
    return jax.ShapeDtypeStruct(shape, dtype)


def to_all(value, axes, peers):
    return lax.all_to_all(jnp.broadcast_to(value[None], (peers,) + value.shape), axes, 0, 0)


def shift(value, axes, step):
    return lax.ppermute(value, axes, [(i, (i + step) % 4) for i in range(4)])


def swap_pairs():
    pairs = []
    for z in range(16):
        for t in range(8):
            pairs.append((z * 8 + t, (2 * t + z % 2) * 8 + z // 2))
    return pairs


def on_device(acts, grad_out, master, moment_one, moment_two, bit_widths, row_dither, col_dither):
    y = lax.axis_index("y")
    z = lax.axis_index(Z)
    core = lax.axis_index("c")
    tensor = lax.axis_index(TENSOR)
    spot = tensor % 4
    unit = 2 * y + tensor // 4
    pos = jnp.stack([core, spot, unit, z, y, tensor // 2]).astype(jnp.int32)
    pairs = swap_pairs()

    packed, state = call(
        pack_kernel,
        (struct((PACK, COLS), BF16), struct((3, 3, SHARD, COLS))),
        0,
        (acts, grad_out, col_dither[None], master, moment_one, moment_two),
        limit=LARGE_LIMIT,
    )
    state = lax.ppermute(state, Z + TENSOR, pairs)
    parts = [packed] + [shift(packed, ("xh", "xl"), step) for step in (1, 2, 3)]
    coded, joined = call(
        spread_kernel,
        (struct((48 * SHARD, COLS), BF16), struct((4, PACK, COLS), BF16)),
        0,
        (state, *parts),
        (pltpu.VMEM((6 * SHARD, COLS), F32),),
    )
    rows = lax.all_to_all(coded.reshape(16, 3 * SHARD, COLS), Z, 0, 0).reshape(48 * SHARD, COLS)
    own = [joined] + [shift(joined, "y", step) for step in (1, 2, 3)]
    other = [lax.ppermute(plane, "c", [(0, 1), (1, 0)]) for plane in own]

    row_part = lax.dynamic_slice(row_dither, (0, BLOCK * (8 * y + tensor)), (3, BLOCK))
    row_part = jnp.broadcast_to(row_part.astype(F32).reshape(3 * BLOCK, 1) * (1.0 / 1024.0), (3 * BLOCK, COLS))

    xs, gs, terms, col_part, peak, keep, give = call(
        front_kernel,
        (
            struct((REPS * TOK, 1024), BF16),
            struct((REPS * TOK, 1024), BF16),
            struct((REPS, 3 * BLOCK, TOK), BF16),
            struct((8, 1024)),
            struct((64, 1, COLS)),
            struct((16, TOK, COLS)),
            struct((16, TOK, COLS)),
        ),
        1,
        (pos, *own, *other, rows),
        (
            pltpu.VMEM((48 * SHARD, COLS), F32),
            pltpu.VMEM((3 * BLOCK, 1024), F32),
            pltpu.VMEM((3 * BLOCK, 1024), BF16),
        ),
        limit=LARGE_LIMIT,
        first=(8, 0, 4, 1, 5, 2, 6, 3, 7),
    )
    peaks = lax.all_to_all(peak, ("xl", "c") + Z, 0, 0)
    got = lax.ppermute(give, "c", [(0, 1), (1, 0)])

    shares, *back = call(
        quant_kernel,
        (struct((16, 3, SHARD, COLS)),) + (struct((4, TOK, COLS)),) * 4,
        1,
        (pos, xs, gs, terms, peaks, bit_widths, row_part, col_part, keep, got),
        limit=LARGE_LIMIT,
        first=(3, 4, 2, 0, 1, 5, 6, 7, 8),
    )
    back = [back[0]] + [shift(back[step], "y", step) for step in (1, 2, 3)]
    shares = lax.all_to_all(shares, Z, 0, 0)

    new_state, new_coded, *back = call(
        adam_kernel,
        (struct((3, 3, SHARD, COLS)), struct((3, SHARD, COLS))) + (struct((TOK, COLS)),) * 4,
        1,
        (pos, shares, state, *back),
    )
    back = [back[0]] + [shift(back[step], ("xh", "xl"), step) for step in (1, 2, 3)]
    ring = to_all(new_coded.astype(BF16), Z, 16)
    new_state = lax.ppermute(new_state, Z + TENSOR, pairs)
    grad_in = ((back[0] + back[1]) + (back[2] + back[3])).astype(BF16)
    ring = jnp.broadcast_to(ring.reshape(1, 8, 2, 3, SHARD, COLS), (4, 8, 2, 3, SHARD, COLS))
    ring = lax.all_to_all(ring.reshape(32, 2, 3, SHARD, COLS), ("y",) + TENSOR, 0, 0)
    new_weights = ring.transpose(2, 0, 1, 3, 4).reshape(3, 64 * SHARD, COLS)
    return (grad_in, new_state[0], new_state[1], new_state[2], new_weights)


def solution(mesh):
    grid = Mesh(mesh.devices.reshape(SIZES), DP + TENSOR)
    return jax.shard_map(
        on_device,
        mesh=grid,
        in_specs=(
            P(DP, TENSOR),
            P(DP, TENSOR),
            P(None, DP, TENSOR),
            P(None, DP, TENSOR),
            P(None, DP, TENSOR),
            P(),
            P(),
            P(TENSOR),
        ),
        out_specs=(
            P(DP, TENSOR),
            P(None, DP, TENSOR),
            P(None, DP, TENSOR),
            P(None, DP, TENSOR),
            P(None, None, TENSOR),
        ),
        check_vma=False,
    )
```

```python
import jax
import jax.numpy as jnp
from jax import lax
from jax.experimental import pallas as pl
from jax.experimental.pallas import tpu as pltpu
from jax.sharding import Mesh, PartitionSpec as P

F32 = jnp.float32
BF16 = jnp.bfloat16

TOK = 128
BROWS = 64
COLS = 128
SHARD = 24
BLOCK = 48
PACK = 2 * TOK + 16
REPS = 4

BETA_ONE = 0.9
BETA_TWO = 0.95
LEARN_RATE = 0.004
WEIGHT_DECAY = 0.1
ADAM_EPS = 1e-08
RANGE_EPS = 1e-06
N_DP = 64

SINE = (
    0.9999995827674866,
    -6.579691410064697,
    12.986435890197754,
    -12.188101768493652,
    6.558042526245117,
    -1.95303213596344,
)

Z = ("zh", "zl")
DP = ("y",) + Z
TENSOR = ("xh", "xl", "c")
SIZES = (4, 4, 4, 2, 2, 2)

SMALL_LIMIT = 20 * 1024 * 1024
LARGE_LIMIT = 60 * 1024 * 1024


def turn(value):
    frac = value - jnp.floor(value + 0.5)
    square = frac * frac
    total = jnp.full_like(square, SINE[-1])
    for coef in SINE[-2::-1]:
        total = total * square + coef
    return total * frac


def soft_round(value):
    return value - turn(value)


def eightbit_f32(weights):
    scale = (jnp.max(jnp.abs(weights), axis=-1, keepdims=True) + RANGE_EPS) / 127.0
    return soft_round(weights / scale) * scale


def dot(left, right, left_dim, right_dim):
    return lax.dot_general(
        left, right, (((left_dim,), (right_dim,)), ((), ())), preferred_element_type=F32
    )


def pack_kernel(acts_ref, grad_ref, dither_ref, master_ref, one_ref, two_ref, packed_ref, coded_ref, state_ref, wide_ref):
    high = (dither_ref[...] >> 3).astype(F32)
    low = (dither_ref[...] & 7).astype(F32)
    row = lax.broadcasted_iota(jnp.int32, (16, COLS), 0)
    extra = jnp.where(row == 0, high, jnp.where(row == 1, low, 0.0)).astype(BF16)
    packed_ref[0:TOK, :] = acts_ref[...]
    packed_ref[TOK : 2 * TOK, :] = grad_ref[...]
    packed_ref[2 * TOK : PACK, :] = extra
    coded = eightbit_f32(master_ref[...])
    for mat in range(6):
        wide_ref[mat * SHARD : (mat + 1) * SHARD, :] = coded[mat % 3]
    narrow = wide_ref[...].astype(BF16)
    for pair in range(8):
        coded_ref[pair * 6 * SHARD : (pair + 1) * 6 * SHARD, :] = narrow
    state_ref[0] = master_ref[...]
    state_ref[1] = one_ref[...]
    state_ref[2] = two_ref[...]


def front_kernel(need, done, pos_ref, *refs):
    planes, refs = (refs[:4], refs[4:8]), refs[8:]
    rows_ref, xs_ref, gs_ref, terms_ref, col_ref, peak_ref, keep_ref, give_ref = refs[:8]
    wide_ref, full_ref, weights_ref = refs[8:]
    core = pos_ref[0]
    need(8)
    wide_ref[...] = rows_ref[...].astype(F32)
    for depth in range(16):
        cols = slice((depth // 2) * COLS, (depth // 2 + 1) * COLS)
        for mat in range(3):
            source = (depth * 3 + mat) * SHARD
            target = mat * BLOCK + (depth % 2) * SHARD
            full_ref[target : target + SHARD, cols] = wide_ref[source : source + SHARD, :]
    weights_ref[...] = full_ref[...].astype(BF16)
    for step in range(REPS):
        rep = (pos_ref[4] + 4 - step) % 4
        rows = pl.ds(pl.multiple_of(rep * TOK, TOK), TOK)
        for side, which in ((0, core), (1, 1 - core)):
            group = planes[side]
            need(4 * side + step)
            for chip in range(4):
                column = (pos_ref[5] + 4 - chip) % 4
                cols = pl.ds(pl.multiple_of((2 * column + which) * COLS, COLS), COLS)
                xs_ref[rows, cols] = group[step][chip, 0:TOK, :]
                gs_ref[rows, cols] = group[step][chip, TOK : 2 * TOK, :]
                if step == 0:
                    pair = group[0][chip, 2 * TOK : PACK, :].astype(F32)
                    dither = pair[0:1] * 8.0 + pair[1:2]
                    col_ref[:, cols] = jnp.broadcast_to(dither * (1.0 / 1024.0), (8, COLS))
    done(0, 1, 3)
    front = dot(weights_ref[0 : 2 * BLOCK, :], xs_ref[...], 1, 1)
    delta = dot(weights_ref[2 * BLOCK : 3 * BLOCK, :], gs_ref[...], 1, 1)
    gate = front[0:BLOCK]
    upper = front[BLOCK:]
    sig = jax.nn.sigmoid(gate)
    active = gate * sig
    dgate = (delta * upper * sig * (1.0 + gate * (1.0 - sig))).astype(BF16)
    dupper = (delta * active).astype(BF16)
    hidden = (active * upper).astype(BF16)
    for rep in range(REPS):
        rows = slice(rep * TOK, (rep + 1) * TOK)
        terms_ref[rep, 0:BLOCK, :] = dgate[:, rows]
        terms_ref[rep, BLOCK : 2 * BLOCK, :] = dupper[:, rows]
        terms_ref[rep, 2 * BLOCK : 3 * BLOCK, :] = hidden[:, rows]
    done(2)
    terms = jnp.concatenate([dgate, dupper], axis=0)
    for target, which in ((keep_ref, core), (give_ref, 1 - core)):
        side = []
        for chip in range(4):
            cols = pl.ds(pl.multiple_of((2 * chip + which) * COLS, COLS), COLS)
            side.append(weights_ref[0 : 2 * BLOCK, cols])
        back = dot(terms, jnp.concatenate(side, axis=1), 0, 0)
        for rep in range(REPS):
            for chip in range(4):
                target[rep * 4 + chip] = back[rep * TOK : (rep + 1) * TOK, chip * COLS : (chip + 1) * COLS]
    done(5, 6)
    peak = jnp.zeros((3 * BLOCK, COLS), F32)
    for rep in range(REPS):
        rows = slice(rep * TOK, (rep + 1) * TOK)
        for part in range(4):
            cols = slice(part * 256, (part + 1) * 256)
            grad_front = dot(terms_ref[rep, 0 : 2 * BLOCK, :], xs_ref[rows, cols], 1, 0)
            grad_down = dot(terms_ref[rep, 2 * BLOCK : 3 * BLOCK, :], gs_ref[rows, cols], 1, 0)
            grads = jnp.abs(jnp.concatenate([grad_front, grad_down], axis=0))
            peak = jnp.maximum(peak, jnp.maximum(grads[:, :COLS], grads[:, COLS:]))
    lane = lax.broadcasted_iota(jnp.int32, (1, COLS), 1)
    packed = jnp.zeros((1, COLS), F32)
    for group in range(9):
        top = jnp.max(peak[group * 16 : (group + 1) * 16], axis=0, keepdims=True)
        top = jnp.max(top, axis=1, keepdims=True)
        packed = jnp.where(lane == group, top, packed)
    peak_ref[...] = jnp.broadcast_to(packed.reshape(1, 1, COLS), peak_ref.shape)
    done(4)


def quant_kernel(need, done, pos_ref, xs_ref, gs_ref, terms_ref, peaks_ref, bits_ref, row_ref, col_ref, keep_ref, got_ref, out_ref, *back_refs):
    need(3, 4)
    spot = pos_ref[1]
    unit = pos_ref[2]
    depth = pos_ref[3]
    lane = lax.broadcasted_iota(jnp.int32, (1, COLS), 1)
    buck = lax.broadcasted_iota(jnp.int32, (1, 24), 1)
    tops = [jnp.max(peaks_ref[i * 16 : (i + 1) * 16], axis=0) for i in range(4)]
    scales = []
    for mat in range(3):
        per_bucket = []
        for bucket in range(3):
            held = jnp.zeros((1, COLS), F32)
            for sub in range(4 * bucket, 4 * bucket + 4):
                held = jnp.maximum(held, jnp.where(lane == mat * 3 + sub % 3, tops[sub // 3], 0.0))
            ranges = jnp.max(held, axis=1, keepdims=True)
            bits = jnp.where(buck == 3 * unit + bucket, bits_ref[mat : mat + 1, :].astype(F32), 0.0)
            bits = jnp.max(bits, axis=1, keepdims=True)
            levels = jnp.ones_like(bits)
            for count in range(3, 9):
                levels = jnp.where(bits == float(count), float(2 ** (count - 1) - 1), levels)
            per_bucket.append((ranges + RANGE_EPS) / levels)
        for sub in range(3):
            which = (3 * spot + sub) // 4
            chosen = jnp.where(which == 0, per_bucket[0], jnp.where(which == 1, per_bucket[1], per_bucket[2]))
            scales.append(jnp.broadcast_to(chosen, (16, COLS)))
    scale = jnp.concatenate(scales, axis=0)
    inverse = 1.0 / scale
    scale = scale * (1.0 / N_DP)
    need(0, 1, 2, 5, 6)
    row_part = row_ref[...]
    for part in range(4):
        cols = slice(part * 256, (part + 1) * 256)
        halves = [jnp.zeros((3 * BLOCK, COLS), F32) for _ in range(2)]
        for rep in range(REPS):
            rows = slice(rep * TOK, (rep + 1) * TOK)
            grad_front = dot(terms_ref[rep, 0 : 2 * BLOCK, :], xs_ref[rows, cols], 1, 0)
            grad_down = dot(terms_ref[rep, 2 * BLOCK : 3 * BLOCK, :], gs_ref[rows, cols], 1, 0)
            grads = jnp.concatenate([grad_front, grad_down], axis=0)
            offset = lax.rem(389 * (rep * 16 + depth), 1024).astype(F32) * (1.0 / 1024.0)
            for half in range(2):
                lanes = slice(half * COLS, (half + 1) * COLS)
                whole = slice(part * 256 + half * COLS, part * 256 + (half + 1) * COLS)
                ratio = grads[:, lanes] * inverse
                phase = row_part + (col_ref[0:1, whole] + offset)
                halves[half] = halves[half] + (ratio + turn(ratio + phase))
        for half in range(2):
            result = halves[half] * scale
            for mat in range(3):
                for low in range(2):
                    start = mat * BLOCK + low * SHARD
                    out_ref[2 * (2 * part + half) + low, mat, :, :] = result[start : start + SHARD]
    done(0)
    need(7, 8)
    plane = pos_ref[4]
    for step, back_ref in enumerate(back_refs):
        first = ((plane + step) % 4) * 4
        for chip in range(4):
            back_ref[chip] = keep_ref[first + chip] + got_ref[first + chip]
        done(1 + step)


def adam_kernel(pos_ref, shares_ref, state_ref, own_ref, up_ref, across_ref, down_ref, new_state_ref, coded_ref, *back_refs):
    chip = pos_ref[5]
    for step, back_ref in enumerate(back_refs):
        which = (chip + step) % 4
        back_ref[...] = (own_ref[which] + up_ref[which]) + (across_ref[which] + down_ref[which])
    mean_grad = shares_ref[0]
    for peer in range(1, 16):
        mean_grad = mean_grad + shares_ref[peer]
    master = state_ref[0]
    first = BETA_ONE * state_ref[1] + (1.0 - BETA_ONE) * mean_grad
    second = BETA_TWO * state_ref[2] + (1.0 - BETA_TWO) * mean_grad * mean_grad
    updated = master - LEARN_RATE * (first / (jnp.sqrt(second) + ADAM_EPS) + WEIGHT_DECAY * master)
    new_state_ref[0] = updated
    new_state_ref[1] = first
    new_state_ref[2] = second
    coded_ref[...] = eightbit_f32(updated)


def finish_kernel(ring_ref, state_ref, own_ref, right_ref, across_ref, left_ref, *outs):
    spread_ref, grad_ref, state_outs = outs[0], outs[1], outs[2:]
    for plane in range(4):
        spread_ref[plane] = ring_ref[...]
    grad_ref[...] = ((own_ref[...] + right_ref[...]) + (across_ref[...] + left_ref[...])).astype(BF16)
    for which, out_ref in enumerate(state_outs):
        out_ref[...] = state_ref[which]


def call(kernel, out_shape, smem=0, operands=(), scratch=(), limit=SMALL_LIMIT, first=None):
    single = not isinstance(out_shape, tuple)
    outs = (out_shape,) if single else out_shape
    n_in = len(operands) - smem
    n_out = len(outs)

    def body(*refs):
        small = refs[:smem]
        sources = refs[smem : smem + n_in]
        targets = refs[smem + n_in : smem + n_in + n_out]
        held = refs[smem + n_in + n_out :]
        taken, made, rest, sems = held[:n_in], held[n_in : n_in + n_out], held[n_in + n_out : -1], held[-1]
        loads = [pltpu.make_async_copy(sources[i], taken[i], sems.at[i]) for i in range(n_in)]
        stores = [pltpu.make_async_copy(made[i], targets[i], sems.at[n_in + i]) for i in range(n_out)]
        if first is None:
            for load in loads:
                load.start()
            for load in loads:
                load.wait()
            kernel(*small, *taken, *made, *rest)
            for store in stores:
                store.start()
        else:
            for i in first:
                loads[i].start()

            def need(*which):
                for i in which:
                    loads[i].wait()

            def done(*which):
                for i in which:
                    stores[i].start()

            kernel(need, done, *small, *taken, *made, *rest)
        for store in stores:
            store.wait()

    anywhere = pl.BlockSpec(memory_space=pl.ANY)
    specs = [pl.BlockSpec(memory_space=pltpu.SMEM)] * smem + [anywhere] * n_in
    buffers = [pltpu.VMEM(item.shape, item.dtype) for item in tuple(operands[smem:]) + outs]
    return pl.pallas_call(
        body,
        out_shape=out_shape,
        in_specs=specs,
        out_specs=anywhere if single else (anywhere,) * n_out,
        scratch_shapes=buffers + list(scratch) + [pltpu.SemaphoreType.DMA((n_in + n_out,))],
        compiler_params=pltpu.CompilerParams(vmem_limit_bytes=limit),
    )(*operands)


def struct(shape, dtype=F32):
    return jax.ShapeDtypeStruct(shape, dtype)


def to_all(value, axes, peers):
    return lax.all_to_all(jnp.broadcast_to(value[None], (peers,) + value.shape), axes, 0, 0)


def shift(value, axes, step):
    return lax.ppermute(value, axes, [(i, (i + step) % 4) for i in range(4)])


def swap_pairs():
    pairs = []
    for z in range(16):
        for t in range(8):
            pairs.append((z * 8 + t, (2 * t + z % 2) * 8 + z // 2))
    return pairs


def on_device(acts, grad_out, master, moment_one, moment_two, bit_widths, row_dither, col_dither):
    y = lax.axis_index("y")
    z = lax.axis_index(Z)
    core = lax.axis_index("c")
    tensor = lax.axis_index(TENSOR)
    spot = tensor % 4
    unit = 2 * y + tensor // 4
    pos = jnp.stack([core, spot, unit, z, y, tensor // 2]).astype(jnp.int32)
    pairs = swap_pairs()

    packed, coded, state = call(
        pack_kernel,
        (struct((PACK, COLS), BF16), struct((48 * SHARD, COLS), BF16), struct((3, 3, SHARD, COLS))),
        0,
        (acts, grad_out, col_dither[None], master, moment_one, moment_two),
        (pltpu.VMEM((6 * SHARD, COLS), F32),),
        limit=LARGE_LIMIT,
    )
    rows = lax.all_to_all(coded.reshape(16, 3 * SHARD, COLS), Z, 0, 0)
    rows = lax.all_to_all(rows.reshape(8, 6 * SHARD, COLS), TENSOR, 0, 0).reshape(48 * SHARD, COLS)
    joined = jnp.stack([packed] + [shift(packed, ("xh", "xl"), step) for step in (1, 2, 3)])
    own = [joined] + [shift(joined, "y", step) for step in (1, 2, 3)]
    other = [lax.ppermute(plane, "c", [(0, 1), (1, 0)]) for plane in own]

    row_part = lax.dynamic_slice(row_dither, (0, BLOCK * (8 * y + tensor)), (3, BLOCK))
    row_part = jnp.broadcast_to(row_part.astype(F32).reshape(3 * BLOCK, 1) * (1.0 / 1024.0), (3 * BLOCK, COLS))

    xs, gs, terms, col_part, peak, keep, give = call(
        front_kernel,
        (
            struct((REPS * TOK, 1024), BF16),
            struct((REPS * TOK, 1024), BF16),
            struct((REPS, 3 * BLOCK, TOK), BF16),
            struct((8, 1024)),
            struct((64, 1, COLS)),
            struct((16, TOK, COLS)),
            struct((16, TOK, COLS)),
        ),
        1,
        (pos, *own, *other, rows),
        (
            pltpu.VMEM((48 * SHARD, COLS), F32),
            pltpu.VMEM((3 * BLOCK, 1024), F32),
            pltpu.VMEM((3 * BLOCK, 1024), BF16),
        ),
        limit=LARGE_LIMIT,
        first=(8, 0, 4, 1, 5, 2, 6, 3, 7),
    )
    peaks = lax.all_to_all(peak, ("xl", "c") + Z, 0, 0)
    got = lax.ppermute(give, "c", [(0, 1), (1, 0)])

    shares, *back = call(
        quant_kernel,
        (struct((16, 3, SHARD, COLS)),) + (struct((4, TOK, COLS)),) * 4,
        1,
        (pos, xs, gs, terms, peaks, bit_widths, row_part, col_part, keep, got),
        limit=LARGE_LIMIT,
        first=(3, 4, 2, 0, 1, 5, 6, 7, 8),
    )
    state = lax.ppermute(state, Z + TENSOR, pairs)
    back = [back[0]] + [shift(back[step], "y", step) for step in (1, 2, 3)]
    shares = lax.all_to_all(shares, Z, 0, 0)

    new_state, new_coded, *back = call(
        adam_kernel,
        (struct((3, 3, SHARD, COLS)), struct((3, SHARD, COLS))) + (struct((TOK, COLS)),) * 4,
        1,
        (pos, shares, state, *back),
    )
    back = [back[0]] + [shift(back[step], ("xh", "xl"), step) for step in (1, 2, 3)]
    new_state = lax.ppermute(new_state, Z + TENSOR, pairs)
    ring = to_all(new_coded.astype(BF16), Z, 16).reshape(48 * SHARD, COLS)
    ring, grad_in, updated, first, second = call(
        finish_kernel,
        (struct((4, 48 * SHARD, COLS), BF16), struct((TOK, COLS), BF16)) + (struct((3, SHARD, COLS)),) * 3,
        0,
        (ring, new_state, *back),
    )
    ring = lax.all_to_all(ring.reshape(32, 6 * SHARD, COLS), ("y",) + TENSOR, 0, 0)
    new_weights = ring.reshape(32, 2, 3, SHARD, COLS).transpose(2, 0, 1, 3, 4).reshape(3, 64 * SHARD, COLS)
    return (grad_in, updated, first, second, new_weights)


def solution(mesh):
    grid = Mesh(mesh.devices.reshape(SIZES), DP + TENSOR)
    return jax.shard_map(
        on_device,
        mesh=grid,
        in_specs=(
            P(DP, TENSOR),
            P(DP, TENSOR),
            P(None, DP, TENSOR),
            P(None, DP, TENSOR),
            P(None, DP, TENSOR),
            P(),
            P(),
            P(TENSOR),
        ),
        out_specs=(
            P(DP, TENSOR),
            P(None, DP, TENSOR),
            P(None, DP, TENSOR),
            P(None, DP, TENSOR),
            P(None, None, TENSOR),
        ),
        check_vma=False,
    )
```

```python
import jax
import jax.numpy as jnp
from jax import lax
from jax.experimental import pallas as pl
from jax.experimental.pallas import tpu as pltpu
from jax.sharding import Mesh, PartitionSpec as P

F32 = jnp.float32
BF16 = jnp.bfloat16

TOK = 128
BROWS = 64
COLS = 128
SHARD = 24
BLOCK = 48
PACK = 2 * TOK + 16
REPS = 4

BETA_ONE = 0.9
BETA_TWO = 0.95
LEARN_RATE = 0.004
WEIGHT_DECAY = 0.1
ADAM_EPS = 1e-08
RANGE_EPS = 1e-06
N_DP = 64

SINE = (
    0.9999995827674866,
    -6.579691410064697,
    12.986435890197754,
    -12.188101768493652,
    6.558042526245117,
    -1.95303213596344,
)

Z = ("zh", "zl")
DP = ("y",) + Z
TENSOR = ("xh", "xl", "c")
SIZES = (4, 4, 4, 2, 2, 2)

SMALL_LIMIT = 20 * 1024 * 1024
LARGE_LIMIT = 60 * 1024 * 1024


def turn(value):
    frac = value - jnp.floor(value + 0.5)
    square = frac * frac
    total = jnp.full_like(square, SINE[-1])
    for coef in SINE[-2::-1]:
        total = total * square + coef
    return total * frac


def soft_round(value):
    return value - turn(value)


def eightbit_f32(weights):
    scale = (jnp.max(jnp.abs(weights), axis=-1, keepdims=True) + RANGE_EPS) / 127.0
    return soft_round(weights / scale) * scale


def dot(left, right, left_dim, right_dim):
    return lax.dot_general(
        left, right, (((left_dim,), (right_dim,)), ((), ())), preferred_element_type=F32
    )


def spread_coded(coded, coded_ref, wide_ref):
    for mat in range(6):
        wide_ref[mat * SHARD : (mat + 1) * SHARD, :] = coded[mat % 3]
    narrow = wide_ref[...].astype(BF16)
    for pair in range(8):
        coded_ref[pair * 6 * SHARD : (pair + 1) * 6 * SHARD, :] = narrow


def pack_kernel(acts_ref, grad_ref, dither_ref, master_ref, packed_ref, coded_ref, wide_ref):
    high = (dither_ref[...] >> 3).astype(F32)
    low = (dither_ref[...] & 7).astype(F32)
    row = lax.broadcasted_iota(jnp.int32, (16, COLS), 0)
    extra = jnp.where(row == 0, high, jnp.where(row == 1, low, 0.0)).astype(BF16)
    packed_ref[0:TOK, :] = acts_ref[...]
    packed_ref[TOK : 2 * TOK, :] = grad_ref[...]
    packed_ref[2 * TOK : PACK, :] = extra
    spread_coded(eightbit_f32(master_ref[...]), coded_ref, wide_ref)


def join_kernel(_, *refs):
    parts, joined_ref, sems = refs[:-2], refs[-2], refs[-1]
    size = joined_ref.shape[0] // len(parts)
    copies = [
        pltpu.make_async_copy(part, joined_ref.at[pl.ds(i * size, size)], sems.at[i])
        for i, part in enumerate(parts)
    ]
    for copy in copies:
        copy.start()
    for copy in copies:
        copy.wait()


def front_kernel(need, done, pos_ref, *refs):
    near, far, refs = refs[0:3:2], refs[1:4:2], refs[4:]
    rows_ref, xs_ref, gs_ref, terms_ref, col_ref, peak_ref, keep_ref, give_ref = refs[:8]
    wide_ref, full_ref, weights_ref = refs[8:]
    core = pos_ref[0]
    need(4)
    wide_ref[...] = rows_ref[...].astype(F32)
    for depth in range(16):
        cols = slice((depth // 2) * COLS, (depth // 2 + 1) * COLS)
        for mat in range(3):
            source = (depth * 3 + mat) * SHARD
            target = mat * BLOCK + (depth % 2) * SHARD
            full_ref[target : target + SHARD, cols] = wide_ref[source : source + SHARD, :]
    weights_ref[...] = full_ref[...].astype(BF16)
    for step in range(REPS):
        rep = (pos_ref[4] + 4 - step) % 4
        rows = pl.ds(pl.multiple_of(rep * TOK, TOK), TOK)
        for side, which in ((0, core), (1, 1 - core)):
            if step < 2:
                need(2 * side + step)
            for chip in range(4):
                source = far[side].at[(step - 1) * 4 + chip] if step else near[side].at[chip]
                column = (pos_ref[5] + 4 - chip) % 4
                cols = pl.ds(pl.multiple_of((2 * column + which) * COLS, COLS), COLS)
                xs_ref[rows, cols] = source[0:TOK, :]
                gs_ref[rows, cols] = source[TOK : 2 * TOK, :]
                if step == 0:
                    pair = source[2 * TOK : PACK, :].astype(F32)
                    dither = pair[0:1] * 8.0 + pair[1:2]
                    col_ref[:, cols] = jnp.broadcast_to(dither * (1.0 / 1024.0), (8, COLS))
    done(0, 1, 3)
    front = dot(weights_ref[0 : 2 * BLOCK, :], xs_ref[...], 1, 1)
    delta = dot(weights_ref[2 * BLOCK : 3 * BLOCK, :], gs_ref[...], 1, 1)
    gate = front[0:BLOCK]
    upper = front[BLOCK:]
    sig = jax.nn.sigmoid(gate)
    active = gate * sig
    dgate = (delta * upper * sig * (1.0 + gate * (1.0 - sig))).astype(BF16)
    dupper = (delta * active).astype(BF16)
    hidden = (active * upper).astype(BF16)
    for rep in range(REPS):
        rows = slice(rep * TOK, (rep + 1) * TOK)
        terms_ref[rep, 0:BLOCK, :] = dgate[:, rows]
        terms_ref[rep, BLOCK : 2 * BLOCK, :] = dupper[:, rows]
        terms_ref[rep, 2 * BLOCK : 3 * BLOCK, :] = hidden[:, rows]
    done(2)
    terms = jnp.concatenate([dgate, dupper], axis=0)
    for target, which in ((keep_ref, core), (give_ref, 1 - core)):
        side = []
        for chip in range(4):
            cols = pl.ds(pl.multiple_of((2 * chip + which) * COLS, COLS), COLS)
            side.append(weights_ref[0 : 2 * BLOCK, cols])
        back = dot(terms, jnp.concatenate(side, axis=1), 0, 0)
        for rep in range(REPS):
            for chip in range(4):
                target[rep * 4 + chip] = back[rep * TOK : (rep + 1) * TOK, chip * COLS : (chip + 1) * COLS]
    done(5, 6)
    peak = jnp.zeros((3 * BLOCK, COLS), F32)
    for rep in range(REPS):
        rows = slice(rep * TOK, (rep + 1) * TOK)
        for part in range(4):
            cols = slice(part * 256, (part + 1) * 256)
            grad_front = dot(terms_ref[rep, 0 : 2 * BLOCK, :], xs_ref[rows, cols], 1, 0)
            grad_down = dot(terms_ref[rep, 2 * BLOCK : 3 * BLOCK, :], gs_ref[rows, cols], 1, 0)
            grads = jnp.abs(jnp.concatenate([grad_front, grad_down], axis=0))
            peak = jnp.maximum(peak, jnp.maximum(grads[:, :COLS], grads[:, COLS:]))
    lane = lax.broadcasted_iota(jnp.int32, (1, COLS), 1)
    packed = jnp.zeros((1, COLS), F32)
    for group in range(9):
        top = jnp.max(peak[group * 16 : (group + 1) * 16], axis=0, keepdims=True)
        top = jnp.max(top, axis=1, keepdims=True)
        packed = jnp.where(lane == group, top, packed)
    peak_ref[...] = jnp.broadcast_to(packed.reshape(1, 1, COLS), peak_ref.shape)
    done(4)


def quant_kernel(need, done, pos_ref, xs_ref, gs_ref, terms_ref, peaks_ref, bits_ref, row_ref, col_ref, keep_ref, got_ref, out_ref, *back_refs):
    need(3, 4)
    spot = pos_ref[1]
    unit = pos_ref[2]
    depth = pos_ref[3]
    lane = lax.broadcasted_iota(jnp.int32, (1, COLS), 1)
    buck = lax.broadcasted_iota(jnp.int32, (1, 24), 1)
    tops = [jnp.max(peaks_ref[i * 16 : (i + 1) * 16], axis=0) for i in range(4)]
    scales = []
    for mat in range(3):
        per_bucket = []
        for bucket in range(3):
            held = jnp.zeros((1, COLS), F32)
            for sub in range(4 * bucket, 4 * bucket + 4):
                held = jnp.maximum(held, jnp.where(lane == mat * 3 + sub % 3, tops[sub // 3], 0.0))
            ranges = jnp.max(held, axis=1, keepdims=True)
            bits = jnp.where(buck == 3 * unit + bucket, bits_ref[mat : mat + 1, :].astype(F32), 0.0)
            bits = jnp.max(bits, axis=1, keepdims=True)
            levels = jnp.ones_like(bits)
            for count in range(3, 9):
                levels = jnp.where(bits == float(count), float(2 ** (count - 1) - 1), levels)
            per_bucket.append((ranges + RANGE_EPS) / levels)
        for sub in range(3):
            which = (3 * spot + sub) // 4
            chosen = jnp.where(which == 0, per_bucket[0], jnp.where(which == 1, per_bucket[1], per_bucket[2]))
            scales.append(jnp.broadcast_to(chosen, (16, COLS)))
    scale = jnp.concatenate(scales, axis=0)
    inverse = 1.0 / scale
    scale = scale * (1.0 / N_DP)
    need(0, 1, 2, 5, 6)
    row_part = row_ref[...]
    for part in range(4):
        cols = slice(part * 256, (part + 1) * 256)
        halves = [jnp.zeros((3 * BLOCK, COLS), F32) for _ in range(2)]
        for rep in range(REPS):
            rows = slice(rep * TOK, (rep + 1) * TOK)
            grad_front = dot(terms_ref[rep, 0 : 2 * BLOCK, :], xs_ref[rows, cols], 1, 0)
            grad_down = dot(terms_ref[rep, 2 * BLOCK : 3 * BLOCK, :], gs_ref[rows, cols], 1, 0)
            grads = jnp.concatenate([grad_front, grad_down], axis=0)
            offset = lax.rem(389 * (rep * 16 + depth), 1024).astype(F32) * (1.0 / 1024.0)
            for half in range(2):
                lanes = slice(half * COLS, (half + 1) * COLS)
                whole = slice(part * 256 + half * COLS, part * 256 + (half + 1) * COLS)
                ratio = grads[:, lanes] * inverse
                phase = row_part + (col_ref[0:1, whole] + offset)
                halves[half] = halves[half] + (ratio + turn(ratio + phase))
        for half in range(2):
            result = halves[half] * scale
            for mat in range(3):
                for low in range(2):
                    start = mat * BLOCK + low * SHARD
                    out_ref[2 * (2 * part + half) + low, mat, :, :] = result[start : start + SHARD]
    done(0)
    need(7, 8)
    plane = pos_ref[4]
    for step, back_ref in enumerate(back_refs):
        first = ((plane + step) % 4) * 4
        for chip in range(4):
            back_ref[chip] = keep_ref[first + chip] + got_ref[first + chip]
        done(1 + step)


def sum_kernel(pos_ref, shares_ref, own_ref, up_ref, across_ref, down_ref, mean_ref, *back_refs):
    mean_grad = shares_ref[0]
    for peer in range(1, 16):
        mean_grad = mean_grad + shares_ref[peer]
    mean_ref[...] = mean_grad
    for step, back_ref in enumerate(back_refs):
        which = (pos_ref[5] + step) % 4
        back_ref[...] = (own_ref[which] + up_ref[which]) + (across_ref[which] + down_ref[which])


def adam_kernel(mean_ref, master_ref, one_ref, two_ref, new_master_ref, new_one_ref, new_two_ref, coded_ref, wide_ref):
    mean_grad = mean_ref[...]
    master = master_ref[...]
    first = BETA_ONE * one_ref[...] + (1.0 - BETA_ONE) * mean_grad
    second = BETA_TWO * two_ref[...] + (1.0 - BETA_TWO) * mean_grad * mean_grad
    updated = master - LEARN_RATE * (first / (jnp.sqrt(second) + ADAM_EPS) + WEIGHT_DECAY * master)
    new_master_ref[...] = updated
    new_one_ref[...] = first
    new_two_ref[...] = second
    spread_coded(eightbit_f32(updated), coded_ref, wide_ref)


def finish_kernel(ring_ref, own_ref, right_ref, across_ref, left_ref, spread_ref, grad_ref):
    for plane in range(4):
        spread_ref[plane] = ring_ref[...]
    grad_ref[...] = ((own_ref[...] + right_ref[...]) + (across_ref[...] + left_ref[...])).astype(BF16)


def call(kernel, out_shape, smem=0, operands=(), scratch=(), limit=SMALL_LIMIT, first=None):
    single = not isinstance(out_shape, tuple)
    outs = (out_shape,) if single else out_shape
    n_in = len(operands) - smem
    n_out = len(outs)

    def body(*refs):
        small = refs[:smem]
        sources = refs[smem : smem + n_in]
        targets = refs[smem + n_in : smem + n_in + n_out]
        held = refs[smem + n_in + n_out :]
        taken, made, rest, sems = held[:n_in], held[n_in : n_in + n_out], held[n_in + n_out : -1], held[-1]
        loads = [pltpu.make_async_copy(sources[i], taken[i], sems.at[i]) for i in range(n_in)]
        stores = [pltpu.make_async_copy(made[i], targets[i], sems.at[n_in + i]) for i in range(n_out)]
        if first is None:
            for load in loads:
                load.start()
            for load in loads:
                load.wait()
            kernel(*small, *taken, *made, *rest)
            for store in stores:
                store.start()
        else:
            for i in first:
                loads[i].start()

            def need(*which):
                for i in which:
                    loads[i].wait()

            def done(*which):
                for i in which:
                    stores[i].start()

            kernel(need, done, *small, *taken, *made, *rest)
        for store in stores:
            store.wait()

    anywhere = pl.BlockSpec(memory_space=pl.ANY)
    specs = [pl.BlockSpec(memory_space=pltpu.SMEM)] * smem + [anywhere] * n_in
    buffers = [pltpu.VMEM(item.shape, item.dtype) for item in tuple(operands[smem:]) + outs]
    return pl.pallas_call(
        body,
        out_shape=out_shape,
        in_specs=specs,
        out_specs=anywhere if single else (anywhere,) * n_out,
        scratch_shapes=buffers + list(scratch) + [pltpu.SemaphoreType.DMA((n_in + n_out,))],
        compiler_params=pltpu.CompilerParams(vmem_limit_bytes=limit),
    )(*operands)


def join(after, parts):
    shape = (len(parts) * parts[0].shape[0],) + parts[0].shape[1:]
    anywhere = pl.BlockSpec(memory_space=pl.ANY)
    return pl.pallas_call(
        join_kernel,
        out_shape=struct(shape, parts[0].dtype),
        in_specs=[anywhere] * (1 + len(parts)),
        out_specs=anywhere,
        scratch_shapes=[pltpu.SemaphoreType.DMA((len(parts),))],
        compiler_params=pltpu.CompilerParams(vmem_limit_bytes=SMALL_LIMIT),
    )(after, *parts)


def struct(shape, dtype=F32):
    return jax.ShapeDtypeStruct(shape, dtype)


def shift(value, axes, step):
    return lax.ppermute(value, axes, [(i, (i + step) % 4) for i in range(4)])


def swap_pairs():
    pairs = []
    for z in range(16):
        for t in range(8):
            pairs.append((z * 8 + t, (2 * t + z % 2) * 8 + z // 2))
    return pairs


def on_device(acts, grad_out, master, moment_one, moment_two, bit_widths, row_dither, col_dither):
    y = lax.axis_index("y")
    z = lax.axis_index(Z)
    core = lax.axis_index("c")
    tensor = lax.axis_index(TENSOR)
    spot = tensor % 4
    unit = 2 * y + tensor // 4
    pos = jnp.stack([core, spot, unit, z, y, tensor // 2]).astype(jnp.int32)
    pairs = swap_pairs()

    packed, coded = call(
        pack_kernel,
        (struct((PACK, COLS), BF16), struct((48 * SHARD, COLS), BF16)),
        0,
        (acts, grad_out, col_dither[None], master),
        (pltpu.VMEM((6 * SHARD, COLS), F32),),
        limit=LARGE_LIMIT,
    )
    rows = lax.all_to_all(coded.reshape(16, 3 * SHARD, COLS), Z, 0, 0).reshape(48 * SHARD, COLS)
    joined = join(rows, [packed[None]] + [shift(packed[None], ("xh", "xl"), step) for step in (1, 2, 3)])
    rows = lax.all_to_all(rows.reshape(8, 6 * SHARD, COLS), TENSOR, 0, 0).reshape(48 * SHARD, COLS)
    joined_other = lax.ppermute(joined, "c", [(0, 1), (1, 0)])
    bundle = join(rows, [shift(joined, "y", step) for step in (1, 2, 3)])
    bundle_other = lax.ppermute(bundle, "c", [(0, 1), (1, 0)])

    row_part = lax.dynamic_slice(row_dither, (0, BLOCK * (8 * y + tensor)), (3, BLOCK))
    row_part = jnp.broadcast_to(row_part.astype(F32).reshape(3 * BLOCK, 1) * (1.0 / 1024.0), (3 * BLOCK, COLS))

    xs, gs, terms, col_part, peak, keep, give = call(
        front_kernel,
        (
            struct((REPS * TOK, 1024), BF16),
            struct((REPS * TOK, 1024), BF16),
            struct((REPS, 3 * BLOCK, TOK), BF16),
            struct((8, 1024)),
            struct((64, 1, COLS)),
            struct((16, TOK, COLS)),
            struct((16, TOK, COLS)),
        ),
        1,
        (pos, joined, bundle, joined_other, bundle_other, rows),
        (
            pltpu.VMEM((48 * SHARD, COLS), F32),
            pltpu.VMEM((3 * BLOCK, 1024), F32),
            pltpu.VMEM((3 * BLOCK, 1024), BF16),
        ),
        limit=LARGE_LIMIT,
        first=(4, 0, 2, 1, 3),
    )
    peaks = lax.all_to_all(peak, ("xl", "c") + Z, 0, 0)
    got = lax.ppermute(give, "c", [(0, 1), (1, 0)])

    shares, *back = call(
        quant_kernel,
        (struct((16, 3, SHARD, COLS)),) + (struct((4, TOK, COLS)),) * 4,
        1,
        (pos, xs, gs, terms, peaks, bit_widths, row_part, col_part, keep, got),
        limit=LARGE_LIMIT,
        first=(3, 4, 2, 0, 1, 5, 6, 7, 8),
    )
    back = [back[0]] + [shift(back[step], "y", step) for step in (1, 2, 3)]
    shares = lax.all_to_all(shares, Z, 0, 0)

    mean_grad, *back = call(
        sum_kernel,
        (struct((3, SHARD, COLS)),) + (struct((TOK, COLS)),) * 4,
        1,
        (pos, shares, *back),
    )
    mean_grad = lax.ppermute(mean_grad, Z + TENSOR, pairs)
    back = [back[0]] + [shift(back[step], ("xh", "xl"), step) for step in (1, 2, 3)]

    updated, first, second, ring = call(
        adam_kernel,
        (struct((3, SHARD, COLS)),) * 3 + (struct((48 * SHARD, COLS), BF16),),
        0,
        (mean_grad, master, moment_one, moment_two),
        (pltpu.VMEM((6 * SHARD, COLS), F32),),
    )
    ring = lax.all_to_all(ring.reshape(16, 3 * SHARD, COLS), Z, 0, 0).reshape(48 * SHARD, COLS)
    ring, grad_in = call(
        finish_kernel,
        (struct((4, 48 * SHARD, COLS), BF16), struct((TOK, COLS), BF16)),
        0,
        (ring, *back),
    )
    ring = lax.all_to_all(ring, "y", 0, 0)
    new_weights = ring.reshape(64, 3, SHARD, COLS).transpose(1, 0, 2, 3).reshape(3, 64 * SHARD, COLS)
    return (grad_in, updated, first, second, new_weights)


def solution(mesh):
    grid = Mesh(mesh.devices.reshape(SIZES), DP + TENSOR)
    return jax.shard_map(
        on_device,
        mesh=grid,
        in_specs=(
            P(DP, TENSOR),
            P(DP, TENSOR),
            P(None, DP, TENSOR),
            P(None, DP, TENSOR),
            P(None, DP, TENSOR),
            P(),
            P(),
            P(TENSOR),
        ),
        out_specs=(
            P(DP, TENSOR),
            P(None, DP, TENSOR),
            P(None, DP, TENSOR),
            P(None, DP, TENSOR),
            P(None, None, TENSOR),
        ),
        check_vma=False,
    )
```

```python
import jax
import jax.numpy as jnp
from jax import lax
from jax.experimental import pallas as pl
from jax.experimental.pallas import tpu as pltpu
from jax.sharding import Mesh, PartitionSpec as P

F32 = jnp.float32
BF16 = jnp.bfloat16

TOK = 128
BROWS = 64
COLS = 128
SHARD = 24
BLOCK = 48
PACK = 2 * TOK + 16
REPS = 4

BETA_ONE = 0.9
BETA_TWO = 0.95
LEARN_RATE = 0.004
WEIGHT_DECAY = 0.1
ADAM_EPS = 1e-08
RANGE_EPS = 1e-06
N_DP = 64

SINE = (
    0.9999995827674866,
    -6.579691410064697,
    12.986435890197754,
    -12.188101768493652,
    6.558042526245117,
    -1.95303213596344,
)

Z = ("zh", "zl")
DP = ("y",) + Z
TENSOR = ("xh", "xl", "c")
SIZES = (4, 4, 4, 2, 2, 2)

SMALL_LIMIT = 20 * 1024 * 1024
LARGE_LIMIT = 60 * 1024 * 1024


def turn(value):
    frac = value - jnp.floor(value + 0.5)
    square = frac * frac
    total = jnp.full_like(square, SINE[-1])
    for coef in SINE[-2::-1]:
        total = total * square + coef
    return total * frac


def soft_round(value):
    return value - turn(value)


def eightbit_f32(weights):
    scale = (jnp.max(jnp.abs(weights), axis=-1, keepdims=True) + RANGE_EPS) / 127.0
    return soft_round(weights / scale) * scale


def dot(left, right, left_dim, right_dim):
    return lax.dot_general(
        left, right, (((left_dim,), (right_dim,)), ((), ())), preferred_element_type=F32
    )


def spread_coded(coded, coded_ref, wide_ref):
    for mat in range(6):
        wide_ref[mat * SHARD : (mat + 1) * SHARD, :] = coded[mat % 3]
    narrow = wide_ref[...].astype(BF16)
    for pair in range(8):
        coded_ref[pair * 6 * SHARD : (pair + 1) * 6 * SHARD, :] = narrow


def pack_kernel(acts_ref, grad_ref, dither_ref, master_ref, one_ref, two_ref, packed_ref, state_ref):
    high = (dither_ref[...] >> 3).astype(F32)
    low = (dither_ref[...] & 7).astype(F32)
    row = lax.broadcasted_iota(jnp.int32, (16, COLS), 0)
    extra = jnp.where(row == 0, high, jnp.where(row == 1, low, 0.0)).astype(BF16)
    for peer in range(16):
        packed_ref[peer, 0:TOK, :] = acts_ref[...]
        packed_ref[peer, TOK : 2 * TOK, :] = grad_ref[...]
        packed_ref[peer, 2 * TOK : PACK, :] = extra
    state_ref[0] = master_ref[...]
    state_ref[1] = one_ref[...]
    state_ref[2] = two_ref[...]


def code_kernel(state_ref, coded_ref, wide_ref):
    spread_coded(eightbit_f32(state_ref[0]), coded_ref, wide_ref)


def front_kernel(need, done, pos_ref, *refs):
    rows_ref, xs_ref, gs_ref, terms_ref, col_ref, peak_ref, keep_ref, give_ref = refs[2:10]
    wide_ref, full_ref, weights_ref = refs[10:]
    core = pos_ref[0]
    need(2)
    wide_ref[...] = rows_ref[...].astype(F32)
    for depth in range(16):
        cols = slice((depth // 2) * COLS, (depth // 2 + 1) * COLS)
        for mat in range(3):
            source = (depth * 3 + mat) * SHARD
            target = mat * BLOCK + (depth % 2) * SHARD
            full_ref[target : target + SHARD, cols] = wide_ref[source : source + SHARD, :]
    weights_ref[...] = full_ref[...].astype(BF16)
    for side, which in ((0, core), (1, 1 - core)):
        need(side)
        for chip in range(4):
            cols = pl.ds(pl.multiple_of((2 * chip + which) * COLS, COLS), COLS)
            for rep in range(REPS):
                rows = slice(rep * TOK, (rep + 1) * TOK)
                xs_ref[rows, cols] = refs[side][rep * 4 + chip, 0:TOK, :]
                gs_ref[rows, cols] = refs[side][rep * 4 + chip, TOK : 2 * TOK, :]
            pair = refs[side][chip, 2 * TOK : PACK, :].astype(F32)
            dither = pair[0:1] * 8.0 + pair[1:2]
            col_ref[:, cols] = jnp.broadcast_to(dither * (1.0 / 1024.0), (8, COLS))
    done(0, 1, 3)
    front = dot(weights_ref[0 : 2 * BLOCK, :], xs_ref[...], 1, 1)
    delta = dot(weights_ref[2 * BLOCK : 3 * BLOCK, :], gs_ref[...], 1, 1)
    gate = front[0:BLOCK]
    upper = front[BLOCK:]
    sig = jax.nn.sigmoid(gate)
    active = gate * sig
    dgate = (delta * upper * sig * (1.0 + gate * (1.0 - sig))).astype(BF16)
    dupper = (delta * active).astype(BF16)
    hidden = (active * upper).astype(BF16)
    for rep in range(REPS):
        rows = slice(rep * TOK, (rep + 1) * TOK)
        terms_ref[rep, 0:BLOCK, :] = dgate[:, rows]
        terms_ref[rep, BLOCK : 2 * BLOCK, :] = dupper[:, rows]
        terms_ref[rep, 2 * BLOCK : 3 * BLOCK, :] = hidden[:, rows]
    done(2)
    terms = jnp.concatenate([dgate, dupper], axis=0)
    for target, which in ((keep_ref, core), (give_ref, 1 - core)):
        side = []
        for chip in range(4):
            cols = pl.ds(pl.multiple_of((2 * chip + which) * COLS, COLS), COLS)
            side.append(weights_ref[0 : 2 * BLOCK, cols])
        back = dot(terms, jnp.concatenate(side, axis=1), 0, 0)
        for rep in range(REPS):
            for chip in range(4):
                target[rep * 4 + chip] = back[rep * TOK : (rep + 1) * TOK, chip * COLS : (chip + 1) * COLS]
    done(5, 6)
    peak = jnp.zeros((3 * BLOCK, COLS), F32)
    for rep in range(REPS):
        rows = slice(rep * TOK, (rep + 1) * TOK)
        for part in range(4):
            cols = slice(part * 256, (part + 1) * 256)
            grad_front = dot(terms_ref[rep, 0 : 2 * BLOCK, :], xs_ref[rows, cols], 1, 0)
            grad_down = dot(terms_ref[rep, 2 * BLOCK : 3 * BLOCK, :], gs_ref[rows, cols], 1, 0)
            grads = jnp.abs(jnp.concatenate([grad_front, grad_down], axis=0))
            peak = jnp.maximum(peak, jnp.maximum(grads[:, :COLS], grads[:, COLS:]))
    lane = lax.broadcasted_iota(jnp.int32, (1, COLS), 1)
    packed = jnp.zeros((1, COLS), F32)
    for group in range(9):
        top = jnp.max(peak[group * 16 : (group + 1) * 16], axis=0, keepdims=True)
        top = jnp.max(top, axis=1, keepdims=True)
        packed = jnp.where(lane == group, top, packed)
    peak_ref[...] = jnp.broadcast_to(packed.reshape(1, 1, COLS), peak_ref.shape)
    done(4)


def quant_kernel(need, done, pos_ref, xs_ref, gs_ref, terms_ref, peaks_ref, bits_ref, row_ref, col_ref, keep_ref, got_ref, out_ref, *back_refs):
    need(3, 4)
    spot = pos_ref[1]
    unit = pos_ref[2]
    depth = pos_ref[3]
    lane = lax.broadcasted_iota(jnp.int32, (1, COLS), 1)
    buck = lax.broadcasted_iota(jnp.int32, (1, 24), 1)
    tops = [jnp.max(peaks_ref[i * 16 : (i + 1) * 16], axis=0) for i in range(4)]
    scales = []
    for mat in range(3):
        per_bucket = []
        for bucket in range(3):
            held = jnp.zeros((1, COLS), F32)
            for sub in range(4 * bucket, 4 * bucket + 4):
                held = jnp.maximum(held, jnp.where(lane == mat * 3 + sub % 3, tops[sub // 3], 0.0))
            ranges = jnp.max(held, axis=1, keepdims=True)
            bits = jnp.where(buck == 3 * unit + bucket, bits_ref[mat : mat + 1, :].astype(F32), 0.0)
            bits = jnp.max(bits, axis=1, keepdims=True)
            levels = jnp.ones_like(bits)
            for count in range(3, 9):
                levels = jnp.where(bits == float(count), float(2 ** (count - 1) - 1), levels)
            per_bucket.append((ranges + RANGE_EPS) / levels)
        for sub in range(3):
            which = (3 * spot + sub) // 4
            chosen = jnp.where(which == 0, per_bucket[0], jnp.where(which == 1, per_bucket[1], per_bucket[2]))
            scales.append(jnp.broadcast_to(chosen, (16, COLS)))
    scale = jnp.concatenate(scales, axis=0)
    inverse = 1.0 / scale
    scale = scale * (1.0 / N_DP)
    need(0, 1, 2, 5, 6)
    row_part = row_ref[...]
    for part in range(4):
        cols = slice(part * 256, (part + 1) * 256)
        halves = [jnp.zeros((3 * BLOCK, COLS), F32) for _ in range(2)]
        for rep in range(REPS):
            rows = slice(rep * TOK, (rep + 1) * TOK)
            grad_front = dot(terms_ref[rep, 0 : 2 * BLOCK, :], xs_ref[rows, cols], 1, 0)
            grad_down = dot(terms_ref[rep, 2 * BLOCK : 3 * BLOCK, :], gs_ref[rows, cols], 1, 0)
            grads = jnp.concatenate([grad_front, grad_down], axis=0)
            offset = lax.rem(389 * (rep * 16 + depth), 1024).astype(F32) * (1.0 / 1024.0)
            for half in range(2):
                lanes = slice(half * COLS, (half + 1) * COLS)
                whole = slice(part * 256 + half * COLS, part * 256 + (half + 1) * COLS)
                ratio = grads[:, lanes] * inverse
                phase = row_part + (col_ref[0:1, whole] + offset)
                halves[half] = halves[half] + (ratio + turn(ratio + phase))
        for half in range(2):
            result = halves[half] * scale
            for mat in range(3):
                for low in range(2):
                    start = mat * BLOCK + low * SHARD
                    out_ref[2 * (2 * part + half) + low, mat, :, :] = result[start : start + SHARD]
    done(0)
    need(7, 8)
    plane = pos_ref[4]
    for step, back_ref in enumerate(back_refs):
        first = ((plane + step) % 4) * 4
        for chip in range(4):
            back_ref[chip] = keep_ref[first + chip] + got_ref[first + chip]
        done(1 + step)


def adam_kernel(pos_ref, shares_ref, state_ref, own_ref, up_ref, across_ref, down_ref, new_state_ref, coded_ref, *refs):
    wide_ref = refs[-1]
    mean_grad = shares_ref[0]
    for peer in range(1, 16):
        mean_grad = mean_grad + shares_ref[peer]
    master = state_ref[0]
    first = BETA_ONE * state_ref[1] + (1.0 - BETA_ONE) * mean_grad
    second = BETA_TWO * state_ref[2] + (1.0 - BETA_TWO) * mean_grad * mean_grad
    updated = master - LEARN_RATE * (first / (jnp.sqrt(second) + ADAM_EPS) + WEIGHT_DECAY * master)
    new_state_ref[0] = updated
    new_state_ref[1] = first
    new_state_ref[2] = second
    spread_coded(eightbit_f32(updated), coded_ref, wide_ref)
    for step, back_ref in enumerate(refs[:-1]):
        which = (pos_ref[5] + step) % 4
        back_ref[...] = (own_ref[which] + up_ref[which]) + (across_ref[which] + down_ref[which])


def finish_kernel(ring_ref, own_ref, right_ref, across_ref, left_ref, spread_ref, grad_ref):
    for plane in range(4):
        spread_ref[plane] = ring_ref[...]
    grad_ref[...] = ((own_ref[...] + right_ref[...]) + (across_ref[...] + left_ref[...])).astype(BF16)


def call(kernel, out_shape, smem=0, operands=(), scratch=(), limit=SMALL_LIMIT, first=None):
    single = not isinstance(out_shape, tuple)
    outs = (out_shape,) if single else out_shape
    n_in = len(operands) - smem
    n_out = len(outs)

    def body(*refs):
        small = refs[:smem]
        sources = refs[smem : smem + n_in]
        targets = refs[smem + n_in : smem + n_in + n_out]
        held = refs[smem + n_in + n_out :]
        taken, made, rest, sems = held[:n_in], held[n_in : n_in + n_out], held[n_in + n_out : -1], held[-1]
        loads = [pltpu.make_async_copy(sources[i], taken[i], sems.at[i]) for i in range(n_in)]
        stores = [pltpu.make_async_copy(made[i], targets[i], sems.at[n_in + i]) for i in range(n_out)]
        if first is None:
            for load in loads:
                load.start()
            for load in loads:
                load.wait()
            kernel(*small, *taken, *made, *rest)
            for store in stores:
                store.start()
        else:
            for i in first:
                loads[i].start()

            def need(*which):
                for i in which:
                    loads[i].wait()

            def done(*which):
                for i in which:
                    stores[i].start()

            kernel(need, done, *small, *taken, *made, *rest)
        for store in stores:
            store.wait()

    anywhere = pl.BlockSpec(memory_space=pl.ANY)
    specs = [pl.BlockSpec(memory_space=pltpu.SMEM)] * smem + [anywhere] * n_in
    buffers = [pltpu.VMEM(item.shape, item.dtype) for item in tuple(operands[smem:]) + outs]
    return pl.pallas_call(
        body,
        out_shape=out_shape,
        in_specs=specs,
        out_specs=anywhere if single else (anywhere,) * n_out,
        scratch_shapes=buffers + list(scratch) + [pltpu.SemaphoreType.DMA((n_in + n_out,))],
        compiler_params=pltpu.CompilerParams(vmem_limit_bytes=limit),
    )(*operands)


def struct(shape, dtype=F32):
    return jax.ShapeDtypeStruct(shape, dtype)


def shift(value, axes, step):
    return lax.ppermute(value, axes, [(i, (i + step) % 4) for i in range(4)])


def swap_pairs():
    pairs = []
    for z in range(16):
        for t in range(8):
            pairs.append((z * 8 + t, (2 * t + z % 2) * 8 + z // 2))
    return pairs


def on_device(acts, grad_out, master, moment_one, moment_two, bit_widths, row_dither, col_dither):
    y = lax.axis_index("y")
    z = lax.axis_index(Z)
    core = lax.axis_index("c")
    tensor = lax.axis_index(TENSOR)
    spot = tensor % 4
    unit = 2 * y + tensor // 4
    pos = jnp.stack([core, spot, unit, z, y, tensor // 2]).astype(jnp.int32)
    pairs = swap_pairs()

    packed, state = call(
        pack_kernel,
        (struct((16, PACK, COLS), BF16), struct((3, 3, SHARD, COLS))),
        0,
        (acts, grad_out, col_dither[None], master, moment_one, moment_two),
        limit=LARGE_LIMIT,
    )
    state = lax.ppermute(state, Z + TENSOR, pairs)
    wide = (pltpu.VMEM((6 * SHARD, COLS), F32),)
    coded = call(code_kernel, struct((48 * SHARD, COLS), BF16), 0, (state,), wide)
    rows = lax.all_to_all(coded.reshape(16, 3 * SHARD, COLS), Z, 0, 0).reshape(48 * SHARD, COLS)
    own = lax.all_to_all(packed, ("y", "xh", "xl"), 0, 0)
    other = lax.ppermute(own, "c", [(0, 1), (1, 0)])

    row_part = lax.dynamic_slice(row_dither, (0, BLOCK * (8 * y + tensor)), (3, BLOCK))
    row_part = jnp.broadcast_to(row_part.astype(F32).reshape(3 * BLOCK, 1) * (1.0 / 1024.0), (3 * BLOCK, COLS))

    xs, gs, terms, col_part, peak, keep, give = call(
        front_kernel,
        (
            struct((REPS * TOK, 1024), BF16),
            struct((REPS * TOK, 1024), BF16),
            struct((REPS, 3 * BLOCK, TOK), BF16),
            struct((8, 1024)),
            struct((64, 1, COLS)),
            struct((16, TOK, COLS)),
            struct((16, TOK, COLS)),
        ),
        1,
        (pos, own, other, rows),
        (
            pltpu.VMEM((48 * SHARD, COLS), F32),
            pltpu.VMEM((3 * BLOCK, 1024), F32),
            pltpu.VMEM((3 * BLOCK, 1024), BF16),
        ),
        limit=LARGE_LIMIT,
        first=(2, 0, 1),
    )
    peaks = lax.all_to_all(peak, ("xl", "c") + Z, 0, 0)
    got = lax.ppermute(give, "c", [(0, 1), (1, 0)])

    shares, *back = call(
        quant_kernel,
        (struct((16, 3, SHARD, COLS)),) + (struct((4, TOK, COLS)),) * 4,
        1,
        (pos, xs, gs, terms, peaks, bit_widths, row_part, col_part, keep, got),
        limit=LARGE_LIMIT,
        first=(3, 4, 2, 0, 1, 5, 6, 7, 8),
    )
    back = [back[0]] + [shift(back[step], "y", step) for step in (1, 2, 3)]
    shares = lax.all_to_all(shares, Z, 0, 0)

    new_state, ring, *back = call(
        adam_kernel,
        (struct((3, 3, SHARD, COLS)), struct((48 * SHARD, COLS), BF16)) + (struct((TOK, COLS)),) * 4,
        1,
        (pos, shares, state, *back),
        wide,
    )
    back = [back[0]] + [shift(back[step], ("xh", "xl"), step) for step in (1, 2, 3)]
    ring = lax.all_to_all(ring.reshape(16, 3 * SHARD, COLS), Z, 0, 0).reshape(48 * SHARD, COLS)
    ring, grad_in = call(
        finish_kernel,
        (struct((4, 48 * SHARD, COLS), BF16), struct((TOK, COLS), BF16)),
        0,
        (ring, *back),
    )
    new_state = lax.ppermute(new_state, Z + TENSOR, pairs)
    ring = lax.all_to_all(ring.reshape(32, 6 * SHARD, COLS), ("y",) + TENSOR, 0, 0)
    new_weights = ring.reshape(32, 2, 3, SHARD, COLS).transpose(2, 0, 1, 3, 4).reshape(3, 64 * SHARD, COLS)
    return (grad_in, new_state[0], new_state[1], new_state[2], new_weights)


def solution(mesh):
    grid = Mesh(mesh.devices.reshape(SIZES), DP + TENSOR)
    return jax.shard_map(
        on_device,
        mesh=grid,
        in_specs=(
            P(DP, TENSOR),
            P(DP, TENSOR),
            P(None, DP, TENSOR),
            P(None, DP, TENSOR),
            P(None, DP, TENSOR),
            P(),
            P(),
            P(TENSOR),
        ),
        out_specs=(
            P(DP, TENSOR),
            P(None, DP, TENSOR),
            P(None, DP, TENSOR),
            P(None, DP, TENSOR),
            P(None, None, TENSOR),
        ),
        check_vma=False,
    )
```

```python
import jax
import jax.numpy as jnp
from jax import lax
from jax.experimental import pallas as pl
from jax.experimental.pallas import tpu as pltpu
from jax.sharding import Mesh, PartitionSpec as P

F32 = jnp.float32
BF16 = jnp.bfloat16

TOK = 128
BROWS = 64
COLS = 128
SHARD = 24
BLOCK = 48
PACK = 2 * TOK + 16
REPS = 4

BETA_ONE = 0.9
BETA_TWO = 0.95
LEARN_RATE = 0.004
WEIGHT_DECAY = 0.1
ADAM_EPS = 1e-08
RANGE_EPS = 1e-06
N_DP = 64

SINE = (
    0.9999995827674866,
    -6.579691410064697,
    12.986435890197754,
    -12.188101768493652,
    6.558042526245117,
    -1.95303213596344,
)

Z = ("zh", "zl")
DP = ("y",) + Z
TENSOR = ("xh", "xl", "c")
SIZES = (4, 4, 4, 2, 2, 2)

SMALL_LIMIT = 20 * 1024 * 1024
LARGE_LIMIT = 60 * 1024 * 1024


def turn(value):
    frac = value - jnp.floor(value + 0.5)
    square = frac * frac
    total = jnp.full_like(square, SINE[-1])
    for coef in SINE[-2::-1]:
        total = total * square + coef
    return total * frac


def soft_round(value):
    return value - turn(value)


def eightbit_f32(weights):
    scale = (jnp.max(jnp.abs(weights), axis=-1, keepdims=True) + RANGE_EPS) / 127.0
    return soft_round(weights / scale) * scale


def dot(left, right, left_dim, right_dim):
    return lax.dot_general(
        left, right, (((left_dim,), (right_dim,)), ((), ())), preferred_element_type=F32
    )


def spread_coded(coded, coded_ref, wide_ref):
    for mat in range(6):
        wide_ref[mat * SHARD : (mat + 1) * SHARD, :] = coded[mat % 3]
    narrow = wide_ref[...].astype(BF16)
    for pair in range(8):
        coded_ref[pair * 6 * SHARD : (pair + 1) * 6 * SHARD, :] = narrow


def pack_kernel(acts_ref, grad_ref, dither_ref, master_ref, one_ref, two_ref, packed_ref, state_ref):
    high = (dither_ref[...] >> 3).astype(F32)
    low = (dither_ref[...] & 7).astype(F32)
    row = lax.broadcasted_iota(jnp.int32, (16, COLS), 0)
    extra = jnp.where(row == 0, high, jnp.where(row == 1, low, 0.0)).astype(BF16)
    for peer in range(16):
        packed_ref[peer, 0:TOK, :] = acts_ref[...]
        packed_ref[peer, TOK : 2 * TOK, :] = grad_ref[...]
        packed_ref[peer, 2 * TOK : PACK, :] = extra
    state_ref[0] = master_ref[...]
    state_ref[1] = one_ref[...]
    state_ref[2] = two_ref[...]


def code_kernel(state_ref, coded_ref, wide_ref):
    spread_coded(eightbit_f32(state_ref[0]), coded_ref, wide_ref)


def front_kernel(need, done, pos_ref, *refs):
    rows_ref, xs_ref, gs_ref, terms_ref, col_ref, peak_ref, keep_ref, give_ref = refs[2:10]
    wide_ref, full_ref, weights_ref = refs[10:]
    core = pos_ref[0]
    need(2)
    wide_ref[...] = rows_ref[...].astype(F32)
    for depth in range(16):
        cols = slice((depth // 2) * COLS, (depth // 2 + 1) * COLS)
        for mat in range(3):
            source = (depth * 3 + mat) * SHARD
            target = mat * BLOCK + (depth % 2) * SHARD
            full_ref[target : target + SHARD, cols] = wide_ref[source : source + SHARD, :]
    weights_ref[...] = full_ref[...].astype(BF16)
    for side, which in ((0, core), (1, 1 - core)):
        need(side)
        for chip in range(4):
            cols = pl.ds(pl.multiple_of((2 * chip + which) * COLS, COLS), COLS)
            for rep in range(REPS):
                rows = slice(rep * TOK, (rep + 1) * TOK)
                xs_ref[rows, cols] = refs[side][rep * 4 + chip, 0:TOK, :]
                gs_ref[rows, cols] = refs[side][rep * 4 + chip, TOK : 2 * TOK, :]
            pair = refs[side][chip, 2 * TOK : PACK, :].astype(F32)
            dither = pair[0:1] * 8.0 + pair[1:2]
            col_ref[:, cols] = jnp.broadcast_to(dither * (1.0 / 1024.0), (8, COLS))
    done(0, 1, 3)
    front = dot(weights_ref[0 : 2 * BLOCK, :], xs_ref[...], 1, 1)
    delta = dot(weights_ref[2 * BLOCK : 3 * BLOCK, :], gs_ref[...], 1, 1)
    gate = front[0:BLOCK]
    upper = front[BLOCK:]
    sig = jax.nn.sigmoid(gate)
    active = gate * sig
    dgate = (delta * upper * sig * (1.0 + gate * (1.0 - sig))).astype(BF16)
    dupper = (delta * active).astype(BF16)
    hidden = (active * upper).astype(BF16)
    for rep in range(REPS):
        rows = slice(rep * TOK, (rep + 1) * TOK)
        terms_ref[rep, 0:BLOCK, :] = dgate[:, rows]
        terms_ref[rep, BLOCK : 2 * BLOCK, :] = dupper[:, rows]
        terms_ref[rep, 2 * BLOCK : 3 * BLOCK, :] = hidden[:, rows]
    done(2)
    for target, which in ((keep_ref, core), (give_ref, 1 - core)):
        side = []
        for chip in range(4):
            cols = pl.ds(pl.multiple_of((2 * chip + which) * COLS, COLS), COLS)
            side.append(weights_ref[0 : 2 * BLOCK, cols])
        side = jnp.concatenate(side, axis=1)
        for rep in range(REPS):
            back = dot(terms_ref[rep, 0 : 2 * BLOCK, :], side, 0, 0)
            for chip in range(4):
                target[rep * 4 + chip] = back[:, chip * COLS : (chip + 1) * COLS]
    done(5, 6)
    peak = jnp.zeros((3 * BLOCK, COLS), F32)
    for rep in range(REPS):
        rows = slice(rep * TOK, (rep + 1) * TOK)
        for part in range(4):
            cols = slice(part * 256, (part + 1) * 256)
            grad_front = dot(terms_ref[rep, 0 : 2 * BLOCK, :], xs_ref[rows, cols], 1, 0)
            grad_down = dot(terms_ref[rep, 2 * BLOCK : 3 * BLOCK, :], gs_ref[rows, cols], 1, 0)
            grads = jnp.abs(jnp.concatenate([grad_front, grad_down], axis=0))
            peak = jnp.maximum(peak, jnp.maximum(grads[:, :COLS], grads[:, COLS:]))
    lane = lax.broadcasted_iota(jnp.int32, (1, COLS), 1)
    packed = jnp.zeros((1, COLS), F32)
    for group in range(9):
        top = jnp.max(peak[group * 16 : (group + 1) * 16], axis=0, keepdims=True)
        top = jnp.max(top, axis=1, keepdims=True)
        packed = jnp.where(lane == group, top, packed)
    peak_ref[...] = jnp.broadcast_to(packed.reshape(1, 1, COLS), peak_ref.shape)
    done(4)


def pair_kernel(pos_ref, keep_ref, got_ref, *back_refs):
    for step, back_ref in enumerate(back_refs):
        first = ((pos_ref[4] + step) % 4) * 4
        for chip in range(4):
            back_ref[chip] = keep_ref[first + chip] + got_ref[first + chip]


def plane_kernel(pos_ref, own_ref, up_ref, across_ref, down_ref, *back_refs):
    for step, back_ref in enumerate(back_refs):
        which = (pos_ref[5] + step) % 4
        back_ref[...] = (own_ref[which] + up_ref[which]) + (across_ref[which] + down_ref[which])


def quant_kernel(need, done, pos_ref, xs_ref, gs_ref, terms_ref, peaks_ref, bits_ref, row_ref, col_ref, out_ref, wide_ref):
    need(3, 4)
    spot = pos_ref[1]
    unit = pos_ref[2]
    depth = pos_ref[3]
    lane = lax.broadcasted_iota(jnp.int32, (1, COLS), 1)
    buck = lax.broadcasted_iota(jnp.int32, (1, 24), 1)
    tops = [jnp.max(peaks_ref[i * 16 : (i + 1) * 16], axis=0) for i in range(4)]
    scales = []
    for mat in range(3):
        per_bucket = []
        for bucket in range(3):
            held = jnp.zeros((1, COLS), F32)
            for sub in range(4 * bucket, 4 * bucket + 4):
                held = jnp.maximum(held, jnp.where(lane == mat * 3 + sub % 3, tops[sub // 3], 0.0))
            ranges = jnp.max(held, axis=1, keepdims=True)
            bits = jnp.where(buck == 3 * unit + bucket, bits_ref[mat : mat + 1, :].astype(F32), 0.0)
            bits = jnp.max(bits, axis=1, keepdims=True)
            levels = jnp.ones_like(bits)
            for count in range(3, 9):
                levels = jnp.where(bits == float(count), float(2 ** (count - 1) - 1), levels)
            per_bucket.append((ranges + RANGE_EPS) / levels)
        for sub in range(3):
            which = (3 * spot + sub) // 4
            chosen = jnp.where(which == 0, per_bucket[0], jnp.where(which == 1, per_bucket[1], per_bucket[2]))
            scales.append(jnp.broadcast_to(chosen, (16, COLS)))
    scale = jnp.concatenate(scales, axis=0)
    inverse = 1.0 / scale
    scale = scale * (1.0 / N_DP)
    need(0, 1, 2, 5, 6)
    row_part = row_ref[...]
    for part in range(4):
        cols = slice(part * 256, (part + 1) * 256)
        halves = [jnp.zeros((3 * BLOCK, COLS), F32) for _ in range(2)]
        for rep in range(REPS):
            rows = slice(rep * TOK, (rep + 1) * TOK)
            grad_front = dot(terms_ref[rep, 0 : 2 * BLOCK, :], xs_ref[rows, cols], 1, 0)
            grad_down = dot(terms_ref[rep, 2 * BLOCK : 3 * BLOCK, :], gs_ref[rows, cols], 1, 0)
            grads = jnp.concatenate([grad_front, grad_down], axis=0)
            offset = lax.rem(389 * (rep * 16 + depth), 1024).astype(F32) * (1.0 / 1024.0)
            for half in range(2):
                lanes = slice(half * COLS, (half + 1) * COLS)
                whole = slice(part * 256 + half * COLS, part * 256 + (half + 1) * COLS)
                ratio = grads[:, lanes] * inverse
                phase = row_part + (col_ref[0:1, whole] + offset)
                halves[half] = halves[half] + (ratio + turn(ratio + phase))
        for half in range(2):
            result = halves[half] * scale
            pair = 6 * SHARD * (2 * part + half)
            for mat in range(3):
                for low in range(2):
                    start = mat * BLOCK + low * SHARD
                    target = pair + (low * 3 + mat) * SHARD
                    wide_ref[target : target + SHARD, :] = result[start : start + SHARD]
            out_ref[pair : pair + 6 * SHARD, :] = wide_ref[pair : pair + 6 * SHARD, :].astype(BF16)
    done(0)


def adam_kernel(shares_ref, state_ref, new_state_ref, coded_ref, wide_ref, all_ref):
    all_ref[...] = shares_ref[...].astype(F32)
    mean_grad = all_ref[0 : 3 * SHARD]
    for peer in range(1, 16):
        mean_grad = mean_grad + all_ref[peer * 3 * SHARD : (peer + 1) * 3 * SHARD]
    mean_grad = mean_grad.reshape(3, SHARD, COLS)
    master = state_ref[0]
    first = BETA_ONE * state_ref[1] + (1.0 - BETA_ONE) * mean_grad
    second = BETA_TWO * state_ref[2] + (1.0 - BETA_TWO) * mean_grad * mean_grad
    updated = master - LEARN_RATE * (first / (jnp.sqrt(second) + ADAM_EPS) + WEIGHT_DECAY * master)
    new_state_ref[0] = updated
    new_state_ref[1] = first
    new_state_ref[2] = second
    spread_coded(eightbit_f32(updated), coded_ref, wide_ref)


def finish_kernel(ring_ref, own_ref, right_ref, across_ref, left_ref, spread_ref, grad_ref):
    for plane in range(4):
        spread_ref[plane] = ring_ref[...]
    grad_ref[...] = ((own_ref[...] + right_ref[...]) + (across_ref[...] + left_ref[...])).astype(BF16)


def call(kernel, out_shape, smem=0, operands=(), scratch=(), limit=SMALL_LIMIT, first=None, idle=0):
    single = not isinstance(out_shape, tuple)
    outs = (out_shape,) if single else out_shape
    n_in = len(operands) - smem - idle
    n_out = len(outs)

    def body(*refs):
        small = refs[:smem]
        sources = refs[smem : smem + n_in]
        targets = refs[smem + n_in + idle : smem + n_in + idle + n_out]
        held = refs[smem + n_in + idle + n_out :]
        taken, made, rest, sems = held[:n_in], held[n_in : n_in + n_out], held[n_in + n_out : -1], held[-1]
        loads = [pltpu.make_async_copy(sources[i], taken[i], sems.at[i]) for i in range(n_in)]
        stores = [pltpu.make_async_copy(made[i], targets[i], sems.at[n_in + i]) for i in range(n_out)]
        if first is None:
            for load in loads:
                load.start()
            for load in loads:
                load.wait()
            kernel(*small, *taken, *made, *rest)
            for store in stores:
                store.start()
        else:
            for i in first:
                loads[i].start()

            def need(*which):
                for i in which:
                    loads[i].wait()

            def done(*which):
                for i in which:
                    stores[i].start()

            kernel(need, done, *small, *taken, *made, *rest)
        for store in stores:
            store.wait()

    anywhere = pl.BlockSpec(memory_space=pl.ANY)
    specs = [pl.BlockSpec(memory_space=pltpu.SMEM)] * smem + [anywhere] * (n_in + idle)
    buffers = [pltpu.VMEM(item.shape, item.dtype) for item in tuple(operands[smem : smem + n_in]) + outs]
    return pl.pallas_call(
        body,
        out_shape=out_shape,
        in_specs=specs,
        out_specs=anywhere if single else (anywhere,) * n_out,
        scratch_shapes=buffers + list(scratch) + [pltpu.SemaphoreType.DMA((n_in + n_out,))],
        compiler_params=pltpu.CompilerParams(vmem_limit_bytes=limit),
    )(*operands)


def struct(shape, dtype=F32):
    return jax.ShapeDtypeStruct(shape, dtype)


def shift(value, axes, step):
    return lax.ppermute(value, axes, [(i, (i + step) % 4) for i in range(4)])


def swap_pairs():
    pairs = []
    for z in range(16):
        for t in range(8):
            pairs.append((z * 8 + t, (2 * t + z % 2) * 8 + z // 2))
    return pairs


def on_device(acts, grad_out, master, moment_one, moment_two, bit_widths, row_dither, col_dither):
    y = lax.axis_index("y")
    z = lax.axis_index(Z)
    core = lax.axis_index("c")
    tensor = lax.axis_index(TENSOR)
    spot = tensor % 4
    unit = 2 * y + tensor // 4
    pos = jnp.stack([core, spot, unit, z, y, tensor // 2]).astype(jnp.int32)
    pairs = swap_pairs()

    packed, state = call(
        pack_kernel,
        (struct((16, PACK, COLS), BF16), struct((3, 3, SHARD, COLS))),
        0,
        (acts, grad_out, col_dither[None], master, moment_one, moment_two),
        limit=LARGE_LIMIT,
    )
    state = lax.ppermute(state, Z + TENSOR, pairs)
    wide = (pltpu.VMEM((6 * SHARD, COLS), F32),)
    coded = call(code_kernel, struct((48 * SHARD, COLS), BF16), 0, (state,), wide)
    rows = lax.all_to_all(coded.reshape(16, 3 * SHARD, COLS), Z, 0, 0).reshape(48 * SHARD, COLS)
    own = lax.all_to_all(packed, ("y", "xh", "xl"), 0, 0)
    other = lax.ppermute(own, "c", [(0, 1), (1, 0)])

    row_part = lax.dynamic_slice(row_dither, (0, BLOCK * (8 * y + tensor)), (3, BLOCK))
    row_part = jnp.broadcast_to(row_part.astype(F32).reshape(3 * BLOCK, 1) * (1.0 / 1024.0), (3 * BLOCK, COLS))

    xs, gs, terms, col_part, peak, keep, give = call(
        front_kernel,
        (
            struct((REPS * TOK, 1024), BF16),
            struct((REPS * TOK, 1024), BF16),
            struct((REPS, 3 * BLOCK, TOK), BF16),
            struct((8, 1024)),
            struct((64, 1, COLS)),
            struct((16, TOK, COLS)),
            struct((16, TOK, COLS)),
        ),
        1,
        (pos, own, other, rows),
        (
            pltpu.VMEM((48 * SHARD, COLS), F32),
            pltpu.VMEM((3 * BLOCK, 1024), F32),
            pltpu.VMEM((3 * BLOCK, 1024), BF16),
        ),
        limit=LARGE_LIMIT,
        first=(2, 0, 1),
    )
    peaks = lax.all_to_all(peak, ("xl", "c") + Z, 0, 0)
    got = lax.ppermute(give, "c", [(0, 1), (1, 0)])
    back = call(pair_kernel, (struct((4, TOK, COLS)),) * 4, 1, (pos, keep, got, row_part), idle=1)

    shares = call(
        quant_kernel,
        struct((48 * SHARD, COLS), BF16),
        1,
        (pos, xs, gs, terms, peaks, bit_widths, row_part, col_part, back[0]),
        (pltpu.VMEM((48 * SHARD, COLS), F32),),
        limit=LARGE_LIMIT,
        first=(3, 4, 2, 0, 1, 5, 6),
        idle=1,
    )
    back = [back[0]] + [shift(back[step], "y", step) for step in (1, 2, 3)]
    shares = lax.all_to_all(shares.reshape(16, 3 * SHARD, COLS), Z, 0, 0).reshape(48 * SHARD, COLS)

    new_state, ring = call(
        adam_kernel,
        (struct((3, 3, SHARD, COLS)), struct((48 * SHARD, COLS), BF16)),
        0,
        (shares, state, *back[1:]),
        wide + (pltpu.VMEM((48 * SHARD, COLS), F32),),
        idle=3,
    )
    back = call(plane_kernel, (struct((TOK, COLS)),) * 4, 1, (pos, *back))
    back = [back[0]] + [shift(back[step], ("xh", "xl"), step) for step in (1, 2, 3)]
    ring = lax.all_to_all(ring.reshape(16, 3 * SHARD, COLS), Z, 0, 0).reshape(48 * SHARD, COLS)
    ring, grad_in = call(
        finish_kernel,
        (struct((4, 48 * SHARD, COLS), BF16), struct((TOK, COLS), BF16)),
        0,
        (ring, *back),
    )
    new_state = lax.ppermute(new_state, Z + TENSOR, pairs)
    ring = lax.all_to_all(ring.reshape(32, 6 * SHARD, COLS), ("y",) + TENSOR, 0, 0)
    new_weights = ring.reshape(32, 2, 3, SHARD, COLS).transpose(2, 0, 1, 3, 4).reshape(3, 64 * SHARD, COLS)
    return (grad_in, new_state[0], new_state[1], new_state[2], new_weights)


def solution(mesh):
    grid = Mesh(mesh.devices.reshape(SIZES), DP + TENSOR)
    return jax.shard_map(
        on_device,
        mesh=grid,
        in_specs=(
            P(DP, TENSOR),
            P(DP, TENSOR),
            P(None, DP, TENSOR),
            P(None, DP, TENSOR),
            P(None, DP, TENSOR),
            P(),
            P(),
            P(TENSOR),
        ),
        out_specs=(
            P(DP, TENSOR),
            P(None, DP, TENSOR),
            P(None, DP, TENSOR),
            P(None, DP, TENSOR),
            P(None, None, TENSOR),
        ),
        check_vma=False,
    )
```

```python
import jax
import jax.numpy as jnp
from jax import lax
from jax.experimental import pallas as pl
from jax.experimental.pallas import tpu as pltpu
from jax.sharding import Mesh, PartitionSpec as P

F32 = jnp.float32
BF16 = jnp.bfloat16

TOK = 128
BROWS = 64
COLS = 128
SHARD = 24
BLOCK = 48
PACK = 2 * TOK + 16
REPS = 4

BETA_ONE = 0.9
BETA_TWO = 0.95
LEARN_RATE = 0.004
WEIGHT_DECAY = 0.1
ADAM_EPS = 1e-08
RANGE_EPS = 1e-06
N_DP = 64

SINE = (
    0.9999995827674866,
    -6.579691410064697,
    12.986435890197754,
    -12.188101768493652,
    6.558042526245117,
    -1.95303213596344,
)

Z = ("zh", "zl")
DP = ("y",) + Z
TENSOR = ("xh", "xl", "c")
SIZES = (4, 4, 4, 2, 2, 2)

SMALL_LIMIT = 20 * 1024 * 1024
LARGE_LIMIT = 60 * 1024 * 1024


def turn(value):
    frac = value - jnp.floor(value + 0.5)
    square = frac * frac
    total = jnp.full_like(square, SINE[-1])
    for coef in SINE[-2::-1]:
        total = total * square + coef
    return total * frac


def soft_round(value):
    return value - turn(value)


def eightbit_f32(weights):
    scale = (jnp.max(jnp.abs(weights), axis=-1, keepdims=True) + RANGE_EPS) / 127.0
    return soft_round(weights / scale) * scale


def dot(left, right, left_dim, right_dim):
    return lax.dot_general(
        left, right, (((left_dim,), (right_dim,)), ((), ())), preferred_element_type=F32
    )


def spread_coded(coded, coded_ref, wide_ref):
    for mat in range(6):
        wide_ref[mat * SHARD : (mat + 1) * SHARD, :] = coded[mat % 3]
    narrow = wide_ref[...].astype(BF16)
    for pair in range(8):
        coded_ref[pair * 6 * SHARD : (pair + 1) * 6 * SHARD, :] = narrow


def pack_kernel(acts_ref, grad_ref, dither_ref, *refs):
    state_in, (packed_ref, state_ref, held_ref, dither_held_ref, sems) = refs[:3], refs[3:]
    loads = [
        pltpu.make_async_copy(acts_ref, held_ref.at[pl.ds(0, TOK)], sems.at[0]),
        pltpu.make_async_copy(grad_ref, held_ref.at[pl.ds(TOK, TOK)], sems.at[1]),
        pltpu.make_async_copy(dither_ref, dither_held_ref, sems.at[2]),
    ]
    copies = [pltpu.make_async_copy(state_in[i], state_ref.at[i], sems.at[3 + i]) for i in range(3)]
    for copy in loads + copies:
        copy.start()
    loads[2].wait()
    high = (dither_held_ref[...] >> 3).astype(F32)
    low = (dither_held_ref[...] & 7).astype(F32)
    row = lax.broadcasted_iota(jnp.int32, (16, COLS), 0)
    held_ref[2 * TOK : PACK, :] = jnp.where(row == 0, high, jnp.where(row == 1, low, 0.0)).astype(BF16)
    loads[0].wait()
    loads[1].wait()
    stores = [pltpu.make_async_copy(held_ref, packed_ref.at[peer], sems.at[6 + peer]) for peer in range(16)]
    for store in stores:
        store.start()
    for copy in copies + stores:
        copy.wait()


def code_kernel(state_ref, coded_ref, wide_ref):
    spread_coded(eightbit_f32(state_ref[0]), coded_ref, wide_ref)


def layout_kernel(pos_ref, own_ref, other_ref, xs_ref, gs_ref, col_ref):
    core = pos_ref[0]
    for source, which in ((own_ref, core), (other_ref, 1 - core)):
        for chip in range(4):
            cols = pl.ds(pl.multiple_of((2 * chip + which) * COLS, COLS), COLS)
            for rep in range(REPS):
                rows = slice(rep * TOK, (rep + 1) * TOK)
                xs_ref[rows, cols] = source[rep * 4 + chip, 0:TOK, :]
                gs_ref[rows, cols] = source[rep * 4 + chip, TOK : 2 * TOK, :]
            pair = source[chip, 2 * TOK : PACK, :].astype(F32)
            dither = pair[0:1] * 8.0 + pair[1:2]
            col_ref[:, cols] = jnp.broadcast_to(dither * (1.0 / 1024.0), (8, COLS))


def front_kernel(need, done, pos_ref, *refs):
    xs_ref, gs_ref, rows_ref, terms_ref, peak_ref, keep_ref, give_ref, wide_ref, full_ref, weights_ref = refs
    core = pos_ref[0]
    need(2)
    wide_ref[...] = rows_ref[...].astype(F32)
    for depth in range(16):
        cols = slice((depth // 2) * COLS, (depth // 2 + 1) * COLS)
        for mat in range(3):
            source = (depth * 3 + mat) * SHARD
            target = mat * BLOCK + (depth % 2) * SHARD
            full_ref[target : target + SHARD, cols] = wide_ref[source : source + SHARD, :]
    weights_ref[...] = full_ref[...].astype(BF16)
    need(0, 1)
    front = dot(weights_ref[0 : 2 * BLOCK, :], xs_ref[...], 1, 1)
    delta = dot(weights_ref[2 * BLOCK : 3 * BLOCK, :], gs_ref[...], 1, 1)
    gate = front[0:BLOCK]
    upper = front[BLOCK:]
    sig = jax.nn.sigmoid(gate)
    active = gate * sig
    dgate = (delta * upper * sig * (1.0 + gate * (1.0 - sig))).astype(BF16)
    dupper = (delta * active).astype(BF16)
    hidden = (active * upper).astype(BF16)
    for rep in range(REPS):
        rows = slice(rep * TOK, (rep + 1) * TOK)
        terms_ref[rep, 0:BLOCK, :] = dgate[:, rows]
        terms_ref[rep, BLOCK : 2 * BLOCK, :] = dupper[:, rows]
        terms_ref[rep, 2 * BLOCK : 3 * BLOCK, :] = hidden[:, rows]
    done(0)
    for target, which in ((keep_ref, core), (give_ref, 1 - core)):
        side = []
        for chip in range(4):
            cols = pl.ds(pl.multiple_of((2 * chip + which) * COLS, COLS), COLS)
            side.append(weights_ref[0 : 2 * BLOCK, cols])
        side = jnp.concatenate(side, axis=1)
        for rep in range(REPS):
            back = dot(terms_ref[rep, 0 : 2 * BLOCK, :], side, 0, 0)
            for chip in range(4):
                target[rep * 4 + chip] = back[:, chip * COLS : (chip + 1) * COLS]
    done(2, 3)
    peak = jnp.zeros((3 * BLOCK, COLS), F32)
    for rep in range(REPS):
        rows = slice(rep * TOK, (rep + 1) * TOK)
        for part in range(4):
            cols = slice(part * 256, (part + 1) * 256)
            grad_front = dot(terms_ref[rep, 0 : 2 * BLOCK, :], xs_ref[rows, cols], 1, 0)
            grad_down = dot(terms_ref[rep, 2 * BLOCK : 3 * BLOCK, :], gs_ref[rows, cols], 1, 0)
            grads = jnp.abs(jnp.concatenate([grad_front, grad_down], axis=0))
            peak = jnp.maximum(peak, jnp.maximum(grads[:, :COLS], grads[:, COLS:]))
    lane = lax.broadcasted_iota(jnp.int32, (1, COLS), 1)
    packed = jnp.zeros((1, COLS), F32)
    for group in range(9):
        top = jnp.max(peak[group * 16 : (group + 1) * 16], axis=0, keepdims=True)
        top = jnp.max(top, axis=1, keepdims=True)
        packed = jnp.where(lane == group, top, packed)
    peak_ref[...] = jnp.broadcast_to(packed.reshape(1, 1, COLS), peak_ref.shape)
    done(1)


def pair_kernel(pos_ref, keep_ref, got_ref, *back_refs):
    for step, back_ref in enumerate(back_refs):
        first = ((pos_ref[4] + step) % 4) * 4
        for chip in range(4):
            back_ref[chip] = keep_ref[first + chip] + got_ref[first + chip]


def plane_kernel(pos_ref, own_ref, up_ref, across_ref, down_ref, *back_refs):
    for step, back_ref in enumerate(back_refs):
        which = (pos_ref[5] + step) % 4
        back_ref[...] = (own_ref[which] + up_ref[which]) + (across_ref[which] + down_ref[which])


def quant_kernel(need, done, pos_ref, xs_ref, gs_ref, terms_ref, peaks_ref, bits_ref, row_ref, col_ref, out_ref, wide_ref):
    need(3, 4)
    spot = pos_ref[1]
    unit = pos_ref[2]
    depth = pos_ref[3]
    lane = lax.broadcasted_iota(jnp.int32, (1, COLS), 1)
    buck = lax.broadcasted_iota(jnp.int32, (1, 24), 1)
    tops = [jnp.max(peaks_ref[i * 16 : (i + 1) * 16], axis=0) for i in range(4)]
    scales = []
    for mat in range(3):
        per_bucket = []
        for bucket in range(3):
            held = jnp.zeros((1, COLS), F32)
            for sub in range(4 * bucket, 4 * bucket + 4):
                held = jnp.maximum(held, jnp.where(lane == mat * 3 + sub % 3, tops[sub // 3], 0.0))
            ranges = jnp.max(held, axis=1, keepdims=True)
            bits = jnp.where(buck == 3 * unit + bucket, bits_ref[mat : mat + 1, :].astype(F32), 0.0)
            bits = jnp.max(bits, axis=1, keepdims=True)
            levels = jnp.ones_like(bits)
            for count in range(3, 9):
                levels = jnp.where(bits == float(count), float(2 ** (count - 1) - 1), levels)
            per_bucket.append((ranges + RANGE_EPS) / levels)
        for sub in range(3):
            which = (3 * spot + sub) // 4
            chosen = jnp.where(which == 0, per_bucket[0], jnp.where(which == 1, per_bucket[1], per_bucket[2]))
            scales.append(jnp.broadcast_to(chosen, (16, COLS)))
    scale = jnp.concatenate(scales, axis=0)
    inverse = 1.0 / scale
    scale = scale * (1.0 / N_DP)
    need(0, 1, 2, 5, 6)
    row_part = row_ref[...]
    for part in range(4):
        cols = slice(part * 256, (part + 1) * 256)
        halves = [jnp.zeros((3 * BLOCK, COLS), F32) for _ in range(2)]
        for rep in range(REPS):
            rows = slice(rep * TOK, (rep + 1) * TOK)
            grad_front = dot(terms_ref[rep, 0 : 2 * BLOCK, :], xs_ref[rows, cols], 1, 0)
            grad_down = dot(terms_ref[rep, 2 * BLOCK : 3 * BLOCK, :], gs_ref[rows, cols], 1, 0)
            grads = jnp.concatenate([grad_front, grad_down], axis=0)
            offset = lax.rem(389 * (rep * 16 + depth), 1024).astype(F32) * (1.0 / 1024.0)
            for half in range(2):
                lanes = slice(half * COLS, (half + 1) * COLS)
                whole = slice(part * 256 + half * COLS, part * 256 + (half + 1) * COLS)
                ratio = grads[:, lanes] * inverse
                phase = row_part + (col_ref[0:1, whole] + offset)
                halves[half] = halves[half] + (ratio + turn(ratio + phase))
        for half in range(2):
            result = halves[half] * scale
            pair = 6 * SHARD * (2 * part + half)
            for mat in range(3):
                for low in range(2):
                    start = mat * BLOCK + low * SHARD
                    target = pair + (low * 3 + mat) * SHARD
                    wide_ref[target : target + SHARD, :] = result[start : start + SHARD]
            out_ref[pair : pair + 6 * SHARD, :] = wide_ref[pair : pair + 6 * SHARD, :].astype(BF16)
    done(0)


def adam_kernel(shares_ref, state_ref, new_state_ref, coded_ref, wide_ref, all_ref):
    all_ref[...] = shares_ref[...].astype(F32)
    mean_grad = all_ref[0 : 3 * SHARD]
    for peer in range(1, 16):
        mean_grad = mean_grad + all_ref[peer * 3 * SHARD : (peer + 1) * 3 * SHARD]
    mean_grad = mean_grad.reshape(3, SHARD, COLS)
    master = state_ref[0]
    first = BETA_ONE * state_ref[1] + (1.0 - BETA_ONE) * mean_grad
    second = BETA_TWO * state_ref[2] + (1.0 - BETA_TWO) * mean_grad * mean_grad
    updated = master - LEARN_RATE * (first / (jnp.sqrt(second) + ADAM_EPS) + WEIGHT_DECAY * master)
    new_state_ref[0] = updated
    new_state_ref[1] = first
    new_state_ref[2] = second
    spread_coded(eightbit_f32(updated), coded_ref, wide_ref)


def finish_kernel(ring_ref, own_ref, right_ref, across_ref, left_ref, spread_ref, grad_ref, sems):
    copies = [pltpu.make_async_copy(ring_ref, spread_ref.at[plane], sems.at[plane]) for plane in range(4)]
    for copy in copies:
        copy.start()
    grad_ref[...] = ((own_ref[...] + right_ref[...]) + (across_ref[...] + left_ref[...])).astype(BF16)
    for copy in copies:
        copy.wait()


def call(kernel, out_shape, smem=0, operands=(), scratch=(), limit=SMALL_LIMIT, first=None, idle=0):
    single = not isinstance(out_shape, tuple)
    outs = (out_shape,) if single else out_shape
    n_in = len(operands) - smem - idle
    n_out = len(outs)

    def body(*refs):
        small = refs[:smem]
        sources = refs[smem : smem + n_in]
        targets = refs[smem + n_in + idle : smem + n_in + idle + n_out]
        held = refs[smem + n_in + idle + n_out :]
        taken, made, rest, sems = held[:n_in], held[n_in : n_in + n_out], held[n_in + n_out : -1], held[-1]
        loads = [pltpu.make_async_copy(sources[i], taken[i], sems.at[i]) for i in range(n_in)]
        stores = [pltpu.make_async_copy(made[i], targets[i], sems.at[n_in + i]) for i in range(n_out)]
        if first is None:
            for load in loads:
                load.start()
            for load in loads:
                load.wait()
            kernel(*small, *taken, *made, *rest)
            for store in stores:
                store.start()
        else:
            for i in first:
                loads[i].start()

            def need(*which):
                for i in which:
                    loads[i].wait()

            def done(*which):
                for i in which:
                    stores[i].start()

            kernel(need, done, *small, *taken, *made, *rest)
        for store in stores:
            store.wait()

    anywhere = pl.BlockSpec(memory_space=pl.ANY)
    specs = [pl.BlockSpec(memory_space=pltpu.SMEM)] * smem + [anywhere] * (n_in + idle)
    buffers = [pltpu.VMEM(item.shape, item.dtype) for item in tuple(operands[smem : smem + n_in]) + outs]
    return pl.pallas_call(
        body,
        out_shape=out_shape,
        in_specs=specs,
        out_specs=anywhere if single else (anywhere,) * n_out,
        scratch_shapes=buffers + list(scratch) + [pltpu.SemaphoreType.DMA((n_in + n_out,))],
        compiler_params=pltpu.CompilerParams(vmem_limit_bytes=limit),
    )(*operands)


def struct(shape, dtype=F32):
    return jax.ShapeDtypeStruct(shape, dtype)


def shift(value, axes, step):
    return lax.ppermute(value, axes, [(i, (i + step) % 4) for i in range(4)])


def swap_pairs():
    pairs = []
    for z in range(16):
        for t in range(8):
            pairs.append((z * 8 + t, (2 * t + z % 2) * 8 + z // 2))
    return pairs


def on_device(acts, grad_out, master, moment_one, moment_two, bit_widths, row_dither, col_dither):
    y = lax.axis_index("y")
    z = lax.axis_index(Z)
    core = lax.axis_index("c")
    tensor = lax.axis_index(TENSOR)
    spot = tensor % 4
    unit = 2 * y + tensor // 4
    pos = jnp.stack([core, spot, unit, z, y, tensor // 2]).astype(jnp.int32)
    pairs = swap_pairs()

    packed, state = pl.pallas_call(
        pack_kernel,
        out_shape=(struct((16, PACK, COLS), BF16), struct((3, 3, SHARD, COLS))),
        in_specs=[pl.BlockSpec(memory_space=pl.ANY)] * 6,
        out_specs=(pl.BlockSpec(memory_space=pl.ANY),) * 2,
        scratch_shapes=[
            pltpu.VMEM((PACK, COLS), BF16),
            pltpu.VMEM((1, COLS), jnp.int32),
            pltpu.SemaphoreType.DMA((22,)),
        ],
        compiler_params=pltpu.CompilerParams(vmem_limit_bytes=LARGE_LIMIT),
    )(acts, grad_out, col_dither[None], master, moment_one, moment_two)
    state = lax.ppermute(state, Z + TENSOR, pairs)
    wide = (pltpu.VMEM((6 * SHARD, COLS), F32),)
    coded = call(code_kernel, struct((48 * SHARD, COLS), BF16), 0, (state,), wide)
    rows = lax.all_to_all(coded.reshape(16, 3 * SHARD, COLS), Z, 0, 0).reshape(48 * SHARD, COLS)
    own = lax.all_to_all(packed, ("y", "xh", "xl"), 0, 0)
    other = lax.ppermute(own, "c", [(0, 1), (1, 0)])

    row_part = lax.dynamic_slice(row_dither, (0, BLOCK * (8 * y + tensor)), (3, BLOCK))
    row_part = jnp.broadcast_to(row_part.astype(F32).reshape(3 * BLOCK, 1) * (1.0 / 1024.0), (3 * BLOCK, COLS))

    xs, gs, col_part = call(
        layout_kernel,
        (struct((REPS * TOK, 1024), BF16), struct((REPS * TOK, 1024), BF16), struct((8, 1024))),
        1,
        (pos, own, other, row_part),
        limit=LARGE_LIMIT,
        idle=1,
    )
    terms, peak, keep, give = call(
        front_kernel,
        (
            struct((REPS, 3 * BLOCK, TOK), BF16),
            struct((64, 1, COLS)),
            struct((16, TOK, COLS)),
            struct((16, TOK, COLS)),
        ),
        1,
        (pos, xs, gs, rows),
        (
            pltpu.VMEM((48 * SHARD, COLS), F32),
            pltpu.VMEM((3 * BLOCK, 1024), F32),
            pltpu.VMEM((3 * BLOCK, 1024), BF16),
        ),
        limit=LARGE_LIMIT,
        first=(2, 0, 1),
    )
    peaks = lax.all_to_all(peak, ("xl", "c") + Z, 0, 0)
    got = lax.ppermute(give, "c", [(0, 1), (1, 0)])
    back = call(pair_kernel, (struct((4, TOK, COLS)),) * 4, 1, (pos, keep, got))

    shares = call(
        quant_kernel,
        struct((48 * SHARD, COLS), BF16),
        1,
        (pos, xs, gs, terms, peaks, bit_widths, row_part, col_part, back[0]),
        (pltpu.VMEM((48 * SHARD, COLS), F32),),
        limit=LARGE_LIMIT,
        first=(3, 4, 2, 0, 1, 5, 6),
        idle=1,
    )
    back = [back[0]] + [shift(back[step], "y", step) for step in (1, 2, 3)]
    shares = lax.all_to_all(shares.reshape(16, 3 * SHARD, COLS), Z, 0, 0).reshape(48 * SHARD, COLS)

    new_state, ring = call(
        adam_kernel,
        (struct((3, 3, SHARD, COLS)), struct((48 * SHARD, COLS), BF16)),
        0,
        (shares, state, *back[1:]),
        wide + (pltpu.VMEM((48 * SHARD, COLS), F32),),
        idle=3,
    )
    back = call(plane_kernel, (struct((TOK, COLS)),) * 4, 1, (pos, *back))
    back = [back[0]] + [shift(back[step], ("xh", "xl"), step) for step in (1, 2, 3)]
    ring = lax.all_to_all(ring.reshape(16, 3 * SHARD, COLS), Z, 0, 0).reshape(48 * SHARD, COLS)
    anywhere = pl.BlockSpec(memory_space=pl.ANY)
    local = pl.BlockSpec(memory_space=pltpu.VMEM)
    ring, grad_in = pl.pallas_call(
        finish_kernel,
        out_shape=(struct((4, 48 * SHARD, COLS), BF16), struct((TOK, COLS), BF16)),
        in_specs=[anywhere] + [local] * 4,
        out_specs=(anywhere, local),
        scratch_shapes=[pltpu.SemaphoreType.DMA((4,))],
        compiler_params=pltpu.CompilerParams(vmem_limit_bytes=SMALL_LIMIT),
    )(ring, *back)
    new_state = lax.ppermute(new_state, Z + TENSOR, pairs)
    ring = lax.all_to_all(ring.reshape(32, 6 * SHARD, COLS), ("y",) + TENSOR, 0, 0)
    new_weights = ring.reshape(32, 2, 3, SHARD, COLS).transpose(2, 0, 1, 3, 4).reshape(3, 64 * SHARD, COLS)
    return (grad_in, new_state[0], new_state[1], new_state[2], new_weights)


def solution(mesh):
    grid = Mesh(mesh.devices.reshape(SIZES), DP + TENSOR)
    return jax.shard_map(
        on_device,
        mesh=grid,
        in_specs=(
            P(DP, TENSOR),
            P(DP, TENSOR),
            P(None, DP, TENSOR),
            P(None, DP, TENSOR),
            P(None, DP, TENSOR),
            P(),
            P(),
            P(TENSOR),
        ),
        out_specs=(
            P(DP, TENSOR),
            P(None, DP, TENSOR),
            P(None, DP, TENSOR),
            P(None, DP, TENSOR),
            P(None, None, TENSOR),
        ),
        check_vma=False,
    )
```

```python
import jax
import jax.numpy as jnp
from jax import lax
from jax.experimental import pallas as pl
from jax.experimental.pallas import tpu as pltpu
from jax.sharding import Mesh, PartitionSpec as P

F32 = jnp.float32
BF16 = jnp.bfloat16

TOK = 128
BROWS = 64
COLS = 128
SHARD = 24
BLOCK = 48
PACK = 2 * TOK + 16
REPS = 4

BETA_ONE = 0.9
BETA_TWO = 0.95
LEARN_RATE = 0.004
WEIGHT_DECAY = 0.1
ADAM_EPS = 1e-08
RANGE_EPS = 1e-06
N_DP = 64

SINE = (
    0.9999995827674866,
    -6.579691410064697,
    12.986435890197754,
    -12.188101768493652,
    6.558042526245117,
    -1.95303213596344,
)

Z = ("zh", "zl")
DP = ("y",) + Z
TENSOR = ("xh", "xl", "c")
SIZES = (4, 4, 4, 2, 2, 2)

SMALL_LIMIT = 20 * 1024 * 1024
LARGE_LIMIT = 60 * 1024 * 1024


def turn(value):
    frac = value - jnp.floor(value + 0.5)
    square = frac * frac
    total = jnp.full_like(square, SINE[-1])
    for coef in SINE[-2::-1]:
        total = total * square + coef
    return total * frac


def soft_round(value):
    return value - turn(value)


def eightbit_f32(weights):
    scale = (jnp.max(jnp.abs(weights), axis=-1, keepdims=True) + RANGE_EPS) / 127.0
    return soft_round(weights / scale) * scale


def dot(left, right, left_dim, right_dim):
    return lax.dot_general(
        left, right, (((left_dim,), (right_dim,)), ((), ())), preferred_element_type=F32
    )


def spread_coded(coded, coded_ref, wide_ref):
    for mat in range(6):
        wide_ref[mat * SHARD : (mat + 1) * SHARD, :] = coded[mat % 3]
    narrow = wide_ref[...].astype(BF16)
    for pair in range(8):
        coded_ref[pair * 6 * SHARD : (pair + 1) * 6 * SHARD, :] = narrow


def pack_kernel(acts_ref, grad_ref, dither_ref, master_ref, one_ref, two_ref, packed_ref, state_ref):
    high = (dither_ref[...] >> 3).astype(F32)
    low = (dither_ref[...] & 7).astype(F32)
    row = lax.broadcasted_iota(jnp.int32, (16, COLS), 0)
    extra = jnp.where(row == 0, high, jnp.where(row == 1, low, 0.0)).astype(BF16)
    for peer in range(16):
        packed_ref[peer, 0:TOK, :] = acts_ref[...]
        packed_ref[peer, TOK : 2 * TOK, :] = grad_ref[...]
        packed_ref[peer, 2 * TOK : PACK, :] = extra
    state_ref[0] = master_ref[...]
    state_ref[1] = one_ref[...]
    state_ref[2] = two_ref[...]


def code_kernel(state_ref, coded_ref, wide_ref):
    spread_coded(eightbit_f32(state_ref[0]), coded_ref, wide_ref)


def layout_kernel(pos_ref, own_ref, other_ref, xs_ref, gs_ref, col_ref):
    core = pos_ref[0]
    for source, which in ((own_ref, core), (other_ref, 1 - core)):
        for chip in range(4):
            cols = pl.ds(pl.multiple_of((2 * chip + which) * COLS, COLS), COLS)
            for rep in range(REPS):
                rows = slice(rep * TOK, (rep + 1) * TOK)
                xs_ref[rows, cols] = source[rep * 4 + chip, 0:TOK, :]
                gs_ref[rows, cols] = source[rep * 4 + chip, TOK : 2 * TOK, :]
            pair = source[chip, 2 * TOK : PACK, :].astype(F32)
            dither = pair[0:1] * 8.0 + pair[1:2]
            col_ref[:, cols] = jnp.broadcast_to(dither * (1.0 / 1024.0), (8, COLS))


def front_kernel(need, done, pos_ref, *refs):
    xs_ref, gs_ref, rows_ref, terms_ref, peak_ref, keep_ref, give_ref, wide_ref, full_ref, weights_ref = refs
    core = pos_ref[0]
    need(2)
    wide_ref[...] = rows_ref[...].astype(F32)
    for depth in range(16):
        cols = slice((depth // 2) * COLS, (depth // 2 + 1) * COLS)
        for mat in range(3):
            source = (depth * 3 + mat) * SHARD
            target = mat * BLOCK + (depth % 2) * SHARD
            full_ref[target : target + SHARD, cols] = wide_ref[source : source + SHARD, :]
    weights_ref[...] = full_ref[...].astype(BF16)
    need(0, 1)
    front = dot(weights_ref[0 : 2 * BLOCK, :], xs_ref[...], 1, 1)
    delta = dot(weights_ref[2 * BLOCK : 3 * BLOCK, :], gs_ref[...], 1, 1)
    gate = front[0:BLOCK]
    upper = front[BLOCK:]
    sig = jax.nn.sigmoid(gate)
    active = gate * sig
    dgate = (delta * upper * sig * (1.0 + gate * (1.0 - sig))).astype(BF16)
    dupper = (delta * active).astype(BF16)
    hidden = (active * upper).astype(BF16)
    for rep in range(REPS):
        rows = slice(rep * TOK, (rep + 1) * TOK)
        terms_ref[rep, 0:BLOCK, :] = dgate[:, rows]
        terms_ref[rep, BLOCK : 2 * BLOCK, :] = dupper[:, rows]
        terms_ref[rep, 2 * BLOCK : 3 * BLOCK, :] = hidden[:, rows]
    done(0)
    for target, which in ((keep_ref, core), (give_ref, 1 - core)):
        side = []
        for chip in range(4):
            cols = pl.ds(pl.multiple_of((2 * chip + which) * COLS, COLS), COLS)
            side.append(weights_ref[0 : 2 * BLOCK, cols])
        side = jnp.concatenate(side, axis=1)
        for rep in range(REPS):
            back = dot(terms_ref[rep, 0 : 2 * BLOCK, :], side, 0, 0)
            for chip in range(4):
                target[rep * 4 + chip] = back[:, chip * COLS : (chip + 1) * COLS]
    done(2, 3)
    peak = jnp.zeros((3 * BLOCK, COLS), F32)
    for rep in range(REPS):
        rows = slice(rep * TOK, (rep + 1) * TOK)
        for part in range(4):
            cols = slice(part * 256, (part + 1) * 256)
            grad_front = dot(terms_ref[rep, 0 : 2 * BLOCK, :], xs_ref[rows, cols], 1, 0)
            grad_down = dot(terms_ref[rep, 2 * BLOCK : 3 * BLOCK, :], gs_ref[rows, cols], 1, 0)
            grads = jnp.abs(jnp.concatenate([grad_front, grad_down], axis=0))
            peak = jnp.maximum(peak, jnp.maximum(grads[:, :COLS], grads[:, COLS:]))
    lane = lax.broadcasted_iota(jnp.int32, (1, COLS), 1)
    packed = jnp.zeros((1, COLS), F32)
    for group in range(9):
        top = jnp.max(peak[group * 16 : (group + 1) * 16], axis=0, keepdims=True)
        top = jnp.max(top, axis=1, keepdims=True)
        packed = jnp.where(lane == group, top, packed)
    peak_ref[...] = jnp.broadcast_to(packed.reshape(1, 1, COLS), peak_ref.shape)
    done(1)


def pair_kernel(pos_ref, keep_ref, got_ref, *back_refs):
    for step, back_ref in enumerate(back_refs):
        first = ((pos_ref[4] + step) % 4) * 4
        for chip in range(4):
            back_ref[chip] = keep_ref[first + chip] + got_ref[first + chip]


def plane_kernel(pos_ref, own_ref, up_ref, across_ref, down_ref, *back_refs):
    for step, back_ref in enumerate(back_refs):
        which = (pos_ref[5] + step) % 4
        back_ref[...] = (own_ref[which] + up_ref[which]) + (across_ref[which] + down_ref[which])


def quant_kernel(need, done, pos_ref, xs_ref, gs_ref, terms_ref, peaks_ref, bits_ref, row_ref, col_ref, out_ref, wide_ref):
    need(3, 4)
    spot = pos_ref[1]
    unit = pos_ref[2]
    depth = pos_ref[3]
    lane = lax.broadcasted_iota(jnp.int32, (1, COLS), 1)
    buck = lax.broadcasted_iota(jnp.int32, (1, 24), 1)
    tops = [jnp.max(peaks_ref[i * 16 : (i + 1) * 16], axis=0) for i in range(4)]
    scales = []
    for mat in range(3):
        per_bucket = []
        for bucket in range(3):
            held = jnp.zeros((1, COLS), F32)
            for sub in range(4 * bucket, 4 * bucket + 4):
                held = jnp.maximum(held, jnp.where(lane == mat * 3 + sub % 3, tops[sub // 3], 0.0))
            ranges = jnp.max(held, axis=1, keepdims=True)
            bits = jnp.where(buck == 3 * unit + bucket, bits_ref[mat : mat + 1, :].astype(F32), 0.0)
            bits = jnp.max(bits, axis=1, keepdims=True)
            levels = jnp.ones_like(bits)
            for count in range(3, 9):
                levels = jnp.where(bits == float(count), float(2 ** (count - 1) - 1), levels)
            per_bucket.append((ranges + RANGE_EPS) / levels)
        for sub in range(3):
            which = (3 * spot + sub) // 4
            chosen = jnp.where(which == 0, per_bucket[0], jnp.where(which == 1, per_bucket[1], per_bucket[2]))
            scales.append(jnp.broadcast_to(chosen, (16, COLS)))
    scale = jnp.concatenate(scales, axis=0)
    inverse = 1.0 / scale
    scale = scale * (1.0 / N_DP)
    need(0, 1, 2, 5, 6)
    row_part = row_ref[...]
    for part in range(4):
        cols = slice(part * 256, (part + 1) * 256)
        halves = [jnp.zeros((3 * BLOCK, COLS), F32) for _ in range(2)]
        for rep in range(REPS):
            rows = slice(rep * TOK, (rep + 1) * TOK)
            grad_front = dot(terms_ref[rep, 0 : 2 * BLOCK, :], xs_ref[rows, cols], 1, 0)
            grad_down = dot(terms_ref[rep, 2 * BLOCK : 3 * BLOCK, :], gs_ref[rows, cols], 1, 0)
            grads = jnp.concatenate([grad_front, grad_down], axis=0)
            offset = lax.rem(389 * (rep * 16 + depth), 1024).astype(F32) * (1.0 / 1024.0)
            for half in range(2):
                lanes = slice(half * COLS, (half + 1) * COLS)
                whole = slice(part * 256 + half * COLS, part * 256 + (half + 1) * COLS)
                ratio = grads[:, lanes] * inverse
                phase = row_part + (col_ref[0:1, whole] + offset)
                halves[half] = halves[half] + (ratio + turn(ratio + phase))
        for half in range(2):
            result = halves[half] * scale
            pair = 6 * SHARD * (2 * part + half)
            for mat in range(3):
                for low in range(2):
                    start = mat * BLOCK + low * SHARD
                    target = pair + (low * 3 + mat) * SHARD
                    wide_ref[target : target + SHARD, :] = result[start : start + SHARD]
            out_ref[pair : pair + 6 * SHARD, :] = wide_ref[pair : pair + 6 * SHARD, :].astype(BF16)
    done(0)


def adam_kernel(shares_ref, state_ref, new_state_ref, coded_ref, wide_ref, all_ref):
    all_ref[...] = shares_ref[...].astype(F32)
    mean_grad = all_ref[0 : 3 * SHARD]
    for peer in range(1, 16):
        mean_grad = mean_grad + all_ref[peer * 3 * SHARD : (peer + 1) * 3 * SHARD]
    mean_grad = mean_grad.reshape(3, SHARD, COLS)
    master = state_ref[0]
    first = BETA_ONE * state_ref[1] + (1.0 - BETA_ONE) * mean_grad
    second = BETA_TWO * state_ref[2] + (1.0 - BETA_TWO) * mean_grad * mean_grad
    updated = master - LEARN_RATE * (first / (jnp.sqrt(second) + ADAM_EPS) + WEIGHT_DECAY * master)
    new_state_ref[0] = updated
    new_state_ref[1] = first
    new_state_ref[2] = second
    spread_coded(eightbit_f32(updated), coded_ref, wide_ref)


def finish_kernel(ring_ref, own_ref, right_ref, across_ref, left_ref, spread_ref, grad_ref, sems):
    copies = [pltpu.make_async_copy(ring_ref, spread_ref.at[plane], sems.at[plane]) for plane in range(4)]
    for copy in copies:
        copy.start()
    grad_ref[...] = ((own_ref[...] + right_ref[...]) + (across_ref[...] + left_ref[...])).astype(BF16)
    for copy in copies:
        copy.wait()


def call(kernel, out_shape, smem=0, operands=(), scratch=(), limit=SMALL_LIMIT, first=None, idle=0):
    single = not isinstance(out_shape, tuple)
    outs = (out_shape,) if single else out_shape
    n_in = len(operands) - smem - idle
    n_out = len(outs)

    def body(*refs):
        small = refs[:smem]
        sources = refs[smem : smem + n_in]
        targets = refs[smem + n_in + idle : smem + n_in + idle + n_out]
        held = refs[smem + n_in + idle + n_out :]
        taken, made, rest, sems = held[:n_in], held[n_in : n_in + n_out], held[n_in + n_out : -1], held[-1]
        loads = [pltpu.make_async_copy(sources[i], taken[i], sems.at[i]) for i in range(n_in)]
        stores = [pltpu.make_async_copy(made[i], targets[i], sems.at[n_in + i]) for i in range(n_out)]
        if first is None:
            for load in loads:
                load.start()
            for load in loads:
                load.wait()
            kernel(*small, *taken, *made, *rest)
            for store in stores:
                store.start()
        else:
            for i in first:
                loads[i].start()

            def need(*which):
                for i in which:
                    loads[i].wait()

            def done(*which):
                for i in which:
                    stores[i].start()

            kernel(need, done, *small, *taken, *made, *rest)
        for store in stores:
            store.wait()

    anywhere = pl.BlockSpec(memory_space=pl.ANY)
    specs = [pl.BlockSpec(memory_space=pltpu.SMEM)] * smem + [anywhere] * (n_in + idle)
    buffers = [pltpu.VMEM(item.shape, item.dtype) for item in tuple(operands[smem : smem + n_in]) + outs]
    return pl.pallas_call(
        body,
        out_shape=out_shape,
        in_specs=specs,
        out_specs=anywhere if single else (anywhere,) * n_out,
        scratch_shapes=buffers + list(scratch) + [pltpu.SemaphoreType.DMA((n_in + n_out,))],
        compiler_params=pltpu.CompilerParams(vmem_limit_bytes=limit),
    )(*operands)


def struct(shape, dtype=F32):
    return jax.ShapeDtypeStruct(shape, dtype)


def shift(value, axes, step):
    return lax.ppermute(value, axes, [(i, (i + step) % 4) for i in range(4)])


def swap_pairs():
    pairs = []
    for z in range(16):
        for t in range(8):
            pairs.append((z * 8 + t, (2 * t + z % 2) * 8 + z // 2))
    return pairs


def on_device(acts, grad_out, master, moment_one, moment_two, bit_widths, row_dither, col_dither):
    y = lax.axis_index("y")
    z = lax.axis_index(Z)
    core = lax.axis_index("c")
    tensor = lax.axis_index(TENSOR)
    spot = tensor % 4
    unit = 2 * y + tensor // 4
    pos = jnp.stack([core, spot, unit, z, y, tensor // 2]).astype(jnp.int32)
    pairs = swap_pairs()

    packed, state = call(
        pack_kernel,
        (struct((16, PACK, COLS), BF16), struct((3, 3, SHARD, COLS))),
        0,
        (acts, grad_out, col_dither[None], master, moment_one, moment_two),
        limit=LARGE_LIMIT,
    )
    state = lax.ppermute(state, Z + TENSOR, pairs)
    wide = (pltpu.VMEM((6 * SHARD, COLS), F32),)
    coded = call(code_kernel, struct((48 * SHARD, COLS), BF16), 0, (state,), wide)
    rows = lax.all_to_all(coded.reshape(16, 3 * SHARD, COLS), Z, 0, 0).reshape(48 * SHARD, COLS)
    own = lax.all_to_all(packed, ("y", "xh", "xl"), 0, 0)
    other = lax.ppermute(own, "c", [(0, 1), (1, 0)])

    row_part = lax.dynamic_slice(row_dither, (0, BLOCK * (8 * y + tensor)), (3, BLOCK))
    row_part = jnp.broadcast_to(row_part.astype(F32).reshape(3 * BLOCK, 1) * (1.0 / 1024.0), (3 * BLOCK, COLS))

    xs, gs, col_part = call(
        layout_kernel,
        (struct((REPS * TOK, 1024), BF16), struct((REPS * TOK, 1024), BF16), struct((8, 1024))),
        1,
        (pos, own, other, row_part),
        limit=LARGE_LIMIT,
        idle=1,
    )
    terms, peak, keep, give = call(
        front_kernel,
        (
            struct((REPS, 3 * BLOCK, TOK), BF16),
            struct((64, 1, COLS)),
            struct((16, TOK, COLS)),
            struct((16, TOK, COLS)),
        ),
        1,
        (pos, xs, gs, rows),
        (
            pltpu.VMEM((48 * SHARD, COLS), F32),
            pltpu.VMEM((3 * BLOCK, 1024), F32),
            pltpu.VMEM((3 * BLOCK, 1024), BF16),
        ),
        limit=LARGE_LIMIT,
        first=(2, 0, 1),
    )
    peaks = lax.all_to_all(peak, ("xl", "c") + Z, 0, 0)
    got = lax.ppermute(give, "c", [(0, 1), (1, 0)])
    back = call(pair_kernel, (struct((4, TOK, COLS)),) * 4, 1, (pos, keep, got))

    shares = call(
        quant_kernel,
        struct((48 * SHARD, COLS), BF16),
        1,
        (pos, xs, gs, terms, peaks, bit_widths, row_part, col_part, back[0]),
        (pltpu.VMEM((48 * SHARD, COLS), F32),),
        limit=LARGE_LIMIT,
        first=(3, 4, 2, 0, 1, 5, 6),
        idle=1,
    )
    back = [back[0]] + [shift(back[step], "y", step) for step in (1, 2, 3)]
    shares = lax.all_to_all(shares.reshape(16, 3 * SHARD, COLS), Z, 0, 0).reshape(48 * SHARD, COLS)

    new_state, ring = call(
        adam_kernel,
        (struct((3, 3, SHARD, COLS)), struct((48 * SHARD, COLS), BF16)),
        0,
        (shares, state, *back[1:]),
        wide + (pltpu.VMEM((48 * SHARD, COLS), F32),),
        idle=3,
    )
    back = call(plane_kernel, (struct((TOK, COLS)),) * 4, 1, (pos, *back))
    back = [back[0]] + [shift(back[step], ("xh", "xl"), step) for step in (1, 2, 3)]
    ring = lax.all_to_all(ring.reshape(16, 3 * SHARD, COLS), Z, 0, 0).reshape(48 * SHARD, COLS)
    anywhere = pl.BlockSpec(memory_space=pl.ANY)
    local = pl.BlockSpec(memory_space=pltpu.VMEM)
    ring, grad_in = pl.pallas_call(
        finish_kernel,
        out_shape=(struct((4, 48 * SHARD, COLS), BF16), struct((TOK, COLS), BF16)),
        in_specs=[anywhere] + [local] * 4,
        out_specs=(anywhere, local),
        scratch_shapes=[pltpu.SemaphoreType.DMA((4,))],
        compiler_params=pltpu.CompilerParams(vmem_limit_bytes=SMALL_LIMIT),
    )(ring, *back)
    new_state = lax.ppermute(new_state, Z + TENSOR, pairs)
    ring = lax.all_to_all(ring.reshape(32, 6 * SHARD, COLS), ("y",) + TENSOR, 0, 0)
    new_weights = ring.reshape(32, 2, 3, SHARD, COLS).transpose(2, 0, 1, 3, 4).reshape(3, 64 * SHARD, COLS)
    return (grad_in, new_state[0], new_state[1], new_state[2], new_weights)


def solution(mesh):
    grid = Mesh(mesh.devices.reshape(SIZES), DP + TENSOR)
    return jax.shard_map(
        on_device,
        mesh=grid,
        in_specs=(
            P(DP, TENSOR),
            P(DP, TENSOR),
            P(None, DP, TENSOR),
            P(None, DP, TENSOR),
            P(None, DP, TENSOR),
            P(),
            P(),
            P(TENSOR),
        ),
        out_specs=(
            P(DP, TENSOR),
            P(None, DP, TENSOR),
            P(None, DP, TENSOR),
            P(None, DP, TENSOR),
            P(None, None, TENSOR),
        ),
        check_vma=False,
    )
```

```python
import jax
import jax.numpy as jnp
from jax import lax
from jax.experimental import pallas as pl
from jax.experimental.pallas import tpu as pltpu
from jax.sharding import Mesh, PartitionSpec as P

F32 = jnp.float32
BF16 = jnp.bfloat16

TOK = 128
BROWS = 64
COLS = 128
SHARD = 24
BLOCK = 48
PACK = 2 * TOK + 16
REPS = 4

BETA_ONE = 0.9
BETA_TWO = 0.95
LEARN_RATE = 0.004
WEIGHT_DECAY = 0.1
ADAM_EPS = 1e-08
RANGE_EPS = 1e-06
N_DP = 64

SINE = (
    0.9999995827674866,
    -6.579691410064697,
    12.986435890197754,
    -12.188101768493652,
    6.558042526245117,
    -1.95303213596344,
)

Z = ("zh", "zl")
DP = ("y",) + Z
TENSOR = ("xh", "xl", "c")
SIZES = (4, 4, 4, 2, 2, 2)

SMALL_LIMIT = 20 * 1024 * 1024
LARGE_LIMIT = 60 * 1024 * 1024


def turn(value):
    frac = value - jnp.floor(value + 0.5)
    square = frac * frac
    total = jnp.full_like(square, SINE[-1])
    for coef in SINE[-2::-1]:
        total = total * square + coef
    return total * frac


def soft_round(value):
    return value - turn(value)


def eightbit_f32(weights):
    scale = (jnp.max(jnp.abs(weights), axis=-1, keepdims=True) + RANGE_EPS) / 127.0
    return soft_round(weights / scale) * scale


def dot(left, right, left_dim, right_dim):
    return lax.dot_general(
        left, right, (((left_dim,), (right_dim,)), ((), ())), preferred_element_type=F32
    )


def spread_coded(coded, coded_ref, wide_ref):
    for mat in range(6):
        wide_ref[mat * SHARD : (mat + 1) * SHARD, :] = coded[mat % 3]
    narrow = wide_ref[...].astype(BF16)
    for pair in range(8):
        coded_ref[pair * 6 * SHARD : (pair + 1) * 6 * SHARD, :] = narrow


def pack_kernel(acts_ref, grad_ref, dither_ref, master_ref, one_ref, two_ref, packed_ref, state_ref):
    high = (dither_ref[...] >> 3).astype(F32)
    low = (dither_ref[...] & 7).astype(F32)
    row = lax.broadcasted_iota(jnp.int32, (16, COLS), 0)
    extra = jnp.where(row == 0, high, jnp.where(row == 1, low, 0.0)).astype(BF16)
    for peer in range(16):
        packed_ref[peer, 0:TOK, :] = acts_ref[...]
        packed_ref[peer, TOK : 2 * TOK, :] = grad_ref[...]
        packed_ref[peer, 2 * TOK : PACK, :] = extra
    state_ref[0] = master_ref[...]
    state_ref[1] = one_ref[...]
    state_ref[2] = two_ref[...]


def code_kernel(state_ref, coded_ref, wide_ref):
    spread_coded(eightbit_f32(state_ref[0]), coded_ref, wide_ref)


def layout_kernel(pos_ref, own_ref, other_ref, xs_ref, gs_ref, col_ref):
    core = pos_ref[0]
    for source, which in ((own_ref, core), (other_ref, 1 - core)):
        for chip in range(4):
            cols = pl.ds(pl.multiple_of((2 * chip + which) * COLS, COLS), COLS)
            for rep in range(REPS):
                rows = slice(rep * TOK, (rep + 1) * TOK)
                xs_ref[rows, cols] = source[rep * 4 + chip, 0:TOK, :]
                gs_ref[rows, cols] = source[rep * 4 + chip, TOK : 2 * TOK, :]
            pair = source[chip, 2 * TOK : PACK, :].astype(F32)
            dither = pair[0:1] * 8.0 + pair[1:2]
            col_ref[:, cols] = jnp.broadcast_to(dither * (1.0 / 1024.0), (8, COLS))


def front_kernel(need, done, pos_ref, *refs):
    xs_ref, gs_ref, rows_ref, terms_ref, peak_ref, keep_ref, give_ref, wide_ref, full_ref, weights_ref = refs
    core = pos_ref[0]
    wide_ref[...] = rows_ref[...].astype(F32)
    for depth in range(16):
        cols = slice((depth // 2) * COLS, (depth // 2 + 1) * COLS)
        for mat in range(3):
            source = (depth * 3 + mat) * SHARD
            target = mat * BLOCK + (depth % 2) * SHARD
            full_ref[target : target + SHARD, cols] = wide_ref[source : source + SHARD, :]
    weights_ref[...] = full_ref[...].astype(BF16)
    need(0, 1)
    front = dot(weights_ref[0 : 2 * BLOCK, :], xs_ref[...], 1, 1)
    delta = dot(weights_ref[2 * BLOCK : 3 * BLOCK, :], gs_ref[...], 1, 1)
    gate = front[0:BLOCK]
    upper = front[BLOCK:]
    sig = jax.nn.sigmoid(gate)
    active = gate * sig
    dgate = (delta * upper * sig * (1.0 + gate * (1.0 - sig))).astype(BF16)
    dupper = (delta * active).astype(BF16)
    hidden = (active * upper).astype(BF16)
    for rep in range(REPS):
        rows = slice(rep * TOK, (rep + 1) * TOK)
        terms_ref[rep, 0:BLOCK, :] = dgate[:, rows]
        terms_ref[rep, BLOCK : 2 * BLOCK, :] = dupper[:, rows]
        terms_ref[rep, 2 * BLOCK : 3 * BLOCK, :] = hidden[:, rows]
    done(0)
    for target, which in ((keep_ref, core), (give_ref, 1 - core)):
        side = []
        for chip in range(4):
            cols = pl.ds(pl.multiple_of((2 * chip + which) * COLS, COLS), COLS)
            side.append(weights_ref[0 : 2 * BLOCK, cols])
        side = jnp.concatenate(side, axis=1)
        for rep in range(REPS):
            back = dot(terms_ref[rep, 0 : 2 * BLOCK, :], side, 0, 0)
            for chip in range(4):
                target[rep * 4 + chip] = back[:, chip * COLS : (chip + 1) * COLS]
    done(2, 3)
    peak = jnp.zeros((3 * BLOCK, COLS), F32)
    for rep in range(REPS):
        rows = slice(rep * TOK, (rep + 1) * TOK)
        for part in range(4):
            cols = slice(part * 256, (part + 1) * 256)
            grad_front = dot(terms_ref[rep, 0 : 2 * BLOCK, :], xs_ref[rows, cols], 1, 0)
            grad_down = dot(terms_ref[rep, 2 * BLOCK : 3 * BLOCK, :], gs_ref[rows, cols], 1, 0)
            grads = jnp.abs(jnp.concatenate([grad_front, grad_down], axis=0))
            peak = jnp.maximum(peak, jnp.maximum(grads[:, :COLS], grads[:, COLS:]))
    lane = lax.broadcasted_iota(jnp.int32, (1, COLS), 1)
    packed = jnp.zeros((1, COLS), F32)
    for group in range(9):
        top = jnp.max(peak[group * 16 : (group + 1) * 16], axis=0, keepdims=True)
        top = jnp.max(top, axis=1, keepdims=True)
        packed = jnp.where(lane == group, top, packed)
    peak_ref[...] = jnp.broadcast_to(packed.reshape(1, 1, COLS), peak_ref.shape)
    done(1)


def pair_kernel(pos_ref, keep_ref, got_ref, *back_refs):
    for step, back_ref in enumerate(back_refs):
        first = ((pos_ref[4] + step) % 4) * 4
        for chip in range(4):
            back_ref[chip] = keep_ref[first + chip] + got_ref[first + chip]


def plane_kernel(pos_ref, own_ref, up_ref, across_ref, down_ref, *back_refs):
    for step, back_ref in enumerate(back_refs):
        which = (pos_ref[5] + step) % 4
        back_ref[...] = (own_ref[which] + up_ref[which]) + (across_ref[which] + down_ref[which])


def quant_kernel(need, done, pos_ref, xs_ref, gs_ref, terms_ref, peaks_ref, bits_ref, row_ref, col_ref, out_ref, wide_ref):
    need(4)
    spot = pos_ref[1]
    unit = pos_ref[2]
    depth = pos_ref[3]
    lane = lax.broadcasted_iota(jnp.int32, (1, COLS), 1)
    buck = lax.broadcasted_iota(jnp.int32, (1, 24), 1)
    tops = [jnp.max(peaks_ref[i * 16 : (i + 1) * 16], axis=0) for i in range(4)]
    scales = []
    for mat in range(3):
        per_bucket = []
        for bucket in range(3):
            held = jnp.zeros((1, COLS), F32)
            for sub in range(4 * bucket, 4 * bucket + 4):
                held = jnp.maximum(held, jnp.where(lane == mat * 3 + sub % 3, tops[sub // 3], 0.0))
            ranges = jnp.max(held, axis=1, keepdims=True)
            bits = jnp.where(buck == 3 * unit + bucket, bits_ref[mat : mat + 1, :].astype(F32), 0.0)
            bits = jnp.max(bits, axis=1, keepdims=True)
            levels = jnp.ones_like(bits)
            for count in range(3, 9):
                levels = jnp.where(bits == float(count), float(2 ** (count - 1) - 1), levels)
            per_bucket.append((ranges + RANGE_EPS) / levels)
        for sub in range(3):
            which = (3 * spot + sub) // 4
            chosen = jnp.where(which == 0, per_bucket[0], jnp.where(which == 1, per_bucket[1], per_bucket[2]))
            scales.append(jnp.broadcast_to(chosen, (16, COLS)))
    scale = jnp.concatenate(scales, axis=0)
    inverse = 1.0 / scale
    scale = scale * (1.0 / N_DP)
    need(0, 1, 2, 5, 6)
    row_part = row_ref[...]
    for part in range(4):
        cols = slice(part * 256, (part + 1) * 256)
        halves = [jnp.zeros((3 * BLOCK, COLS), F32) for _ in range(2)]
        for rep in range(REPS):
            rows = slice(rep * TOK, (rep + 1) * TOK)
            grad_front = dot(terms_ref[rep, 0 : 2 * BLOCK, :], xs_ref[rows, cols], 1, 0)
            grad_down = dot(terms_ref[rep, 2 * BLOCK : 3 * BLOCK, :], gs_ref[rows, cols], 1, 0)
            grads = jnp.concatenate([grad_front, grad_down], axis=0)
            offset = lax.rem(389 * (rep * 16 + depth), 1024).astype(F32) * (1.0 / 1024.0)
            for half in range(2):
                lanes = slice(half * COLS, (half + 1) * COLS)
                whole = slice(part * 256 + half * COLS, part * 256 + (half + 1) * COLS)
                ratio = grads[:, lanes] * inverse
                phase = row_part + (col_ref[0:1, whole] + offset)
                halves[half] = halves[half] + (ratio + turn(ratio + phase))
        for half in range(2):
            result = halves[half] * scale
            pair = 6 * SHARD * (2 * part + half)
            for mat in range(3):
                for low in range(2):
                    start = mat * BLOCK + low * SHARD
                    target = pair + (low * 3 + mat) * SHARD
                    wide_ref[target : target + SHARD, :] = result[start : start + SHARD]
            out_ref[pair : pair + 6 * SHARD, :] = wide_ref[pair : pair + 6 * SHARD, :].astype(BF16)
    done(0)


def adam_kernel(shares_ref, state_ref, new_state_ref, coded_ref, wide_ref, all_ref):
    all_ref[...] = shares_ref[...].astype(F32)
    mean_grad = all_ref[0 : 3 * SHARD]
    for peer in range(1, 16):
        mean_grad = mean_grad + all_ref[peer * 3 * SHARD : (peer + 1) * 3 * SHARD]
    mean_grad = mean_grad.reshape(3, SHARD, COLS)
    master = state_ref[0]
    first = BETA_ONE * state_ref[1] + (1.0 - BETA_ONE) * mean_grad
    second = BETA_TWO * state_ref[2] + (1.0 - BETA_TWO) * mean_grad * mean_grad
    updated = master - LEARN_RATE * (first / (jnp.sqrt(second) + ADAM_EPS) + WEIGHT_DECAY * master)
    new_state_ref[0] = updated
    new_state_ref[1] = first
    new_state_ref[2] = second
    spread_coded(eightbit_f32(updated), coded_ref, wide_ref)


def finish_kernel(ring_ref, own_ref, right_ref, across_ref, left_ref, spread_ref, grad_ref, sems):
    copies = [pltpu.make_async_copy(ring_ref, spread_ref.at[plane], sems.at[plane]) for plane in range(4)]
    for copy in copies:
        copy.start()
    grad_ref[...] = ((own_ref[...] + right_ref[...]) + (across_ref[...] + left_ref[...])).astype(BF16)
    for copy in copies:
        copy.wait()


def call(kernel, out_shape, smem=0, operands=(), scratch=(), limit=SMALL_LIMIT, first=None, idle=0, near=None):
    single = not isinstance(out_shape, tuple)
    outs = (out_shape,) if single else out_shape
    n_in = len(operands) - smem - idle
    n_out = len(outs)

    def body(*refs):
        small = refs[:smem]
        sources = refs[smem : smem + n_in]
        targets = refs[smem + n_in + idle : smem + n_in + idle + n_out]
        held = refs[smem + n_in + idle + n_out :]
        taken, made, rest, sems = held[:n_in], held[n_in : n_in + n_out], held[n_in + n_out : -1], held[-1]
        if near is not None:
            taken = taken[:near] + (sources[near],) + taken[near + 1 :]
        loads = [
            None if i == near else pltpu.make_async_copy(sources[i], taken[i], sems.at[i]) for i in range(n_in)
        ]
        stores = [pltpu.make_async_copy(made[i], targets[i], sems.at[n_in + i]) for i in range(n_out)]
        if first is None:
            for load in loads:
                load.start()
            for load in loads:
                load.wait()
            kernel(*small, *taken, *made, *rest)
            for store in stores:
                store.start()
        else:
            for i in first:
                loads[i].start()

            def need(*which):
                for i in which:
                    loads[i].wait()

            def done(*which):
                for i in which:
                    stores[i].start()

            kernel(need, done, *small, *taken, *made, *rest)
        for store in stores:
            store.wait()

    anywhere = pl.BlockSpec(memory_space=pl.ANY)
    specs = [pl.BlockSpec(memory_space=pltpu.SMEM)] * smem + [anywhere] * (n_in + idle)
    if near is not None:
        specs[smem + near] = pl.BlockSpec(memory_space=pltpu.VMEM)
    buffers = [pltpu.VMEM(item.shape, item.dtype) for item in tuple(operands[smem : smem + n_in]) + outs]
    if near is not None:
        buffers[near] = pltpu.VMEM((8, COLS), F32)
    return pl.pallas_call(
        body,
        out_shape=out_shape,
        in_specs=specs,
        out_specs=anywhere if single else (anywhere,) * n_out,
        scratch_shapes=buffers + list(scratch) + [pltpu.SemaphoreType.DMA((n_in + n_out,))],
        compiler_params=pltpu.CompilerParams(vmem_limit_bytes=limit),
    )(*operands)


def struct(shape, dtype=F32):
    return jax.ShapeDtypeStruct(shape, dtype)


def shift(value, axes, step):
    return lax.ppermute(value, axes, [(i, (i + step) % 4) for i in range(4)])


def swap_pairs():
    pairs = []
    for z in range(16):
        for t in range(8):
            pairs.append((z * 8 + t, (2 * t + z % 2) * 8 + z // 2))
    return pairs


def on_device(acts, grad_out, master, moment_one, moment_two, bit_widths, row_dither, col_dither):
    y = lax.axis_index("y")
    z = lax.axis_index(Z)
    core = lax.axis_index("c")
    tensor = lax.axis_index(TENSOR)
    spot = tensor % 4
    unit = 2 * y + tensor // 4
    pos = jnp.stack([core, spot, unit, z, y, tensor // 2]).astype(jnp.int32)
    pairs = swap_pairs()

    packed, state = call(
        pack_kernel,
        (struct((16, PACK, COLS), BF16), struct((3, 3, SHARD, COLS))),
        0,
        (acts, grad_out, col_dither[None], master, moment_one, moment_two),
        limit=LARGE_LIMIT,
    )
    state = lax.ppermute(state, Z + TENSOR, pairs)
    wide = (pltpu.VMEM((6 * SHARD, COLS), F32),)
    coded = call(code_kernel, struct((48 * SHARD, COLS), BF16), 0, (state,), wide)
    rows = lax.all_to_all(coded.reshape(16, 3 * SHARD, COLS), Z, 0, 0).reshape(48 * SHARD, COLS)
    own = lax.all_to_all(packed, ("y", "xh", "xl"), 0, 0)
    other = lax.ppermute(own, "c", [(0, 1), (1, 0)])

    row_part = lax.dynamic_slice(row_dither, (0, BLOCK * (8 * y + tensor)), (3, BLOCK))
    row_part = jnp.broadcast_to(row_part.astype(F32).reshape(3 * BLOCK, 1) * (1.0 / 1024.0), (3 * BLOCK, COLS))

    xs, gs, col_part = call(
        layout_kernel,
        (struct((REPS * TOK, 1024), BF16), struct((REPS * TOK, 1024), BF16), struct((8, 1024))),
        1,
        (pos, own, other, row_part),
        limit=LARGE_LIMIT,
        idle=1,
    )
    terms, peak, keep, give = call(
        front_kernel,
        (
            struct((REPS, 3 * BLOCK, TOK), BF16),
            struct((64, 1, COLS)),
            struct((16, TOK, COLS)),
            struct((16, TOK, COLS)),
        ),
        1,
        (pos, xs, gs, rows),
        (
            pltpu.VMEM((48 * SHARD, COLS), F32),
            pltpu.VMEM((3 * BLOCK, 1024), F32),
            pltpu.VMEM((3 * BLOCK, 1024), BF16),
        ),
        limit=LARGE_LIMIT,
        first=(0, 1),
        near=2,
    )
    peaks = lax.all_to_all(peak, ("xl", "c") + Z, 0, 0)
    got = lax.ppermute(give, "c", [(0, 1), (1, 0)])
    back = call(pair_kernel, (struct((4, TOK, COLS)),) * 4, 1, (pos, keep, got))

    shares = call(
        quant_kernel,
        struct((48 * SHARD, COLS), BF16),
        1,
        (pos, xs, gs, terms, peaks, bit_widths, row_part, col_part, back[0]),
        (pltpu.VMEM((48 * SHARD, COLS), F32),),
        limit=LARGE_LIMIT,
        first=(4, 2, 0, 1, 5, 6),
        idle=1,
        near=3,
    )
    back = [back[0]] + [shift(back[step], "y", step) for step in (1, 2, 3)]
    shares = lax.all_to_all(shares.reshape(16, 3 * SHARD, COLS), Z, 0, 0).reshape(48 * SHARD, COLS)

    new_state, ring = call(
        adam_kernel,
        (struct((3, 3, SHARD, COLS)), struct((48 * SHARD, COLS), BF16)),
        0,
        (shares, state, *back[1:]),
        wide + (pltpu.VMEM((48 * SHARD, COLS), F32),),
        idle=3,
    )
    back = call(plane_kernel, (struct((TOK, COLS)),) * 4, 1, (pos, *back))
    back = [back[0]] + [shift(back[step], ("xh", "xl"), step) for step in (1, 2, 3)]
    ring = lax.all_to_all(ring.reshape(16, 3 * SHARD, COLS), Z, 0, 0).reshape(48 * SHARD, COLS)
    anywhere = pl.BlockSpec(memory_space=pl.ANY)
    local = pl.BlockSpec(memory_space=pltpu.VMEM)
    ring, grad_in = pl.pallas_call(
        finish_kernel,
        out_shape=(struct((4, 48 * SHARD, COLS), BF16), struct((TOK, COLS), BF16)),
        in_specs=[anywhere] + [local] * 4,
        out_specs=(anywhere, local),
        scratch_shapes=[pltpu.SemaphoreType.DMA((4,))],
        compiler_params=pltpu.CompilerParams(vmem_limit_bytes=SMALL_LIMIT),
    )(ring, *back)
    new_state = lax.ppermute(new_state, Z + TENSOR, pairs)
    ring = lax.all_to_all(ring.reshape(32, 6 * SHARD, COLS), ("y",) + TENSOR, 0, 0)
    new_weights = ring.reshape(32, 2, 3, SHARD, COLS).transpose(2, 0, 1, 3, 4).reshape(3, 64 * SHARD, COLS)
    return (grad_in, new_state[0], new_state[1], new_state[2], new_weights)


def solution(mesh):
    grid = Mesh(mesh.devices.reshape(SIZES), DP + TENSOR)
    return jax.shard_map(
        on_device,
        mesh=grid,
        in_specs=(
            P(DP, TENSOR),
            P(DP, TENSOR),
            P(None, DP, TENSOR),
            P(None, DP, TENSOR),
            P(None, DP, TENSOR),
            P(),
            P(),
            P(TENSOR),
        ),
        out_specs=(
            P(DP, TENSOR),
            P(None, DP, TENSOR),
            P(None, DP, TENSOR),
            P(None, DP, TENSOR),
            P(None, None, TENSOR),
        ),
        check_vma=False,
    )
```

```python
import jax
import jax.numpy as jnp
from jax import lax
from jax.experimental import pallas as pl
from jax.experimental.pallas import tpu as pltpu
from jax.sharding import Mesh, PartitionSpec as P

F32 = jnp.float32
BF16 = jnp.bfloat16

TOK = 128
BROWS = 64
COLS = 128
SHARD = 24
BLOCK = 48
PACK = 2 * TOK + 16
REPS = 4

BETA_ONE = 0.9
BETA_TWO = 0.95
LEARN_RATE = 0.004
WEIGHT_DECAY = 0.1
ADAM_EPS = 1e-08
RANGE_EPS = 1e-06
N_DP = 64

SINE = (
    0.9999995827674866,
    -6.579691410064697,
    12.986435890197754,
    -12.188101768493652,
    6.558042526245117,
    -1.95303213596344,
)

Z = ("zh", "zl")
DP = ("y",) + Z
TENSOR = ("xh", "xl", "c")
SIZES = (4, 4, 4, 2, 2, 2)

SMALL_LIMIT = 20 * 1024 * 1024
LARGE_LIMIT = 60 * 1024 * 1024


def turn(value):
    frac = value - jnp.floor(value + 0.5)
    square = frac * frac
    total = jnp.full_like(square, SINE[-1])
    for coef in SINE[-2::-1]:
        total = total * square + coef
    return total * frac


def soft_round(value):
    return value - turn(value)


def eightbit_f32(weights):
    scale = (jnp.max(jnp.abs(weights), axis=-1, keepdims=True) + RANGE_EPS) / 127.0
    return soft_round(weights / scale) * scale


def dot(left, right, left_dim, right_dim):
    return lax.dot_general(
        left, right, (((left_dim,), (right_dim,)), ((), ())), preferred_element_type=F32
    )


def spread_coded(coded, coded_ref, wide_ref):
    for mat in range(6):
        wide_ref[mat * SHARD : (mat + 1) * SHARD, :] = coded[mat % 3]
    narrow = wide_ref[...].astype(BF16)
    for pair in range(8):
        coded_ref[pair * 6 * SHARD : (pair + 1) * 6 * SHARD, :] = narrow


def pack_kernel(acts_ref, grad_ref, dither_ref, master_ref, one_ref, two_ref, packed_ref, state_ref):
    high = (dither_ref[...] >> 3).astype(F32)
    low = (dither_ref[...] & 7).astype(F32)
    row = lax.broadcasted_iota(jnp.int32, (16, COLS), 0)
    extra = jnp.where(row == 0, high, jnp.where(row == 1, low, 0.0)).astype(BF16)
    for peer in range(16):
        packed_ref[peer, 0:TOK, :] = acts_ref[...]
        packed_ref[peer, TOK : 2 * TOK, :] = grad_ref[...]
        packed_ref[peer, 2 * TOK : PACK, :] = extra
    state_ref[0] = master_ref[...]
    state_ref[1] = one_ref[...]
    state_ref[2] = two_ref[...]


def code_kernel(state_ref, coded_ref, wide_ref):
    spread_coded(eightbit_f32(state_ref[0]), coded_ref, wide_ref)


def layout_kernel(pos_ref, own_ref, other_ref, xs_ref, gs_ref, col_ref):
    core = pos_ref[0]
    for source, which in ((own_ref, core), (other_ref, 1 - core)):
        for chip in range(4):
            cols = pl.ds(pl.multiple_of((2 * chip + which) * COLS, COLS), COLS)
            for rep in range(REPS):
                rows = slice(rep * TOK, (rep + 1) * TOK)
                xs_ref[rows, cols] = source[rep * 4 + chip, 0:TOK, :]
                gs_ref[rows, cols] = source[rep * 4 + chip, TOK : 2 * TOK, :]
            pair = source[chip, 2 * TOK : PACK, :].astype(F32)
            dither = pair[0:1] * 8.0 + pair[1:2]
            col_ref[:, cols] = jnp.broadcast_to(dither * (1.0 / 1024.0), (8, COLS))


def front_kernel(need, done, pos_ref, *refs):
    xs_ref, gs_ref, rows_ref, terms_ref, peak_ref, keep_ref, give_ref, wide_ref, full_ref, weights_ref = refs
    core = pos_ref[0]
    need(2)
    wide_ref[...] = rows_ref[...].astype(F32)
    for depth in range(16):
        cols = slice((depth // 2) * COLS, (depth // 2 + 1) * COLS)
        for mat in range(3):
            source = (depth * 3 + mat) * SHARD
            target = mat * BLOCK + (depth % 2) * SHARD
            full_ref[target : target + SHARD, cols] = wide_ref[source : source + SHARD, :]
    weights_ref[...] = full_ref[...].astype(BF16)
    need(0, 1)
    front = dot(weights_ref[0 : 2 * BLOCK, :], xs_ref[...], 1, 1)
    delta = dot(weights_ref[2 * BLOCK : 3 * BLOCK, :], gs_ref[...], 1, 1)
    gate = front[0:BLOCK]
    upper = front[BLOCK:]
    sig = jax.nn.sigmoid(gate)
    active = gate * sig
    dgate = (delta * upper * sig * (1.0 + gate * (1.0 - sig))).astype(BF16)
    dupper = (delta * active).astype(BF16)
    hidden = (active * upper).astype(BF16)
    for rep in range(REPS):
        rows = slice(rep * TOK, (rep + 1) * TOK)
        terms_ref[rep, 0:BLOCK, :] = dgate[:, rows]
        terms_ref[rep, BLOCK : 2 * BLOCK, :] = dupper[:, rows]
        terms_ref[rep, 2 * BLOCK : 3 * BLOCK, :] = hidden[:, rows]
    done(0)
    for target, which in ((keep_ref, core), (give_ref, 1 - core)):
        side = []
        for chip in range(4):
            cols = pl.ds(pl.multiple_of((2 * chip + which) * COLS, COLS), COLS)
            side.append(weights_ref[0 : 2 * BLOCK, cols])
        side = jnp.concatenate(side, axis=1)
        for rep in range(REPS):
            back = dot(terms_ref[rep, 0 : 2 * BLOCK, :], side, 0, 0)
            for chip in range(4):
                target[rep * 4 + chip] = back[:, chip * COLS : (chip + 1) * COLS]
    done(2, 3)
    peak = jnp.zeros((3 * BLOCK, COLS), F32)
    for rep in range(REPS):
        rows = slice(rep * TOK, (rep + 1) * TOK)
        for part in range(4):
            cols = slice(part * 256, (part + 1) * 256)
            grad_front = dot(terms_ref[rep, 0 : 2 * BLOCK, :], xs_ref[rows, cols], 1, 0)
            grad_down = dot(terms_ref[rep, 2 * BLOCK : 3 * BLOCK, :], gs_ref[rows, cols], 1, 0)
            grads = jnp.abs(jnp.concatenate([grad_front, grad_down], axis=0))
            peak = jnp.maximum(peak, jnp.maximum(grads[:, :COLS], grads[:, COLS:]))
    lane = lax.broadcasted_iota(jnp.int32, (1, COLS), 1)
    packed = jnp.zeros((1, COLS), F32)
    for group in range(9):
        top = jnp.max(peak[group * 16 : (group + 1) * 16], axis=0, keepdims=True)
        top = jnp.max(top, axis=1, keepdims=True)
        packed = jnp.where(lane == group, top, packed)
    peak_ref[...] = jnp.broadcast_to(packed.reshape(1, 1, COLS), peak_ref.shape)
    done(1)


def pair_kernel(pos_ref, keep_ref, got_ref, *back_refs):
    for step, back_ref in enumerate(back_refs):
        first = ((pos_ref[4] + step) % 4) * 4
        for chip in range(4):
            back_ref[chip] = keep_ref[first + chip] + got_ref[first + chip]


def plane_kernel(pos_ref, own_ref, up_ref, across_ref, down_ref, *back_refs):
    for step, back_ref in enumerate(back_refs):
        which = (pos_ref[5] + step) % 4
        back_ref[...] = (own_ref[which] + up_ref[which]) + (across_ref[which] + down_ref[which])


def quant_kernel(need, done, pos_ref, xs_ref, gs_ref, terms_ref, peaks_ref, bits_ref, row_ref, col_ref, out_ref, wide_ref):
    need(3, 4)
    spot = pos_ref[1]
    unit = pos_ref[2]
    depth = pos_ref[3]
    lane = lax.broadcasted_iota(jnp.int32, (1, COLS), 1)
    buck = lax.broadcasted_iota(jnp.int32, (1, 24), 1)
    tops = [jnp.max(peaks_ref[i * 16 : (i + 1) * 16], axis=0) for i in range(4)]
    scales = []
    for mat in range(3):
        per_bucket = []
        for bucket in range(3):
            held = jnp.zeros((1, COLS), F32)
            for sub in range(4 * bucket, 4 * bucket + 4):
                held = jnp.maximum(held, jnp.where(lane == mat * 3 + sub % 3, tops[sub // 3], 0.0))
            ranges = jnp.max(held, axis=1, keepdims=True)
            bits = jnp.where(buck == 3 * unit + bucket, bits_ref[mat : mat + 1, :].astype(F32), 0.0)
            bits = jnp.max(bits, axis=1, keepdims=True)
            levels = jnp.ones_like(bits)
            for count in range(3, 9):
                levels = jnp.where(bits == float(count), float(2 ** (count - 1) - 1), levels)
            per_bucket.append((ranges + RANGE_EPS) / levels)
        for sub in range(3):
            which = (3 * spot + sub) // 4
            chosen = jnp.where(which == 0, per_bucket[0], jnp.where(which == 1, per_bucket[1], per_bucket[2]))
            scales.append(jnp.broadcast_to(chosen, (16, COLS)))
    scale = jnp.concatenate(scales, axis=0)
    inverse = 1.0 / scale
    scale = scale * (1.0 / N_DP)
    need(0, 1, 2, 5, 6)
    row_part = row_ref[...]
    for part in range(4):
        cols = slice(part * 256, (part + 1) * 256)
        halves = [jnp.zeros((3 * BLOCK, COLS), F32) for _ in range(2)]
        for rep in range(REPS):
            rows = slice(rep * TOK, (rep + 1) * TOK)
            grad_front = dot(terms_ref[rep, 0 : 2 * BLOCK, :], xs_ref[rows, cols], 1, 0)
            grad_down = dot(terms_ref[rep, 2 * BLOCK : 3 * BLOCK, :], gs_ref[rows, cols], 1, 0)
            grads = jnp.concatenate([grad_front, grad_down], axis=0)
            offset = lax.rem(389 * (rep * 16 + depth), 1024).astype(F32) * (1.0 / 1024.0)
            for half in range(2):
                lanes = slice(half * COLS, (half + 1) * COLS)
                whole = slice(part * 256 + half * COLS, part * 256 + (half + 1) * COLS)
                ratio = grads[:, lanes] * inverse
                phase = row_part + (col_ref[0:1, whole] + offset)
                halves[half] = halves[half] + (ratio + turn(ratio + phase))
        for half in range(2):
            result = halves[half] * scale
            pair = 6 * SHARD * (2 * part + half)
            for mat in range(3):
                for low in range(2):
                    start = mat * BLOCK + low * SHARD
                    target = pair + (low * 3 + mat) * SHARD
                    wide_ref[target : target + SHARD, :] = result[start : start + SHARD]
            out_ref[pair : pair + 6 * SHARD, :] = wide_ref[pair : pair + 6 * SHARD, :].astype(BF16)
    done(0)


def adam_kernel(shares_ref, state_ref, new_state_ref, coded_ref, wide_ref, all_ref):
    all_ref[...] = shares_ref[...].astype(F32)
    mean_grad = all_ref[0 : 3 * SHARD]
    for peer in range(1, 16):
        mean_grad = mean_grad + all_ref[peer * 3 * SHARD : (peer + 1) * 3 * SHARD]
    mean_grad = mean_grad.reshape(3, SHARD, COLS)
    master = state_ref[0]
    first = BETA_ONE * state_ref[1] + (1.0 - BETA_ONE) * mean_grad
    second = BETA_TWO * state_ref[2] + (1.0 - BETA_TWO) * mean_grad * mean_grad
    updated = master - LEARN_RATE * (first / (jnp.sqrt(second) + ADAM_EPS) + WEIGHT_DECAY * master)
    new_state_ref[0] = updated
    new_state_ref[1] = first
    new_state_ref[2] = second
    spread_coded(eightbit_f32(updated), coded_ref, wide_ref)


def finish_kernel(ring_ref, own_ref, right_ref, across_ref, left_ref, spread_ref, grad_ref, sems):
    copies = [pltpu.make_async_copy(ring_ref, spread_ref.at[plane], sems.at[plane]) for plane in range(4)]
    for copy in copies:
        copy.start()
    grad_ref[...] = ((own_ref[...] + right_ref[...]) + (across_ref[...] + left_ref[...])).astype(BF16)
    for copy in copies:
        copy.wait()


def call(kernel, out_shape, smem=0, operands=(), scratch=(), limit=SMALL_LIMIT, first=None, idle=0):
    single = not isinstance(out_shape, tuple)
    outs = (out_shape,) if single else out_shape
    n_in = len(operands) - smem - idle
    n_out = len(outs)

    def body(*refs):
        small = refs[:smem]
        sources = refs[smem : smem + n_in]
        targets = refs[smem + n_in + idle : smem + n_in + idle + n_out]
        held = refs[smem + n_in + idle + n_out :]
        taken, made, rest, sems = held[:n_in], held[n_in : n_in + n_out], held[n_in + n_out : -1], held[-1]
        loads = [pltpu.make_async_copy(sources[i], taken[i], sems.at[i]) for i in range(n_in)]
        stores = [pltpu.make_async_copy(made[i], targets[i], sems.at[n_in + i]) for i in range(n_out)]
        if first is None:
            for load in loads:
                load.start()
            for load in loads:
                load.wait()
            kernel(*small, *taken, *made, *rest)
            for store in stores:
                store.start()
        else:
            for i in first:
                loads[i].start()

            def need(*which):
                for i in which:
                    loads[i].wait()

            def done(*which):
                for i in which:
                    stores[i].start()

            kernel(need, done, *small, *taken, *made, *rest)
        for store in stores:
            store.wait()

    anywhere = pl.BlockSpec(memory_space=pl.ANY)
    specs = [pl.BlockSpec(memory_space=pltpu.SMEM)] * smem + [anywhere] * (n_in + idle)
    buffers = [pltpu.VMEM(item.shape, item.dtype) for item in tuple(operands[smem : smem + n_in]) + outs]
    return pl.pallas_call(
        body,
        out_shape=out_shape,
        in_specs=specs,
        out_specs=anywhere if single else (anywhere,) * n_out,
        scratch_shapes=buffers + list(scratch) + [pltpu.SemaphoreType.DMA((n_in + n_out,))],
        compiler_params=pltpu.CompilerParams(vmem_limit_bytes=limit),
    )(*operands)


def struct(shape, dtype=F32):
    return jax.ShapeDtypeStruct(shape, dtype)


def shift(value, axes, step):
    return lax.ppermute(value, axes, [(i, (i + step) % 4) for i in range(4)])


def swap_pairs():
    pairs = []
    for z in range(16):
        for t in range(8):
            pairs.append((z * 8 + t, (2 * t + z % 2) * 8 + z // 2))
    return pairs


def on_device(acts, grad_out, master, moment_one, moment_two, bit_widths, row_dither, col_dither):
    y = lax.axis_index("y")
    z = lax.axis_index(Z)
    core = lax.axis_index("c")
    tensor = lax.axis_index(TENSOR)
    spot = tensor % 4
    unit = 2 * y + tensor // 4
    pos = jnp.stack([core, spot, unit, z, y, tensor // 2]).astype(jnp.int32)
    pairs = swap_pairs()

    packed, state = call(
        pack_kernel,
        (struct((16, PACK, COLS), BF16), struct((3, 3, SHARD, COLS))),
        0,
        (acts, grad_out, col_dither[None], master, moment_one, moment_two),
        limit=LARGE_LIMIT,
    )
    state = lax.ppermute(state, Z + TENSOR, pairs)
    wide = (pltpu.VMEM((6 * SHARD, COLS), F32),)
    coded = call(code_kernel, struct((48 * SHARD, COLS), BF16), 0, (state,), wide)
    rows = lax.all_to_all(coded.reshape(16, 3 * SHARD, COLS), Z, 0, 0).reshape(48 * SHARD, COLS)
    own = lax.all_to_all(packed, ("y", "xh", "xl"), 0, 0)
    other = lax.ppermute(own, "c", [(0, 1), (1, 0)])

    row_part = lax.dynamic_slice(row_dither, (0, BLOCK * (8 * y + tensor)), (3, BLOCK))
    row_part = jnp.broadcast_to(row_part.astype(F32).reshape(3 * BLOCK, 1) * (1.0 / 1024.0), (3 * BLOCK, COLS))

    xs, gs, col_part = call(
        layout_kernel,
        (struct((REPS * TOK, 1024), BF16), struct((REPS * TOK, 1024), BF16), struct((8, 1024))),
        1,
        (pos, own, other, row_part),
        limit=LARGE_LIMIT,
        idle=1,
    )
    terms, peak, keep, give = call(
        front_kernel,
        (
            struct((REPS, 3 * BLOCK, TOK), BF16),
            struct((64, 1, COLS)),
            struct((16, TOK, COLS)),
            struct((16, TOK, COLS)),
        ),
        1,
        (pos, xs, gs, rows),
        (
            pltpu.VMEM((48 * SHARD, COLS), F32),
            pltpu.VMEM((3 * BLOCK, 1024), F32),
            pltpu.VMEM((3 * BLOCK, 1024), BF16),
        ),
        limit=LARGE_LIMIT,
        first=(2, 0, 1),
    )
    peaks = lax.all_to_all(peak, ("xl", "c") + Z, 0, 0)
    got = lax.ppermute(give, "c", [(0, 1), (1, 0)])
    back = call(pair_kernel, (struct((4, TOK, COLS)),) * 4, 1, (pos, keep, got))

    shares = call(
        quant_kernel,
        struct((48 * SHARD, COLS), BF16),
        1,
        (pos, xs, gs, terms, peaks, bit_widths, row_part, col_part, back[0]),
        (pltpu.VMEM((48 * SHARD, COLS), F32),),
        limit=LARGE_LIMIT,
        first=(3, 4, 2, 0, 1, 5, 6),
        idle=1,
    )
    back = [back[0]] + [shift(back[step], "y", step) for step in (1, 2, 3)]
    shares = lax.all_to_all(shares.reshape(16, 3 * SHARD, COLS), Z, 0, 0).reshape(48 * SHARD, COLS)

    new_state, ring = call(
        adam_kernel,
        (struct((3, 3, SHARD, COLS)), struct((48 * SHARD, COLS), BF16)),
        0,
        (shares, state, back[1], back[2]),
        wide + (pltpu.VMEM((48 * SHARD, COLS), F32),),
        idle=2,
    )
    back = call(plane_kernel, (struct((TOK, COLS)),) * 4, 1, (pos, *back))
    back = [back[0]] + [shift(back[step], ("xh", "xl"), step) for step in (1, 2, 3)]
    ring = lax.all_to_all(ring.reshape(16, 3 * SHARD, COLS), Z, 0, 0).reshape(48 * SHARD, COLS)
    anywhere = pl.BlockSpec(memory_space=pl.ANY)
    local = pl.BlockSpec(memory_space=pltpu.VMEM)
    ring, grad_in = pl.pallas_call(
        finish_kernel,
        out_shape=(struct((4, 48 * SHARD, COLS), BF16), struct((TOK, COLS), BF16)),
        in_specs=[anywhere] + [local] * 4,
        out_specs=(anywhere, local),
        scratch_shapes=[pltpu.SemaphoreType.DMA((4,))],
        compiler_params=pltpu.CompilerParams(vmem_limit_bytes=SMALL_LIMIT),
    )(ring, *back)
    new_state = lax.ppermute(new_state, Z + TENSOR, pairs)
    ring = lax.all_to_all(ring.reshape(32, 6 * SHARD, COLS), ("y",) + TENSOR, 0, 0)
    new_weights = ring.reshape(32, 2, 3, SHARD, COLS).transpose(2, 0, 1, 3, 4).reshape(3, 64 * SHARD, COLS)
    return (grad_in, new_state[0], new_state[1], new_state[2], new_weights)


def solution(mesh):
    grid = Mesh(mesh.devices.reshape(SIZES), DP + TENSOR)
    return jax.shard_map(
        on_device,
        mesh=grid,
        in_specs=(
            P(DP, TENSOR),
            P(DP, TENSOR),
            P(None, DP, TENSOR),
            P(None, DP, TENSOR),
            P(None, DP, TENSOR),
            P(),
            P(),
            P(TENSOR),
        ),
        out_specs=(
            P(DP, TENSOR),
            P(None, DP, TENSOR),
            P(None, DP, TENSOR),
            P(None, DP, TENSOR),
            P(None, None, TENSOR),
        ),
        check_vma=False,
    )
```
